32 devices in a mesh: seq: 8 (over z, y), blk: 4 (over x, core).
Axes of the slice: x: 2, y: 2, z: 4, core: 2. Of those that a mesh axis runs over, the one named last changes fastest.
Arguments:
- hidden_in: bfloat16 [16, 1024, 768], P('seq', 'blk'), may hold values from -6 to 6
- depth_group: int32 [16], P('seq'), may hold values from 0 to 2
- query_weight: bfloat16 [768, 768], replicated, may hold values from -0.21875 to 0.21875
- query_bias: bfloat16 [768], replicated, may hold values from -3 to 3
- key_weight: bfloat16 [768, 768], replicated, may hold values from -0.21875 to 0.21875
- value_weight: bfloat16 [768, 768], replicated, may hold values from -0.21875 to 0.21875
- value_bias: bfloat16 [768], replicated, may hold values from -0.119628906 to 0.119628906
- output_weight: bfloat16 [768, 768], replicated, may hold values from -4 to 4
- output_bias: bfloat16 [768], replicated, may hold values from -3 to 3
- attn_gain: bfloat16 [768], replicated, may hold values from 0.5 to 1.5
- attn_shift: bfloat16 [768], replicated, may hold values from -3 to 3
- inner_weight: bfloat16 [768, 3072], replicated, may hold values from -0.21875 to 0.21875
- inner_bias: bfloat16 [3072], replicated, may hold values from -3 to 3
- outer_weight: bfloat16 [3072, 768], replicated, may hold values from -0.109375 to 0.109375
- outer_bias: bfloat16 [768], replicated, may hold values from -3 to 3
- final_gain: bfloat16 [768], replicated, may hold values from 0.5 to 1.5
- final_shift: bfloat16 [768], replicated, may hold values from -3 to 3
- grad_out: bfloat16 [16, 1024, 768], P('seq', 'blk'), may hold values from -6 to 6
Outputs:
- hidden_out: bfloat16 [16, 1024, 768], P('seq', 'blk')
- grad_in: bfloat16 [16, 1024, 768], P('seq', 'blk')
- grad_query_weight: float32 [768, 768], P('seq')
- grad_query_bias: float32 [768], P('seq')
- grad_key_weight: float32 [768, 768], P('seq')
- grad_value_weight: float32 [768, 768], P('seq')
- grad_value_bias: float32 [768], P('seq')
- grad_output_weight: float32 [768, 768], P('seq')
- grad_output_bias: float32 [768], P('seq')
- grad_attn_gain: float32 [768], P('seq')
- grad_attn_shift: float32 [768], P('seq')
- grad_inner_weight: float32 [768, 3072], P('seq')
- grad_inner_bias: float32 [3072], P('seq')
- grad_outer_weight: float32 [3072, 768], P('seq')
- grad_outer_bias: float32 [768], P('seq')
- grad_final_gain: float32 [768], P('seq')
- grad_final_shift: float32 [768], P('seq')
The draws below stay inside these ranges and needn't reach their ends.
All inputs are finite; a program needn't handle non-finite values.
Results may differ from the reference program's by a relative error of at most 0.02.
Values may be sent and summed in bfloat16 or wider, within the bound.
A program may use at most 128 MiB of HBM per device.

```python
from functools import partial
import jax
import jax.numpy as jnp
from jax import lax

D = 768
HEADS = 12
HD = 64
FF = 3072
SEQ_LEN = 1024
SEQS = 16


def place_ends(values, rng, low, high):
    longest = values.shape.index(max(values.shape))
    spots = []
    for shift in (0, 1):
        where = [jax.random.randint(jax.random.fold_in(rng, axis), (), 0, length) for axis, length in enumerate(values.shape)]
        where[longest] = (where[longest] + shift) % values.shape[longest]
        spots.append(tuple(where))
    return values.at[spots[0]].set(low).at[spots[1]].set(high)


def spiked(values, rng, source, target, blocks, factor):
    owner, partner = [(jnp.arange(values.shape[position]) // (values.shape[position] // blocks)).reshape([-1 if axis == position else 1 for axis in range(values.ndim)]) for position in (source, target)]
    chosen = jax.random.permutation(rng, blocks)[partner]
    strong = (owner == chosen) | (owner == (partner + blocks // 2) % blocks)
    return jnp.where(strong, factor * values, values)


def levels(stream_key, extent, pieces, low, high):
    level, own = 1.0, jax.random.fold_in(stream_key, 6)
    for dim, blocks in pieces:
        draws = jnp.exp(jax.random.uniform(jax.random.fold_in(own, dim), (blocks,), jnp.float32, low / len(pieces), high / len(pieces)))
        level = level * jnp.repeat(draws, extent[dim] // blocks).reshape([-1 if axis == dim else 1 for axis in range(len(extent))])
    return level


def centred(key, shape, deviation, most, pieces=(), dtype=jnp.bfloat16):
    entries = jax.random.normal(key, shape, jnp.float32) * deviation
    if len(pieces) > 0:
        entries = levels(key, shape, pieces, -0.22, 0.18) * entries
    return jnp.clip(entries, min=-most, max=most).astype(dtype)


def bell_draw_with(own_key, shape, scale, bound, shards, heavy, kind=jnp.bfloat16):
    values = scale * jax.random.normal(own_key, shape, jnp.float32)
    if shards:
        values = values * levels(own_key, shape, shards, -0.22, 0.18)
    return jnp.clip(spiked(values, jax.random.fold_in(own_key, 3), *heavy), -bound, bound).astype(kind)


def setup_inputs(seed: int = 0) -> dict:
    arg_keys = jax.random.split(jax.random.key(seed), 19)
    return {
        "hidden_in": centred(arg_keys[0], (SEQS, SEQ_LEN, D), 1.0, 6.0, ((0, 8), (1, 4))),
        "depth_group": place_ends(jax.random.randint(arg_keys[1], (SEQS,), 0, 3), jax.random.fold_in(arg_keys[1], 1), 0, 2).astype(jnp.int32),
        "query_weight": centred(arg_keys[2], (D, D), D ** -0.5, 0.21875),
        "query_bias": centred(arg_keys[3], (D,), 0.5, 3.0),
        "key_weight": centred(arg_keys[4], (D, D), D ** -0.5, 0.21875),
        "value_weight": centred(arg_keys[5], (D, D), D ** -0.5, 0.21875),
        "value_bias": centred(arg_keys[6], (D,), 0.02, 0.119628906),
        "output_weight": centred(arg_keys[7], (D, D), 2 ** -0.5, 4.0),
        "output_bias": centred(arg_keys[8], (D,), 0.5, 3.0),
        "attn_gain": jnp.clip(1.0 + 0.1 * jax.random.normal(arg_keys[9], (D,), jnp.float32), 0.5, 1.5).astype(jnp.bfloat16),
        "attn_shift": centred(arg_keys[10], (D,), 0.5, 3.0),
        "inner_weight": centred(arg_keys[11], (D, FF), D ** -0.5, 0.21875),
        "inner_bias": centred(arg_keys[12], (FF,), 0.5, 3.0),
        "outer_weight": centred(arg_keys[13], (FF, D), FF ** -0.5, 0.109375),
        "outer_bias": centred(arg_keys[14], (D,), 0.5, 3.0),
        "final_gain": jnp.clip(1.0 + 0.1 * jax.random.normal(arg_keys[15], (D,), jnp.float32), 0.5, 1.5).astype(jnp.bfloat16),
        "final_shift": centred(arg_keys[16], (D,), 0.5, 3.0),
        "grad_out": bell_draw_with(arg_keys[17], (SEQS, SEQ_LEN, D), 1.0, 6.0, ((0, 8), (1, 4)), (0, 2, 8, 2.0)),
    }


@jax.custom_vjp
def low(v):
    return lax.optimization_barrier(v.astype(jnp.bfloat16)).astype(jnp.float32)

@jax.custom_vjp
def low_back(v):
    return v

def low_keep(v):
    return (low(v), None)

def low_pass(kept, grad):
    return (grad,)

def back_keep(v):
    return (v, None)

def back_low(kept, grad):
    return (low(grad),)
low.defvjp(low_keep, low_pass)
low_back.defvjp(back_keep, back_low)

def exact_dot(left, right):
    return jnp.dot(left, right, precision=lax.Precision.HIGHEST)

def layer_norm(values, gain, shift):
    row_mean = lax.optimization_barrier(jnp.mean(values, axis=-1, keepdims=True))
    centered = values - row_mean
    variance = lax.optimization_barrier(jnp.mean(centered * centered, axis=-1, keepdims=True))
    return centered * lax.rsqrt(variance + 1e-05) * gain + shift

def attend_block(query_rows, keys_all, values_all):
    scores = low_back(0.125 * jnp.einsum('hqd,hkd->hqk', query_rows, keys_all, precision=lax.Precision.HIGHEST))
    row_max = lax.optimization_barrier(jnp.max(scores, axis=-1, keepdims=True))
    exponent = jnp.exp(scores - row_max)
    probs = low(exponent / lax.optimization_barrier(jnp.sum(exponent, axis=-1, keepdims=True)))
    return jnp.einsum('hqk,hkd->hqd', probs, values_all, precision=lax.Precision.HIGHEST)

def encoder_layer(x_float, kept_flag, query_weight, query_bias, key_weight, value_weight, value_bias, output_weight, output_bias, attn_gain, attn_shift, inner_weight, inner_bias, outer_weight, outer_bias, final_gain, final_shift):
    row_count = x_float.shape[0]
    queries = low(low_back(exact_dot(x_float, query_weight) + query_bias))
    keys_full = low(low_back(exact_dot(x_float, key_weight)))
    values_full = low(low_back(exact_dot(x_float, value_weight) + value_bias))

    def split_heads(matrix):
        return matrix.reshape(row_count, HEADS, HD).transpose(1, 0, 2)
    block_rows = min(512, row_count)
    query_blocks = split_heads(queries).reshape(HEADS, row_count // block_rows, block_rows, HD).transpose(1, 0, 2, 3)
    attended = lax.map(jax.checkpoint(partial(attend_block, keys_all=split_heads(keys_full), values_all=split_heads(values_full))), query_blocks)
    attended = attended.transpose(0, 2, 1, 3).reshape(row_count, HEADS * HD)
    attended = low(low_back(attended))
    attn_out = low_back(exact_dot(attended, output_weight) + output_bias)
    normed = layer_norm(x_float + attn_out, attn_gain, attn_shift)
    inner_in = low(normed)
    pre_act = low_back(exact_dot(inner_in, inner_weight) + inner_bias)
    activated = low(jax.nn.gelu(pre_act, approximate=False))
    ffn_out = low_back(exact_dot(activated, outer_weight) + outer_bias)
    result = layer_norm(normed + ffn_out, final_gain, final_shift)
    return kept_flag * result + (1.0 - kept_flag) * x_float

def reference(hidden_in, depth_group, query_weight, query_bias, key_weight, value_weight, value_bias, output_weight, output_bias, attn_gain, attn_shift, inner_weight, inner_bias, outer_weight, outer_bias, final_gain, final_shift, grad_out):
    params = tuple((weight.astype(jnp.float32) for weight in (query_weight, query_bias, key_weight, value_weight, value_bias, output_weight, output_bias, attn_gain, attn_shift, inner_weight, inner_bias, outer_weight, outer_bias, final_gain, final_shift)))
    kept_all = (depth_group != 2).astype(jnp.float32)

    def one_sequence(totals, members):
        tokens, kept_flag, cotangent = members

        def local_layer(x_float, *weights):
            return encoder_layer(x_float, kept_flag, *weights)
        result, pullback = jax.vjp(local_layer, tokens.astype(jnp.float32), *params)
        grads = pullback(cotangent.astype(jnp.float32))
        new_totals = tuple((running + fresh for running, fresh in zip(totals, grads[1:])))
        return (new_totals, (result.astype(jnp.bfloat16), grads[0].astype(jnp.bfloat16)))
    zero_grads = tuple((jnp.zeros(weight.shape, jnp.float32) for weight in params))
    totals, (outputs, input_grads) = lax.scan(one_sequence, zero_grads, (hidden_in, kept_all, grad_out))
    return (outputs, input_grads, totals[0], totals[1], totals[2], totals[3], totals[4], totals[5], totals[6], totals[7], totals[8], totals[9], totals[10], totals[11], totals[12], totals[13], totals[14])
```

```python
import itertools
import math

import jax
import jax.numpy as jnp
from jax import lax
from jax.experimental import pallas as pl
from jax.experimental.pallas import tpu as pltpu
from jax.sharding import PartitionSpec as P

HEADS = 12
HD = 64
MESH = pl.DeviceIdType.MESH
BF = jnp.bfloat16
F32 = jnp.float32
LOG2E = math.log2(math.e)
SCALE2 = 0.125 * LOG2E
EPS = 1e-05

FLOWS = 12
BITS = ("z1", "z0", "y")
ORDER_Y = ("y", "x", "z0", "z1")
ORDER_Z = ("z0", "y", "x", "z1")
ORDERS = [ORDER_Y, ORDER_Z] * 6

NAMES = ("qb", "vb", "ob", "ag", "as", "xb", "fg", "fs", "ib")


def nn(left, right):
    return jnp.dot(left, right, preferred_element_type=F32)


def nt(left, right):
    return lax.dot_general(left, right, (((1,), (1,)), ((), ())), preferred_element_type=F32)


def tn(left, right):
    return lax.dot_general(left, right, (((0,), (0,)), ((), ())), preferred_element_type=F32)


def fold8(values):
    rows, width = values.shape
    return jnp.sum(values.reshape(rows // 8, 8, width), axis=0)


def recv_shape(order, k, rows, cols):
    done = order[: k + 1]
    free = [2 for ax in BITS if ax not in done]
    return (*free, rows // 2 if "x" in done else rows, cols)


def layer_kernel(groups, names, *refs):
    r = dict(zip(names, refs))
    seq = lax.axis_index("seq")
    blk = lax.axis_index("blk")
    x = lax.div(blk, 2)
    c = lax.rem(blk, 2)
    hi = lax.div(seq, groups)
    own = {"x": x, "y": lax.rem(hi, 2), "z0": lax.rem(lax.div(hi, 2), 2), "z1": lax.div(hi, 4)}
    blk_x = blk + 2 - 4 * x
    blk_c = blk + 1 - 2 * c
    blk_xc = blk_x + 1 - 2 * c
    peers = {
        "c": (seq, blk_c),
        "x": (seq, blk_x),
        "y": (seq + (1 - 2 * own["y"]) * groups, blk),
        "z0": (seq + (1 - 2 * own["z0"]) * 2 * groups, blk),
        "z1": (seq + (1 - 2 * own["z1"]) * 4 * groups, blk),
    }
    slots, tok, width = r["xall"].shape
    seq_len = slots * tok
    half = width // 2
    ff = r["wi"].shape[1]
    pairs = half // (2 * HD)
    mine = (blk, blk_x)
    col0 = pl.multiple_of(c * half, 128)
    place = {name: width * i for i, name in enumerate(NAMES)}

    def vec(name, start=0, size=width):
        return r["vec"][:, pl.ds(place[name] + start, size)]

    def remote(src, dst, sems, i, peer):
        return pltpu.make_async_remote_copy(
            src_ref=src,
            dst_ref=dst,
            send_sem=r[sems + "_s"].at[i] if not isinstance(i, tuple) else r[sems + "_s"].at[i[0], i[1]],
            recv_sem=r[sems + "_r"].at[i] if not isinstance(i, tuple) else r[sems + "_r"].at[i[0], i[1]],
            device_id=peers[peer],
            device_id_type=MESH,
        )

    cols = pl.ds(col0, half)
    local = [
        pltpu.make_async_copy(r["hid"].at[x], r["xall"].at[blk], r["lsem"].at[0]),
        pltpu.make_async_copy(r["wq"].at[:, cols], r["wqkv"].at[0], r["lsem"].at[1]),
        pltpu.make_async_copy(r["wk"].at[:, cols], r["wqkv"].at[1], r["lsem"].at[2]),
        pltpu.make_async_copy(r["wv"].at[:, cols], r["wqkv"].at[2], r["lsem"].at[3]),
        pltpu.make_async_copy(r["go"].at[x], r["gown"].at[0], r["lsem"].at[4]),
        pltpu.make_async_copy(r["wo_in"], r["wo"], r["lsem"].at[5]),
        pltpu.make_async_copy(r["wi_in"], r["wi"], r["lsem"].at[6]),
        pltpu.make_async_copy(r["wx_in"], r["wx"], r["lsem"].at[7]),
    ]
    for copy in local:
        copy.start()

    barrier = pltpu.get_barrier_semaphore()
    for peer in peers.values():
        pl.semaphore_signal(barrier, inc=1, device_id=peer, device_id_type=MESH)
    pl.semaphore_wait(barrier, len(peers))

    def ex(i):
        if i == 0:
            return remote(r["hid"].at[1 - x], r["xall"].at[blk], "ex", 0, "x")
        if i == 1:
            return remote(r["hid"].at[x], r["xall"].at[blk], "ex", 1, "c")
        if i == 2:
            return remote(r["xall"].at[blk_x], r["xall"].at[blk_x], "ex", 2, "c")
        if i == 3:
            return remote(r["go"].at[1 - x], r["gown"].at[1], "ex", 3, "x")
        if i < 4 + pairs:
            lanes = pl.ds(pl.multiple_of(c * half + (i - 4) * 128, 128), 128)
            return remote(r["att"].at[:, :, lanes], r["att"].at[:, :, lanes], "ex", i, "c")
        i -= 4 + pairs
        if i < 2:
            return remote(r["ga"].at[mine[i]], r["ga"].at[mine[i]], "ex", i + 4 + pairs, "c")
        if i == 2:
            return remote(r["hbuf"].at[1], r["hout"].at[x], "ex", i + 4 + pairs, "x")
        if i == 3:
            return remote(r["gffn"], r["grecv"], "ex", i + 4 + pairs, "c")
        return remote(r["inn"].at[pl.ds(tok, tok)], r["gin"].at[x], "ex", i + 4 + pairs, "x")

    ex_ga, ex_hout, ex_part, ex_gin = 4 + pairs, 6 + pairs, 7 + pairs, 8 + pairs
    ex(0).start()
    ex(1).start()
    kept = jnp.where(r["dg"][x] == 2, 0.0, 1.0).astype(F32)
    r["sg8"][...] = jnp.zeros_like(r["sg8"])

    def project(j):
        rows = pl.ds(pl.multiple_of(j * tok, tok), tok)
        block = r["xall"][j]
        r["q"][rows, :] = (nn(block, r["wqkv"][0]) + r["vec"][:, pl.ds(col0, half)]).astype(BF)
        r["k"][rows, :] = nn(block, r["wqkv"][1]).astype(BF)
        r["v"][rows, :] = (
            nn(block, r["wqkv"][2]) + r["vec"][:, pl.ds(pl.multiple_of(place["vb"] + col0, 128), half)]
        ).astype(BF)

    for i in range(4):
        local[i].wait()
    project(blk)
    ex(1).wait_recv()
    project(blk_c)
    ex(0).wait_recv()
    ex(2).start()
    ex(3).start()
    project(blk_x)
    ex(2).wait_recv()
    project(blk_xc)

    for p in range(pairs):
        lanes = pl.ds(p * 128, 128)
        r["kt"][lanes, :] = r["k"][:, lanes].T
        vt = r["v"][:, lanes].T
        for h in range(2):
            r["vx"][2 * p + h, pl.ds(0, HD), :] = vt[h * HD : (h + 1) * HD]
            r["vx"][2 * p + h, pl.ds(HD, 16), :] = jnp.ones((16, seq_len), BF)

    qb = tok
    blocks = seq_len // qb
    lane_head = lax.broadcasted_iota(jnp.int32, (qb, 128), 1) // HD

    def forward(p, t):
        lanes = pl.ds(p * 128, 128)
        rows = pl.ds(pl.multiple_of(t * qb, qb), qb)
        qp = r["q"][rows, lanes]
        outs = []
        for h in range(2):
            qm = jnp.where(lane_head == h, qp, jnp.zeros_like(qp))
            st = nt(r["k"][:, lanes], qm)
            top = jnp.max(st, axis=0, keepdims=True)
            pt = jnp.exp2((st - top) * SCALE2).astype(BF)
            ot = nn(r["vx"][2 * p + h], pt)
            total = ot[HD : HD + 1]
            outs.append(ot[:HD] / total)
            r["lse"][2 * p + h, :, rows] = top * SCALE2 + jnp.log2(total)
        both = jnp.concatenate(outs, axis=0).astype(BF)
        r["att"][t, :, pl.ds(pl.multiple_of(c * half + p * 128, 128), 128)] = both.T

    for p in range(pairs):

        @pl.loop(0, blocks)
        def _(t):
            forward(p, t)

        ex(4 + p).start()

    for i in range(4, 8):
        local[i].wait()
    for p in range(pairs):
        ex(4 + p).wait_recv()
    ex(3).wait_recv()

    chunk = 32
    per = tok // chunk

    def own_rows(i):
        second = lax.div(i, per)
        slot = blk + second * (blk_x - blk)
        inner = pl.ds(pl.multiple_of(lax.rem(i, per) * chunk, chunk), chunk)
        rows = pl.ds(pl.multiple_of(i * chunk, chunk), chunk)
        return slot, second, inner, rows

    def fold_in(name, values):
        at = pl.ds(place[name], values.shape[1])
        r["sg8"][:, at] += fold8(values)

    for i in range(2):
        r["acc"][pl.ds(i * tok, tok), :] = nn(r["att"][mine[i]], r["wo"][...])

    @pl.loop(0, 2 * per)
    def _(i):
        slot, second, inner, rows = own_rows(i)
        v = r["acc"][rows, :] + vec("ob") + r["xall"][slot, inner, :].astype(F32)
        cen = v - jnp.mean(v, axis=-1, keepdims=True)
        rstd = lax.rsqrt(jnp.mean(cen * cen, axis=-1, keepdims=True) + EPS)
        xh = cen * rstd
        normed = xh * vec("ag") + vec("as")
        r["xh"][rows, :] = xh
        r["rs"][rows, :] = rstd
        r["acc"][rows, :] = normed
        r["inn"][rows, :] = normed.astype(BF)

    tile = 256

    @pl.loop(0, ff // tile)
    def _(j):
        at = pl.ds(pl.multiple_of(j * tile, tile), tile)
        bias = r["vec"][:, pl.ds(pl.multiple_of(place["ib"] + j * tile, 128), tile)]
        pre = nn(r["inn"][...], r["wi"][:, at]) + bias
        phi = 0.5 + 0.5 * lax.erf(pre * math.sqrt(0.5))
        dens = jnp.exp2(pre * pre * (-0.5 * LOG2E)) * (1.0 / math.sqrt(2.0 * math.pi))
        low = (pre * phi).astype(BF)
        r["act"][:, at] = low
        r["gp"][:, at] = (phi + pre * dens).astype(BF)
        r["acc"][...] += nn(low, r["wx"][at, :])

    @pl.loop(0, 2 * per)
    def _(i):
        slot, second, inner, rows = own_rows(i)
        xf = r["xall"][slot, inner, :].astype(F32)
        v = r["acc"][rows, :] + vec("xb")
        cen = v - jnp.mean(v, axis=-1, keepdims=True)
        rstd = lax.rsqrt(jnp.mean(cen * cen, axis=-1, keepdims=True) + EPS)
        xh = cen * rstd
        out = kept * (xh * vec("fg") + vec("fs")) + (1.0 - kept) * xf
        r["hbuf"][second, inner, :] = out.astype(BF)
        g = kept * r["gown"][second, inner, :].astype(F32)
        fold_in("fg", g * xh)
        fold_in("fs", g)
        gx = g * vec("fg")
        m1 = jnp.mean(gx, axis=-1, keepdims=True)
        m2 = jnp.mean(gx * xh, axis=-1, keepdims=True)
        gs = rstd * (gx - m1 - xh * m2)
        low = gs.astype(BF)
        r["acc"][rows, :] = gs
        r["gffn"][rows, :] = low
        fold_in("xb", low.astype(F32))

    ex(ex_hout).start()
    hout_local = pltpu.make_async_copy(r["hbuf"].at[0], r["hout"].at[x], r["lsem"].at[0])
    hout_local.start()

    def pay(f):
        return r["d2"].at[c, f] if f < 8 else r["dc"].at[f - 8]

    rows_f, cols_f = r["dc"].shape[-2:]

    def view(ref, order, k, send):
        idx = [slice(None)] * 3
        row = pl.ds(0, rows_f)
        for j, ax in enumerate(order[: k + 1]):
            want = 1 - own[ax] if (j == k and send) else own[ax]
            if ax == "x":
                row = pl.ds(pl.multiple_of(want * (rows_f // 2), 16), rows_f // 2)
            else:
                idx[BITS.index(ax)] = want
        return (*idx, row, slice(None))

    def hop(f, k):
        order = ORDERS[f]
        at = view(None, order, k, True)
        return remote(pay(f).at[at], r[f"r{f}_{k}"], "rs", (f, k), order[k])

    def add_in(f, k):
        order = ORDERS[f]
        idx = list(view(None, order, k, False))
        ref = pay(f)
        free = [ax for ax in BITS if ax not in order[: k + 1]]
        for combo in itertools.product((0, 1), repeat=len(free)):
            for ax, bit in zip(free, combo):
                idx[BITS.index(ax)] = bit
            at = tuple(idx)
            got = r[f"r{f}_{k}"][(*combo, slice(None), slice(None))]
            ref[at] = ref[at] + got

    x_rows = pl.ds(pl.multiple_of(x * (rows_f // 2), 16), rows_f // 2)

    def spread(f, k):
        if k == 0:
            part = r["fin"].at[f, c, x_rows]
            return remote(part, part, "rs", (f, 4), "x")
        part = r["fin"].at[f, c]
        return remote(part, part, "rs", (f, 5), "c")

    def d2d(f):
        return remote(r["d2"].at[1 - c, f], r["rc"].at[f], "rs", (f, 6), "c")

    def step(f, k):
        order = ORDERS[f]
        if k == -1:
            d2d(f).wait_recv()
            for combo in itertools.product((0, 1), repeat=3):
                ref = pay(f)
                ref[combo] = ref[combo] + r["rc"][(f, *combo)]
            hop(f, 0).start()
        elif k == 0:
            hop(f, 0).start()
        elif k < 4:
            hop(f, k - 1).wait_recv()
            add_in(f, k - 1)
            hop(f, k).start()
        elif k == 4:
            hop(f, 3).wait_recv()
            add_in(f, 3)
            r["fin"][f, c, x_rows, :] = pay(f)[(own["z1"], own["z0"], own["y"], x_rows, slice(None))]
            spread(f, 0).start()
        elif k == 5:
            spread(f, 0).wait_recv()
            spread(f, 1).start()
        else:
            spread(f, 1).wait_recv()

    bits8 = [(a, b, d) for a in range(2) for b in range(2) for d in range(2)]
    outer_rows = ff // 8

    @pl.loop(0, 8)
    def _(j):
        at = r["act"][:, pl.ds(pl.multiple_of(j * outer_rows, 128), outer_rows)]
        val = tn(at, r["gffn"][...]).astype(BF)
        i1, i2, i3 = lax.div(j, 4), lax.rem(lax.div(j, 2), 2), lax.rem(j, 2)
        for f in range(4):
            for h in range(2):
                r["d2"][h, f, i1, i2, i3] = val[f * rows_f : (f + 1) * rows_f, h * cols_f : (h + 1) * cols_f]

    for f in range(4):
        d2d(f).start()

    r["innt"][...] = r["inn"][...].T
    per_half = (ff // 2) // 128

    def inner_tile(j):
        at = pl.ds(pl.multiple_of(j * tile, tile), tile)
        dact = nt(r["gffn"][...], r["wx"][at, :])
        gpre = (dact * r["gp"][:, at].astype(F32)).astype(BF)
        r["sg8"][:, pl.ds(pl.multiple_of(place["ib"] + j * tile, 128), tile)] = fold8(gpre.astype(F32))
        val = nn(r["innt"][...], gpre).astype(BF)
        for g2 in range(tile // 128):
            g = (tile // 128) * j + g2
            rest = lax.rem(g, per_half)
            f = 4 + lax.div(rest, cols_f // 128)
            lane = pl.multiple_of(lax.rem(rest, cols_f // 128) * 128, 128)
            piece = val[:, g2 * 128 : (g2 + 1) * 128]
            r["d2"][lax.div(g, per_half), f, :, :, :, :, pl.ds(lane, 128)] = piece.reshape(2, 2, 2, rows_f, 128)
        r["acc"][...] += nt(gpre, r["wi"][:, at])

    tiles = ff // tile
    for part in range(2):

        @pl.loop(part * tiles // 2, (part + 1) * tiles // 2)
        def _(j):
            inner_tile(j)

        for f in ((0, 1), (2, 3))[part]:
            step(f, -1)

    for f in range(4, 8):
        d2d(f).start()

    @pl.loop(0, 2 * per)
    def _(i):
        slot, second, inner, rows = own_rows(i)
        g = r["acc"][rows, :]
        xh = r["xh"][rows, :]
        fold_in("ag", g * xh)
        fold_in("as", g)
        gx = g * vec("ag")
        m1 = jnp.mean(gx, axis=-1, keepdims=True)
        m2 = jnp.mean(gx * xh, axis=-1, keepdims=True)
        gs = r["rs"][rows, :] * (gx - m1 - xh * m2)
        low = gs.astype(BF)
        r["acc"][rows, :] = gs
        r["ga"][slot, inner, :] = low
        fold_in("ob", low.astype(F32))

    ex(ex_ga).start()
    ex(ex_ga + 1).start()
    for f in range(4, 8):
        step(f, -1)

    do = r["wx"].at[pl.ds(0, seq_len), pl.ds(0, half)]
    dq = r["wx"].at[pl.ds(0, seq_len), pl.ds(half, half)]
    dk = r["wx"].at[pl.ds(seq_len, seq_len), pl.ds(0, half)]
    dv = r["wx"].at[pl.ds(seq_len, seq_len), pl.ds(half, half)]
    wo_own = r["wo"].at[pl.ds(pl.multiple_of(c * half, 128), half), :]

    def upstream(slot):
        rows = pl.ds(pl.multiple_of(slot * tok, tok), tok)
        do[rows, :] = nt(r["ga"][slot], wo_own[...]).astype(BF)

    upstream(blk)
    upstream(blk_x)
    ex(ex_ga).wait_recv()
    ex(ex_ga + 1).wait_recv()
    upstream(blk_c)
    upstream(blk_xc)

    for p in range(pairs):
        lanes = pl.ds(p * 128, 128)
        at = r["att"][:, :, pl.ds(pl.multiple_of(c * half + p * 128, 128), 128)].reshape(seq_len, 128)
        prod = (at.astype(F32) * do[:, lanes].astype(F32)).T
        for h in range(2):
            r["delta"][2 * p + h] = jnp.sum(prod[h * HD : (h + 1) * HD], axis=0, keepdims=True)

    att_all = r["att"][...].reshape(seq_len, width)
    ga_cols = r["ga"][:, :, pl.ds(col0, half)].reshape(seq_len, half)
    r["dc"][3] = tn(att_all, ga_cols).astype(BF).reshape(2, 2, 2, rows_f, cols_f)

    def backward(p, t):
        lanes = pl.ds(p * 128, 128)
        rows = pl.ds(pl.multiple_of(t * qb, qb), qb)
        qp = r["q"][rows, lanes]
        dp = do[rows, lanes]
        kp = r["k"][:, lanes]
        vp = r["v"][:, lanes]
        zero = jnp.zeros_like(qp)
        dqs = []
        for h in range(2):
            qm = jnp.where(lane_head == h, qp, zero)
            dm = jnp.where(lane_head == h, dp, zero)
            pt = jnp.exp2(nt(kp, qm) * SCALE2 - r["lse"][2 * p + h, :, rows])
            dpt = nt(vp, dm)
            ds = (pt * (dpt - r["delta"][2 * p + h, :, rows])).astype(BF)
            r["dva"][...] += nn(pt.astype(BF), dm)
            r["dka"][...] += nn(ds, qm)
            dqs.append(nn(r["kt"][pl.ds(p * 128 + h * HD, HD), :], ds))
        both = (jnp.concatenate(dqs, axis=0) * 0.125).astype(BF)
        dq[rows, lanes] = both.T

    later = {
        0: [(f, 1) for f in range(0, 4)],
        1: [(f, 1) for f in range(4, 8)] + [(f, 2) for f in range(0, 4)],
        2: [(f, 2) for f in range(4, 8)] + [(f, 3) for f in range(0, 4)],
    }
    for p in range(pairs):
        r["dka"][...] = jnp.zeros_like(r["dka"])
        r["dva"][...] = jnp.zeros_like(r["dva"])

        @pl.loop(0, blocks)
        def _(t):
            backward(p, t)

        lanes = pl.ds(p * 128, 128)
        dk[:, lanes] = (r["dka"][...] * 0.125).astype(BF)
        dv[:, lanes] = r["dva"][...].astype(BF)
        for f, k in later[p]:
            step(f, k)

    xt = r["wi"].at[:, pl.ds(0, seq_len)]
    xt[...] = r["xall"][...].reshape(seq_len, width).T
    for i, g in enumerate((dq, dk, dv)):
        r["dc"][i] = nn(xt[...], g[...]).astype(BF).reshape(2, 2, 2, rows_f, cols_f)
        step(8 + i, 0)
    step(11, 0)
    r["sg8"][:, pl.ds(col0, half)] = fold8(dq[...].astype(F32))
    r["sg8"][:, pl.ds(pl.multiple_of(place["vb"] + col0, 128), half)] = fold8(dv[...].astype(F32))
    r["sgs"][0] = jnp.sum(r["sg8"][...], axis=0, keepdims=True)

    def small(k):
        return remote(r["sgs"].at[k], r["sgr"].at[k], "sm", k, ("c", "x", "y", "z0", "z1")[k])

    small(0).start()

    def partial(slot):
        rows = pl.ds(pl.multiple_of(slot * tok, tok), tok)
        return (
            nt(dq[rows, :], r["wqkv"][0]) + nt(dk[rows, :], r["wqkv"][1]) + nt(dv[rows, :], r["wqkv"][2])
        )

    r["gffn"][pl.ds(0, tok), :] = partial(blk_c).astype(BF)
    r["gffn"][pl.ds(tok, tok), :] = partial(blk_xc).astype(BF)
    ex(ex_part).start()
    for i in range(2):
        rows = pl.ds(i * tok, tok)
        r["acc"][rows, :] += partial(mine[i])
    ex(ex_part).wait_recv()
    for i in range(2):
        rows = pl.ds(i * tok, tok)
        total = r["acc"][rows, :] + r["grecv"][rows, :].astype(F32) + (1.0 - kept) * r["gown"][i].astype(F32)
        r["inn"][rows, :] = total.astype(BF)
    ex(ex_gin).start()
    gin_local = pltpu.make_async_copy(r["inn"].at[pl.ds(0, tok)], r["gin"].at[x], r["lsem"].at[1])
    gin_local.start()

    for k in range(5):
        small(k).wait_recv()
        r["sgs"][k + 1] = r["sgs"][k] + r["sgr"][k]
        if k < 4:
            small(k + 1).start()
    r["sout"][...] = r["sgs"][5]

    rest = [[(f, 3) for f in range(4, 8)], [(f, 4) for f in range(0, 8)], [(f, 5) for f in range(0, 8)]]
    rest += [[(f, k) for f in range(8, 12)] for k in range(1, 6)]
    rest += [[(f, 6) for f in range(12)]]
    for group in rest:
        for f, k in group:
            step(f, k)

    ex(ex_hout).wait_recv()
    ex(ex_gin).wait_recv()
    hout_local.wait()
    gin_local.wait()
    for i in range(9 + pairs):
        ex(i).wait_send()
    for k in range(5):
        small(k).wait_send()
    for f in range(FLOWS):
        for k in range(4):
            hop(f, k).wait_send()
        spread(f, 0).wait_send()
        spread(f, 1).wait_send()
        if f < 8:
            d2d(f).wait_send()


def build(mesh):
    n_seq = mesh.shape["seq"]
    groups = n_seq // 8

    def local(
        hidden_in,
        depth_group,
        query_weight,
        query_bias,
        key_weight,
        value_weight,
        value_bias,
        output_weight,
        output_bias,
        attn_gain,
        attn_shift,
        inner_weight,
        inner_bias,
        outer_weight,
        outer_bias,
        final_gain,
        final_shift,
        grad_out,
    ):
        seqs, tok, width = hidden_in.shape
        ff = inner_weight.shape[1]
        slots = mesh.shape["blk"]
        seq_len = slots * tok
        half = width // 2
        heads = half // HD
        rows_f, cols_f = width // 8, half
        vec = jnp.concatenate(
            [query_bias, value_bias, output_bias, attn_gain, attn_shift, outer_bias, final_gain, final_shift, inner_bias]
        ).astype(F32)[None]
        small = vec.shape[1]
        hbm = pl.BlockSpec(memory_space=pl.ANY)
        vmem = pl.BlockSpec(memory_space=pltpu.VMEM)
        ins = [
            ("dg", depth_group, pl.BlockSpec(memory_space=pltpu.SMEM)),
            ("vec", vec, vmem),
            ("hid", hidden_in, hbm),
            ("go", grad_out, hbm),
            ("wq", query_weight, hbm),
            ("wk", key_weight, hbm),
            ("wv", value_weight, hbm),
            ("wo_in", output_weight, hbm),
            ("wi_in", inner_weight, hbm),
            ("wx_in", outer_weight, hbm),
        ]
        outs = [
            ("hout", (seqs, tok, width), BF, hbm),
            ("gin", (seqs, tok, width), BF, hbm),
            ("fin", (FLOWS, 2, rows_f, cols_f), BF, vmem),
            ("sout", (1, small), F32, vmem),
        ]
        v = pltpu.VMEM
        dma = pltpu.SemaphoreType.DMA
        pairs = half // 128
        scratch = [
            ("xall", v((slots, tok, width), BF)),
            ("gown", v((2, tok, width), BF)),
            ("wqkv", v((3, width, half), BF)),
            ("wo", v((width, width), BF)),
            ("wi", v((width, ff), BF)),
            ("wx", v((ff, width), BF)),
            ("q", v((seq_len, half), BF)),
            ("k", v((seq_len, half), BF)),
            ("v", v((seq_len, half), BF)),
            ("kt", v((half, seq_len), BF)),
            ("vx", v((heads, HD + 16, seq_len), BF)),
            ("lse", v((heads, 1, seq_len), F32)),
            ("delta", v((heads, 1, seq_len), F32)),
            ("att", v((slots, tok, width), BF)),
            ("ga", v((slots, tok, width), BF)),
            ("act", v((2 * tok, ff), BF)),
            ("gp", v((2 * tok, ff), BF)),
            ("inn", v((2 * tok, width), BF)),
            ("innt", v((width, 2 * tok), BF)),
            ("gffn", v((2 * tok, width), BF)),
            ("xh", v((2 * tok, width), F32)),
            ("acc", v((2 * tok, width), F32)),
            ("rs", v((2 * tok, 1), F32)),
            ("hbuf", v((2, tok, width), BF)),
            ("grecv", v((2 * tok, width), BF)),
            ("dka", v((seq_len, 128), F32)),
            ("dva", v((seq_len, 128), F32)),
            ("d2", v((2, 8, 2, 2, 2, rows_f, cols_f), BF)),
            ("rc", v((8, 2, 2, 2, rows_f, cols_f), BF)),
            ("dc", v((4, 2, 2, 2, rows_f, cols_f), BF)),
            ("sg8", v((8, small), F32)),
            ("sgs", v((6, 1, small), F32)),
            ("sgr", v((5, 1, small), F32)),
            ("lsem", dma((8,))),
            ("ex_s", dma((9 + pairs,))),
            ("ex_r", dma((9 + pairs,))),
            ("rs_s", dma((FLOWS, 7))),
            ("rs_r", dma((FLOWS, 7))),
            ("sm_s", dma((5,))),
            ("sm_r", dma((5,))),
        ]
        for f in range(FLOWS):
            for k in range(4):
                scratch.append((f"r{f}_{k}", v(recv_shape(ORDERS[f], k, rows_f, cols_f), BF)))
        names = [e[0] for e in ins] + [e[0] for e in outs] + [e[0] for e in scratch]

        def body(*refs):
            layer_kernel(groups, names, *refs)

        hout, gin, fin, sout = pl.pallas_call(
            body,
            out_shape=[jax.ShapeDtypeStruct(e[1], e[2]) for e in outs],
            in_specs=[e[2] for e in ins],
            out_specs=[e[3] for e in outs],
            scratch_shapes=[e[1] for e in scratch],
            compiler_params=pltpu.CompilerParams(
                collective_id=0, has_side_effects=True, vmem_limit_bytes=64 * 1024 * 1024
            ),
            name="layer",
        )(*[e[1] for e in ins])

        def across(values):
            if groups == 1:
                return values
            rows = [[g * groups + i for i in range(groups)] for g in range(8)]
            return lax.psum_scatter(values, "seq", scatter_dimension=0, axis_index_groups=rows, tiled=True)

        def sides(part):
            return jnp.concatenate([part[0], part[1]], axis=-1)

        wide = fin.astype(F32)
        g_outer = across(jnp.concatenate([sides(wide[f]) for f in range(4)], axis=0))
        g_inner = across(jnp.concatenate([wide[f, h] for h in range(2) for f in range(4, 8)], axis=-1))
        g_q, g_k, g_v, g_o = [across(sides(wide[f])) for f in range(8, 12)]
        if groups > 1:
            rows = [[g * groups + i for i in range(groups)] for g in range(8)]
            sout = lax.psum(sout, "seq", axis_index_groups=rows)
        seq = lax.axis_index("seq")
        flat = sout[0]

        def share(i, size):
            return lax.dynamic_slice(flat, (i * width + seq * (size // n_seq),), (size // n_seq,))

        s = [share(i, width) for i in range(8)] + [share(8, ff)]
        return (
            hout,
            gin,
            g_q,
            s[0],
            g_k,
            g_v,
            s[1],
            g_o,
            s[2],
            s[3],
            s[4],
            g_inner,
            s[8],
            g_outer,
            s[5],
            s[6],
            s[7],
        )

    return local


def solution(mesh):
    rows = P("seq", "blk", None)
    placed = (rows, P("seq"), *([P()] * 15), rows)
    mat, one = P("seq", None), P("seq")
    return jax.shard_map(
        build(mesh),
        mesh=mesh,
        in_specs=placed,
        out_specs=(rows, rows, mat, one, mat, mat, one, mat, one, one, one, mat, one, mat, one, one, one),
        check_vma=False,
    )
```

```python
import itertools
import math

import jax
import jax.numpy as jnp
from jax import lax
from jax.experimental import pallas as pl
from jax.experimental.pallas import tpu as pltpu
from jax.sharding import PartitionSpec as P

HD = 64
MESH = pl.DeviceIdType.MESH
BF = jnp.bfloat16
F32 = jnp.float32
LOG2E = math.log2(math.e)
SCALE2 = 0.125 * LOG2E
EPS = 1e-05

PIECES = 12
BITS = ("z1", "z0", "y")
FLOWS = {
    "A0": (0, 0, 384, ("y", "x", "z0", "z1")),
    "A1": (1, 0, 384, ("z0", "y", "x", "z1")),
    "A2": (2, 0, 384, ("z1", "y", "x", "z0")),
    "A3": (3, 0, 384, ("z0", "y", "x", "z1")),
    "B0": (4, 0, 384, ("y", "x", "z0", "z1")),
    "B1": (5, 0, 384, ("x", "y", "z1", "z0")),
    "B2": (6, 0, 384, ("y", "x", "z0", "z1")),
    "B3": (7, 0, 384, ("z1", "z0", "y", "x")),
    "O": (11, 0, 384, ("x", "y", "z0", "z1")),
    "P0": (8, 0, 384, ("y", "x", "z0", "z1")),
    "P1": (9, 0, 384, ("x", "z1", "y", "z0")),
    "P2a": (10, 0, 128, ("y", "z1", "z0", "x")),
    "P2b": (10, 128, 128, ("y", "z1", "x", "z0")),
    "P2c": (10, 256, 128, ("z0", "z1", "y", "x")),
}
PLAN = {
    "dact3": [("A0", -1)],
    "c0": [("A1", -1)],
    "c1": [("A2", -1)],
    "c2": [("A3", -1)],
    "d0": [("B0", -1), ("B1", -1)],
    "d1": [("B2", -1)],
    "d2": [("B3", -1)],
    "up0": [("A0", 0)],
    "att01": [("B1", 0), ("B0", 0), ("A1", 0)],
    "att02": [("A2", 0), ("A0", 1)],
    "att10": [("B2", 0)],
    "att11": [("O", 0)],
    "att12": [("B1", 1)],
    "att13": [("B0", 1), ("A1", 1), ("A3", 0)],
    "part1": [("B3", 0), ("B2", 1)],
    "att20": [("A2", 1), ("A0", 2), ("A1", 2)],
    "att21": [("B1", 2), ("B0", 2)],
    "att23": [("A0", 3), ("P0", 0), ("A1", 3), ("P1", 0), ("B3", 1)],
    "dws2": [("B0", 3), ("A2", 2), ("O", 1), ("B2", 2), ("A0", 4)],
    "part2": [("B1", 3)],
    "gin": [("A0", 5), ("small", 0), ("A3", 1), ("P0", 1)],
    "tail": [
        ("A1", 4), ("B3", 2), ("B0", 4), ("A1", 5), ("B1", 4), ("P2c", 0), ("B0", 5), ("P1", 1), ("P2a", 0),
        ("B1", 5), ("A2", 3), ("B2", 3), ("P2b", 0), ("O", 2), ("P1", 2), ("P2c", 1), ("P2a", 1), ("P0", 2),
        ("P2c", 2), ("small", 1), ("P2b", 1), ("P1", 3), ("P2a", 2), ("A3", 2), ("O", 3), ("B3", 3),
        ("small", 2), ("A2", 4), ("P0", 3), ("B2", 4), ("P2c", 3), ("P2b", 2), ("A2", 5), ("B2", 5), ("P1", 4),
        ("P2a", 3), ("A3", 3), ("small", 3), ("O", 4), ("P1", 5), ("P2b", 3), ("B3", 4), ("P0", 4), ("O", 5),
        ("P2c", 4), ("P2a", 4), ("B3", 5), ("A3", 4), ("P0", 5), ("P2b", 4), ("P2c", 5), ("P2a", 5),
        ("small", 4), ("A3", 5), ("P2b", 5),
    ],
}

NAMES = ("qb", "vb", "ob", "ag", "as", "xb", "fg", "fs", "ib")


def nn(left, right):
    return jnp.dot(left, right, preferred_element_type=F32)


def nt(left, right):
    return lax.dot_general(left, right, (((1,), (1,)), ((), ())), preferred_element_type=F32)


def tn(left, right):
    return lax.dot_general(left, right, (((0,), (0,)), ((), ())), preferred_element_type=F32)


def fold8(values):
    rows, width = values.shape
    return jnp.sum(values.reshape(rows // 8, 8, width), axis=0)


def recv_shape(order, k, rows, cols):
    done = order[: k + 1]
    free = [2 for ax in BITS if ax not in done]
    return (*free, rows // 2 if "x" in done else rows, cols)


def layer_kernel(groups, names, *refs):
    r = dict(zip(names, refs))
    seq = lax.axis_index("seq")
    blk = lax.axis_index("blk")
    x = lax.div(blk, 2)
    c = lax.rem(blk, 2)
    hi = lax.div(seq, groups)
    own = {"x": x, "y": lax.rem(hi, 2), "z0": lax.rem(lax.div(hi, 2), 2), "z1": lax.div(hi, 4)}
    blk_x = blk + 2 - 4 * x
    blk_c = blk + 1 - 2 * c
    blk_xc = blk_x + 1 - 2 * c
    peers = {
        "c": (seq, blk_c),
        "x": (seq, blk_x),
        "y": (seq + (1 - 2 * own["y"]) * groups, blk),
        "z0": (seq + (1 - 2 * own["z0"]) * 2 * groups, blk),
        "z1": (seq + (1 - 2 * own["z1"]) * 4 * groups, blk),
    }
    slots, tok, width = r["xall"].shape
    seq_len = slots * tok
    half = width // 2
    ff = r["wi"].shape[1]
    pairs = half // 128
    mine = (blk, blk_x)
    col0 = pl.multiple_of(c * half, 128)
    place = {name: width * i for i, name in enumerate(NAMES)}

    def vec(name, start=0, size=width):
        return r["vec"][:, pl.ds(place[name] + start, size)]

    def remote(src, dst, send, recv, peer):
        return pltpu.make_async_remote_copy(
            src_ref=src, dst_ref=dst, send_sem=send, recv_sem=recv, device_id=peers[peer], device_id_type=MESH
        )

    barrier = pltpu.get_barrier_semaphore()
    for peer in peers.values():
        pl.semaphore_signal(barrier, inc=1, device_id=peer, device_id_type=MESH)

    def pair_lanes(p):
        return pl.ds(pl.multiple_of(c * half + p * 128, 128), 128)

    lcount = itertools.count()

    def fetch(src, dst):
        return pltpu.make_async_copy(src, dst, r["lsem"].at[next(lcount)])

    first = [fetch(r["hid"].at[x], r["xall"].at[blk])]
    for p in range(pairs):
        for i, w in enumerate(("wq", "wk", "wv")):
            first.append(fetch(r[w].at[:, pair_lanes(p)], r["wcat"].at[:, pl.ds((3 * p + i) * 128, 128)]))
    second = [
        fetch(r["go"].at[x], r["gown"].at[0]),
        fetch(r["wo_in"], r["wo"]),
        fetch(r["wi_in"], r["wi"]),
        fetch(r["wx_in"], r["wx"]),
    ]
    for copy in first + second:
        copy.start()
    for i, name in enumerate(NAMES):
        ref = r["p_" + name]
        r["vec"][:, pl.ds(place[name], ref.shape[0])] = ref[...].astype(F32).reshape(1, ref.shape[0])
    r["sg8"][...] = jnp.zeros_like(r["sg8"])
    kept = jnp.where(r["dg"][x] == 2, 0.0, 1.0).astype(F32)
    pl.semaphore_wait(barrier, len(peers))

    hrows = tok // 2

    def ex(name):
        kind, i = name[:-1], int(name[-1])
        hs = pl.ds(i * hrows, hrows)
        if kind == "hx":
            src, dst, peer = r["hid"].at[1 - x, hs], r["xall"].at[blk, hs], "x"
        elif kind == "hc":
            src, dst, peer = r["hid"].at[x], r["xall"].at[blk], "c"
        elif kind == "hf":
            src, dst, peer = r["xall"].at[blk_x, hs], r["xall"].at[blk_x, hs], "c"
        elif kind == "go":
            src, dst, peer = r["go"].at[1 - x], r["gown"].at[1], "x"
        elif kind == "at":
            src, dst, peer = r["att"].at[:, :, pair_lanes(i)], r["att"].at[:, :, pair_lanes(i)], "c"
        elif kind == "ga":
            src, dst, peer = r["ga"].at[mine[i]], r["ga"].at[mine[i]], "c"
        elif kind == "ho":
            src, dst, peer = r["hbuf"].at[1], r["hout"].at[x], "x"
        elif kind == "gp":
            rows = pl.ds(i * tok, tok)
            src, dst, peer = r["gffn"].at[rows], r["grecv"].at[rows], "c"
        else:
            src, dst, peer = r["inn"].at[pl.ds(tok, tok)], r["gin"].at[x], "x"
        at = EXCHANGES.index(name)
        return remote(src, dst, r["ex_s"].at[at], r["ex_r"].at[at], peer)

    for name in ("hx0", "hx1", "hc0", "go0"):
        ex(name).start()

    lane_head = lax.broadcasted_iota(jnp.int32, (tok, 128), 1) // HD
    ones = jnp.ones((seq_len, 128), BF)
    for p in range(pairs):
        r["vp"][p, :, pl.ds(128, 128)] = ones

    def project(slot, start, rows):
        block = r["xall"][slot, pl.ds(start, rows), :]
        out = nn(block, r["wcat"][...])
        at = pl.ds(pl.multiple_of(slot * tok + start, rows), rows)
        for p in range(pairs):
            lanes = pl.ds(p * 128, 128)
            qbias = r["vec"][:, pair_lanes(p)]
            vbias = r["vec"][:, pl.ds(pl.multiple_of(place["vb"] + c * half + p * 128, 128), 128)]
            base = 3 * p * 128
            r["q"][at, lanes] = (out[:, base : base + 128] + qbias).astype(BF)
            key = out[:, base + 128 : base + 256].astype(BF)
            r["k"][at, lanes] = key
            r["kt"][lanes, at] = key.T
            r["vp"][p, at, pl.ds(0, 128)] = (out[:, base + 256 : base + 384] + vbias).astype(BF)

    for copy in first:
        copy.wait()
    project(blk, 0, tok)
    ex("hc0").wait_recv()
    project(blk_c, 0, tok)
    for i in range(2):
        ex(f"hx{i}").wait_recv()
        ex(f"hf{i}").start()
        project(blk_x, i * hrows, hrows)
    for i in range(2):
        ex(f"hf{i}").wait_recv()
        project(blk_xc, i * hrows, hrows)

    def forward(p, t):
        lanes = pl.ds(p * 128, 128)
        rows = pl.ds(t * tok, tok)
        qp = r["q"][rows, lanes]
        outs, sums = [], []
        for h in range(2):
            qm = jnp.where(lane_head == h, qp, jnp.zeros_like(qp))
            s = nn(qm, r["kt"][lanes, :])
            top = jnp.max(s, axis=1, keepdims=True)
            pt = jnp.exp2((s - top) * SCALE2).astype(BF)
            o = nn(pt, r["vp"][p])
            sums.append(top * SCALE2 + jnp.log2(o[:, 128:]))
            outs.append(o[:, :128] / o[:, 128:])
        r["att"][t, :, pair_lanes(p)] = jnp.where(lane_head == 0, outs[0], outs[1]).astype(BF)
        both = jnp.where(lane_head == 0, sums[0], sums[1]).T
        for h in range(2):
            r["lse"][2 * p + h, :, rows] = both[h * HD : h * HD + 1]

    for p in range(pairs):
        for t in range(slots):
            forward(p, t)
        ex(f"at{p}").start()

    for copy in second:
        copy.wait()
    for p in range(pairs):
        ex(f"at{p}").wait_recv()

    chunk = tok // 2

    def own_rows(i):
        inner = pl.ds((i % 2) * chunk, chunk)
        return mine[i // 2], i // 2, inner, pl.ds(i * chunk, chunk)

    def fold_in(name, values):
        at = pl.ds(place[name], values.shape[1])
        r["sg8"][:, at] += fold8(values)

    for i in range(2):
        r["acc"][pl.ds(i * tok, tok), :] = nn(r["att"][mine[i]], r["wo"][...])

    for i in range(4):
        slot, which, inner, rows = own_rows(i)
        v = r["acc"][rows, :] + vec("ob") + r["xall"][slot, inner, :].astype(F32)
        cen = v - jnp.mean(v, axis=-1, keepdims=True)
        rstd = lax.rsqrt(jnp.mean(cen * cen, axis=-1, keepdims=True) + EPS)
        xh = cen * rstd
        normed = xh * vec("ag") + vec("as")
        r["xh"][rows, :] = xh
        r["rs"][rows, :] = rstd
        r["acc"][rows, :] = normed
        r["inn"][rows, :] = normed.astype(BF)

    tile = 512
    for j in range(ff // tile):
        at = pl.ds(j * tile, tile)
        pre = nn(r["inn"][...], r["wi"][:, at]) + vec("ib", j * tile, tile)
        phi = 0.5 + 0.5 * lax.erf(pre * math.sqrt(0.5))
        dens = jnp.exp2(pre * pre * (-0.5 * LOG2E)) * (1.0 / math.sqrt(2.0 * math.pi))
        r["act"][:, at] = (pre * phi).astype(BF)
        r["gp"][:, at] = (phi + pre * dens).astype(BF)
    for j in range(width // 256):
        at = pl.ds(j * 256, 256)
        r["acc"][:, at] += nn(r["act"][...], r["wx"][:, at])

    ex("go0").wait_recv()
    for i in range(4):
        slot, which, inner, rows = own_rows(i)
        xf = r["xall"][slot, inner, :].astype(F32)
        v = r["acc"][rows, :] + vec("xb")
        cen = v - jnp.mean(v, axis=-1, keepdims=True)
        rstd = lax.rsqrt(jnp.mean(cen * cen, axis=-1, keepdims=True) + EPS)
        xh = cen * rstd
        out = kept * (xh * vec("fg") + vec("fs")) + (1.0 - kept) * xf
        r["hbuf"][which, inner, :] = out.astype(BF)
        g = kept * r["gown"][which, inner, :].astype(F32)
        fold_in("fg", g * xh)
        fold_in("fs", g)
        gx = g * vec("fg")
        m1 = jnp.mean(gx, axis=-1, keepdims=True)
        m2 = jnp.mean(gx * xh, axis=-1, keepdims=True)
        gs = rstd * (gx - m1 - xh * m2)
        low = gs.astype(BF)
        r["acc"][rows, :] = gs
        r["gffn"][rows, :] = low
        fold_in("xb", low.astype(F32))

    ex("ho0").start()
    hout_local = fetch(r["hbuf"].at[0], r["hout"].at[x])
    hout_local.start()

    rows_f = r["dc"].shape[-2]
    flow_id = {name: i for i, name in enumerate(FLOWS)}

    def piece(f):
        return r["d2"].at[c, f] if f < 8 else r["dc"].at[f - 8]

    def view(name, k, send):
        f, start, cols, order = FLOWS[name]
        idx = [slice(None)] * 3
        row = pl.ds(0, rows_f)
        for j, ax in enumerate(order[: k + 1]):
            want = 1 - own[ax] if (j == k and send) else own[ax]
            if ax == "x":
                row = pl.ds(pl.multiple_of(want * (rows_f // 2), 16), rows_f // 2)
            else:
                idx[BITS.index(ax)] = want
        return (*idx, row, pl.ds(start, cols))

    def hop(name, k):
        f, start, cols, order = FLOWS[name]
        i = flow_id[name]
        src = piece(f).at[view(name, k, True)]
        return remote(src, r[f"r_{name}_{k}"], r["rs_s"].at[i, k], r["rs_r"].at[i, k], order[k])

    def add_in(name, k):
        f, start, cols, order = FLOWS[name]
        idx = list(view(name, k, False))
        ref = piece(f)
        free = [ax for ax in BITS if ax not in order[: k + 1]]
        for combo in itertools.product((0, 1), repeat=len(free)):
            for ax, bit in zip(free, combo):
                idx[BITS.index(ax)] = bit
            at = tuple(idx)
            ref[at] = ref[at] + r[f"r_{name}_{k}"][(*combo, slice(None), slice(None))]

    x_rows = pl.ds(pl.multiple_of(x * (rows_f // 2), 16), rows_f // 2)

    def spread(name, k):
        f, start, cols, order = FLOWS[name]
        rows = x_rows if k == 4 else pl.ds(0, rows_f)
        part = r["fin"].at[f, c, rows, pl.ds(start, cols)]
        i = flow_id[name]
        return remote(part, part, r["rs_s"].at[i, k], r["rs_r"].at[i, k], "x" if k == 4 else "c")

    def d2d(name):
        f, i = FLOWS[name][0], flow_id[name]
        return remote(r["d2"].at[1 - c, f], r["rc"].at[f], r["rs_s"].at[i, 6], r["rs_r"].at[i, 6], "c")

    def small(k):
        return remote(
            r["sgs"].at[k], r["sgr"].at[k], r["sm_s"].at[k], r["sm_r"].at[k], ("c", "x", "y", "z0", "z1")[k]
        )

    def step(name, k):
        if name == "small":
            small(k).wait_recv()
            r["sgs"][k + 1] = r["sgs"][k] + r["sgr"][k]
            if k < 4:
                small(k + 1).start()
            return
        f, start, cols, order = FLOWS[name]
        if k == -1:
            d2d(name).wait_recv()
            ref = piece(f)
            for combo in itertools.product((0, 1), repeat=3):
                ref[combo] = ref[combo] + r["rc"][(f, *combo)]
            hop(name, 0).start()
        elif k < 3:
            hop(name, k).wait_recv()
            add_in(name, k)
            hop(name, k + 1).start()
        elif k == 3:
            hop(name, 3).wait_recv()
            add_in(name, 3)
            at = pl.ds(start, cols)
            r["fin"][f, c, x_rows, at] = piece(f)[(own["z1"], own["z0"], own["y"], x_rows, at)]
            spread(name, 4).start()
        elif k == 4:
            spread(name, 4).wait_recv()
            spread(name, 5).start()
        else:
            spread(name, 5).wait_recv()

    def tick(name):
        for flow, k in PLAN.get(name, ()):
            step(flow, k)

    outer_rows = ff // 8
    cols_f = half
    for j in range(8):
        val = tn(r["act"][:, pl.ds(j * outer_rows, outer_rows)], r["gffn"][...]).astype(BF)
        for f in range(4):
            for h in range(2):
                part = val[f * rows_f : (f + 1) * rows_f, h * cols_f : (h + 1) * cols_f]
                r["d2"][h, f, j // 4, (j // 2) % 2, j % 2] = part

    for i in range(4):
        d2d(f"A{i}").start()
    tick("loopB")

    tile = ff // 4
    for j in range(4):
        at = pl.ds(j * tile, tile)
        gpre = (nt(r["gffn"][...], r["wx"][at, :]) * r["gp"][:, at].astype(F32)).astype(BF)
        r["gp"][:, at] = gpre
        r["sg8"][:, pl.ds(place["ib"] + j * tile, tile)] = fold8(gpre.astype(F32))
        tick(f"dact{j}")
    for i, j in enumerate((0, 2, 1, 3)):
        val = tn(r["inn"][...], r["gp"][:, pl.ds(j * tile, tile)]).astype(BF)
        for m in range(2):
            g = 2 * j + m
            part = val[:, m * cols_f : (m + 1) * cols_f]
            r["d2"][g // 4, 4 + g % 4] = part.reshape(2, 2, 2, rows_f, cols_f)
        if i % 2:
            d2d(f"B{i - 1}").start()
            d2d(f"B{i}").start()
        tick(f"c{i}")
    for j in range(3):
        at = pl.ds(j * 256, 256)
        r["acc"][:, at] += nt(r["gp"][...], r["wi"][at, :])
        tick(f"d{j}")

    for i in range(4):
        slot, which, inner, rows = own_rows(i)
        g = r["acc"][rows, :]
        xh = r["xh"][rows, :]
        fold_in("ag", g * xh)
        fold_in("as", g)
        gx = g * vec("ag")
        m1 = jnp.mean(gx, axis=-1, keepdims=True)
        m2 = jnp.mean(gx * xh, axis=-1, keepdims=True)
        gs = r["rs"][rows, :] * (gx - m1 - xh * m2)
        low = gs.astype(BF)
        r["acc"][rows, :] = gs
        r["ga"][slot, inner, :] = low
        fold_in("ob", low.astype(F32))

    ex("ga0").start()
    ex("ga1").start()
    tick("lnb")

    def dqkv(p):
        return r["wx"].at[pl.ds((p // 2) * seq_len, seq_len), pl.ds((p % 2) * 384, 384)]

    do = r["wx"].at[pl.ds(seq_len, seq_len), pl.ds(384, half)]
    wo_own = r["wo"].at[pl.ds(pl.multiple_of(c * half, 128), half), :]
    xt = r["wi"].at[:, pl.ds(0, seq_len)]

    def upstream(slot):
        rows = pl.ds(pl.multiple_of(slot * tok, tok), tok)
        do[rows, :] = nt(r["ga"][slot], wo_own[...]).astype(BF)

    xt[...] = r["xall"][...].reshape(seq_len, width).T
    upstream(blk)
    upstream(blk_x)
    tick("up0")
    ex("ga0").wait_recv()
    ex("ga1").wait_recv()
    upstream(blk_c)
    upstream(blk_xc)

    for p in range(pairs):
        at = r["att"][:, :, pair_lanes(p)].reshape(seq_len, 128)
        prod = (at.astype(F32) * do[:, pl.ds(p * 128, 128)].astype(F32)).T
        for h in range(2):
            r["delta"][2 * p + h] = jnp.sum(prod[h * HD : (h + 1) * HD], axis=0, keepdims=True)
    tick("up1")

    att_all = r["att"][...].reshape(seq_len, width)
    ga_cols = r["ga"][:, :, pl.ds(col0, half)].reshape(seq_len, half)
    r["dc"][3] = tn(att_all, ga_cols).astype(BF).reshape(2, 2, 2, rows_f, cols_f)
    hop("O", 0).start()
    tick("dwo")

    def backward(p, t):
        lanes = pl.ds(p * 128, 128)
        rows = pl.ds(t * tok, tok)
        qp = r["q"][rows, lanes]
        dp = do[rows, lanes]
        kp = r["k"][:, lanes]
        vp = r["vp"][p, :, pl.ds(0, 128)]
        zero = jnp.zeros_like(qp)
        dqs = []
        for h in range(2):
            qm = jnp.where(lane_head == h, qp, zero)
            dm = jnp.where(lane_head == h, dp, zero)
            pt = jnp.exp2(nt(kp, qm) * SCALE2 - r["lse"][2 * p + h, :, rows])
            ds = (pt * (nt(vp, dm) - r["delta"][2 * p + h, :, rows])).astype(BF)
            dv, dk = nn(pt.astype(BF), dm), nn(ds, qm)
            if t == 0 and h == 0:
                r["dva"][...] = dv
                r["dka"][...] = dk
            else:
                r["dva"][...] += dv
                r["dka"][...] += dk
            dqs.append(nn(r["kt"][pl.ds(p * 128 + h * HD, HD), :], ds))
        both = (jnp.concatenate(dqs, axis=0) * 0.125).astype(BF)
        dqkv(p)[rows, pl.ds(0, 128)] = both.T

    def partial(p, slot):
        rows = pl.ds(pl.multiple_of(slot * tok, tok), tok)
        return nt(dqkv(p)[rows, :], r["wcat"][:, pl.ds(p * 384, 384)])

    def weight_part(p):
        r["dc"][p] = nn(xt[...], dqkv(p)[...]).astype(BF).reshape(2, 2, 2, rows_f, cols_f)
        r["sg8"][:, pair_lanes(p)] = fold8(dqkv(p)[:, pl.ds(0, 128)].astype(F32))
        at = pl.ds(pl.multiple_of(place["vb"] + c * half + p * 128, 128), 128)
        r["sg8"][:, at] = fold8(dqkv(p)[:, pl.ds(256, 128)].astype(F32))
        for name in FLOWS:
            if name.startswith(f"P{p}"):
                hop(name, 0).start()

    def other_part(p, i):
        rows = pl.ds(i * tok, tok)
        part = partial(p, (blk_c, blk_xc)[i])
        if p == 0:
            r["xh"][rows, :] = part
        elif p < pairs - 1:
            r["xh"][rows, :] += part
        else:
            r["gffn"][rows, :] = (r["xh"][rows, :] + part).astype(BF)

    def own_part(p, i):
        r["acc"][pl.ds(i * tok, tok), :] += partial(p, mine[i])

    for p in range(pairs):
        for t in range(slots):
            backward(p, t)
            if t == slots - 1:
                dqkv(p)[:, pl.ds(128, 128)] = (r["dka"][...] * 0.125).astype(BF)
                dqkv(p)[:, pl.ds(256, 128)] = r["dva"][...].astype(BF)
            tick(f"att{p}{t}")
        if p < pairs - 1:
            weight_part(p)
            tick(f"dws{p}")
            for i in range(2):
                other_part(p, i)
                own_part(p, i)
            tick(f"part{p}")
        else:
            for i in (1, 0):
                other_part(p, i)
                ex(f"gp{i}").start()
            weight_part(p)
            r["sgs"][0] = jnp.sum(r["sg8"][...], axis=0, keepdims=True)
            small(0).start()
            tick(f"dws{p}")
            for i in (1, 0):
                own_part(p, i)
            tick(f"part{p}")

    for i in (1, 0):
        rows = pl.ds(i * tok, tok)
        ex(f"gp{i}").wait_recv()
        total = r["acc"][rows, :] + r["grecv"][rows, :].astype(F32) + (1.0 - kept) * r["gown"][i].astype(F32)
        r["inn"][rows, :] = total.astype(BF)
        if i == 1:
            ex("gi0").start()
    gin_local = fetch(r["inn"].at[pl.ds(0, tok)], r["gin"].at[x])
    gin_local.start()
    tick("gin")
    tick("tail")
    r["sout"][...] = r["sgs"][5]

    ex("ho0").wait_recv()
    ex("gi0").wait_recv()
    hout_local.wait()
    gin_local.wait()
    for name in EXCHANGES:
        ex(name).wait_send()
    for k in range(5):
        small(k).wait_send()
    for name in FLOWS:
        for k in range(4):
            hop(name, k).wait_send()
        spread(name, 4).wait_send()
        spread(name, 5).wait_send()
        if FLOWS[name][0] < 8:
            d2d(name).wait_send()


EXCHANGES = (
    "hx0", "hx1", "hc0", "hf0", "hf1", "go0", "at0", "at1", "at2", "ga0", "ga1", "ho0", "gp0", "gp1", "gi0"
)


def finish_kernel(n_seq, names, *refs):
    r = dict(zip(names, refs))
    copies = [
        pltpu.make_async_copy(r["hout_in"], r["hout"], r["sem"].at[0]),
        pltpu.make_async_copy(r["gin_in"], r["gin"], r["sem"].at[1]),
    ]
    for copy in copies:
        copy.start()
    fin = r["fin"]
    rows_f, cols_f = fin.shape[2:]
    half = cols_f
    for h in range(2):
        for f in range(4):
            r["outer"][pl.ds(f * rows_f, rows_f), pl.ds(h * half, half)] = fin[f, h].astype(F32)
            r["inner"][:, pl.ds((4 * h + f) * cols_f, cols_f)] = fin[4 + f, h].astype(F32)
        r["output"][:, pl.ds(h * half, half)] = fin[11, h].astype(F32)
        for p in range(half // 128):
            for i, name in enumerate(("query", "key", "value")):
                part = fin[8 + p, h, :, pl.ds(i * 128, 128)].astype(F32)
                r[name][:, pl.ds(h * half + p * 128, 128)] = part
    seq = lax.axis_index("seq")
    width = 2 * half
    share = width // n_seq
    for i in range(8):
        r["rows"][pl.ds(i, 1), :] = r["sout"][:, pl.ds(i * width, width)]
    turned = pltpu.roll(r["rows"][...], lax.rem(width - seq * share, width), 1)
    for i, name in enumerate(NAMES[:-1]):
        r["s_" + name][...] = turned[i, :share]
    ib = r["s_ib"].shape[0]
    full = r["sout"].shape[1] - 8 * width
    r["wide"][...] = jnp.broadcast_to(r["sout"][:, pl.ds(8 * width, full)], (8, full))
    r["s_ib"][...] = pltpu.roll(r["wide"][...], lax.rem(full - seq * ib, full), 1)[0, :ib]
    for copy in copies:
        copy.wait()


def build(mesh):
    n_seq = mesh.shape["seq"]
    groups = n_seq // 8

    def local(
        hidden_in,
        depth_group,
        query_weight,
        query_bias,
        key_weight,
        value_weight,
        value_bias,
        output_weight,
        output_bias,
        attn_gain,
        attn_shift,
        inner_weight,
        inner_bias,
        outer_weight,
        outer_bias,
        final_gain,
        final_shift,
        grad_out,
    ):
        seqs, tok, width = hidden_in.shape
        ff = inner_weight.shape[1]
        slots = mesh.shape["blk"]
        seq_len = slots * tok
        half = width // 2
        heads = half // HD
        pairs = half // 128
        rows_f, cols_f = width // 8, half
        small = 8 * width + ff
        hbm = pl.BlockSpec(memory_space=pl.ANY)
        vmem = pl.BlockSpec(memory_space=pltpu.VMEM)
        vectors = (
            query_bias, value_bias, output_bias, attn_gain, attn_shift, outer_bias, final_gain, final_shift, inner_bias
        )
        ins = [("p_" + name, value, vmem) for name, value in zip(NAMES, vectors)] + [
            ("dg", depth_group, pl.BlockSpec(memory_space=pltpu.SMEM)),
            ("hid", hidden_in, hbm),
            ("go", grad_out, hbm),
            ("wq", query_weight, hbm),
            ("wk", key_weight, hbm),
            ("wv", value_weight, hbm),
            ("wo_in", output_weight, hbm),
            ("wi_in", inner_weight, hbm),
            ("wx_in", outer_weight, hbm),
        ]
        outs = [
            ("hout", (seqs, tok, width), BF, hbm),
            ("gin", (seqs, tok, width), BF, hbm),
            ("fin", (PIECES, 2, rows_f, cols_f), BF, vmem),
            ("sout", (1, small), F32, vmem),
        ]
        v = pltpu.VMEM
        dma = pltpu.SemaphoreType.DMA
        scratch = [
            ("vec", v((1, small), F32)),
            ("xall", v((slots, tok, width), BF)),
            ("gown", v((2, tok, width), BF)),
            ("wcat", v((width, 3 * half), BF)),
            ("wo", v((width, width), BF)),
            ("wi", v((width, ff), BF)),
            ("wx", v((ff, width), BF)),
            ("q", v((seq_len, half), BF)),
            ("k", v((seq_len, half), BF)),
            ("kt", v((half, seq_len), BF)),
            ("vp", v((pairs, seq_len, 256), BF)),
            ("lse", v((heads, 1, seq_len), F32)),
            ("delta", v((heads, 1, seq_len), F32)),
            ("att", v((slots, tok, width), BF)),
            ("ga", v((slots, tok, width), BF)),
            ("act", v((2 * tok, ff), BF)),
            ("gp", v((2 * tok, ff), BF)),
            ("inn", v((2 * tok, width), BF)),
            ("gffn", v((2 * tok, width), BF)),
            ("xh", v((2 * tok, width), F32)),
            ("acc", v((2 * tok, width), F32)),
            ("rs", v((2 * tok, 1), F32)),
            ("hbuf", v((2, tok, width), BF)),
            ("grecv", v((2 * tok, width), BF)),
            ("dka", v((seq_len, 128), F32)),
            ("dva", v((seq_len, 128), F32)),
            ("d2", v((2, 8, 2, 2, 2, rows_f, cols_f), BF)),
            ("rc", v((8, 2, 2, 2, rows_f, cols_f), BF)),
            ("dc", v((4, 2, 2, 2, rows_f, cols_f), BF)),
            ("sg8", v((8, small), F32)),
            ("sgs", v((6, 1, small), F32)),
            ("sgr", v((5, 1, small), F32)),
            ("lsem", dma((7 + 3 * pairs,))),
            ("ex_s", dma((len(EXCHANGES),))),
            ("ex_r", dma((len(EXCHANGES),))),
            ("rs_s", dma((len(FLOWS), 7))),
            ("rs_r", dma((len(FLOWS), 7))),
            ("sm_s", dma((5,))),
            ("sm_r", dma((5,))),
        ]
        for name, (f, start, cols, order) in FLOWS.items():
            for k in range(4):
                scratch.append((f"r_{name}_{k}", v(recv_shape(order, k, rows_f, cols), BF)))
        names = [e[0] for e in ins] + [e[0] for e in outs] + [e[0] for e in scratch]

        def body(*refs):
            layer_kernel(groups, names, *refs)

        hout, gin, fin, sout = pl.pallas_call(
            body,
            out_shape=[jax.ShapeDtypeStruct(e[1], e[2]) for e in outs],
            in_specs=[e[2] for e in ins],
            out_specs=[e[3] for e in outs],
            scratch_shapes=[e[1] for e in scratch],
            compiler_params=pltpu.CompilerParams(
                collective_id=0, has_side_effects=True, vmem_limit_bytes=64 * 1024 * 1024
            ),
            name="layer",
        )(*[e[1] for e in ins])

        rows = [[g * groups + i for i in range(groups)] for g in range(8)]
        if groups > 1:
            sout = lax.psum(sout, "seq", axis_index_groups=rows)
        mats = ("query", "key", "value", "output", "inner", "outer")
        tail_ins = [("hout_in", hout, hbm), ("gin_in", gin, hbm), ("fin", fin, vmem), ("sout", sout, vmem)]
        tail_outs = [("hout", hout.shape, BF, hbm), ("gin", gin.shape, BF, hbm)]
        tail_outs += [(name, (rows_f, width), F32, vmem) for name in mats[:4]]
        tail_outs += [("inner", (rows_f, ff), F32, vmem), ("outer", (ff // 8, width), F32, vmem)]
        tail_outs += [("s_" + name, (width // n_seq,), F32, vmem) for name in NAMES[:-1]]
        tail_outs += [("s_ib", (ff // n_seq,), F32, vmem)]
        tail_scratch = [("sem", dma((2,))), ("rows", v((8, width), F32)), ("wide", v((8, ff), F32))]
        tail_names = [e[0] for e in tail_ins] + [e[0] for e in tail_outs] + [e[0] for e in tail_scratch]

        def tail_body(*refs):
            finish_kernel(n_seq, tail_names, *refs)

        res = pl.pallas_call(
            tail_body,
            out_shape=[jax.ShapeDtypeStruct(e[1], e[2]) for e in tail_outs],
            in_specs=[e[2] for e in tail_ins],
            out_specs=[e[3] for e in tail_outs],
            scratch_shapes=[e[1] for e in tail_scratch],
            compiler_params=pltpu.CompilerParams(vmem_limit_bytes=32 * 1024 * 1024),
            name="finish",
        )(*[e[1] for e in tail_ins])
        o = {e[0]: value for e, value in zip(tail_outs, res)}
        if groups > 1:
            for name in mats:
                o[name] = lax.psum_scatter(o[name], "seq", scatter_dimension=0, axis_index_groups=rows, tiled=True)
        order = (
            "hout", "gin", "query", "s_qb", "key", "value", "s_vb", "output", "s_ob", "s_ag", "s_as", "inner",
            "s_ib", "outer", "s_xb", "s_fg", "s_fs",
        )
        return tuple(o[name] for name in order)

    return local


def solution(mesh):
    rows = P("seq", "blk", None)
    placed = (rows, P("seq"), *([P()] * 15), rows)
    mat, one = P("seq", None), P("seq")
    return jax.shard_map(
        build(mesh),
        mesh=mesh,
        in_specs=placed,
        out_specs=(rows, rows, mat, one, mat, mat, one, mat, one, one, one, mat, one, mat, one, one, one),
        check_vma=False,
    )
```

```python
import itertools
import math
from types import SimpleNamespace

import jax
import jax.numpy as jnp
from jax import lax
from jax.experimental import pallas as pl
from jax.experimental.pallas import tpu as pltpu
from jax.sharding import PartitionSpec as P

HD = 64
MESH = pl.DeviceIdType.MESH
BF = jnp.bfloat16
F32 = jnp.float32
LOG2E = math.log2(math.e)
SCALE2 = 0.125 * LOG2E
EPS = 1e-05

X, Y, Z0, Z1, C = range(5)
BITS = (Z1, Z0, Y)

PIECES = 12
OUTER, INNER, OUTPUT, PAIR = range(4)
S1, S2 = -1, -2
SMALL_ORDER = {S1: (C, Y, Z0, Z1, X), S2: (X, C, Y, Z0, Z1)}
FLOWS = (
    (OUTER, 0, 1, 0, 384, (Z0, X, Z1, Y)),
    (OUTER, 1, 1, 0, 384, (Y, X, Z1, Z0)),
    (OUTER, 2, 1, 0, 384, (Y, X, Z0, Z1)),
    (OUTER, 3, 1, 0, 384, (Y, Z0, Z1, X)),
    (INNER, 4, 1, 0, 384, (Z0, Y, X, Z1)),
    (INNER, 5, 1, 0, 384, (X, Z0, Z1, Y)),
    (INNER, 6, 1, 0, 384, (Z1, Y, Z0, X)),
    (INNER, 7, 1, 0, 384, (Y, X, Z0, Z1)),
    (OUTPUT, 11, 1, 0, 256, (Y, Z0, Z1, X)),
    (OUTPUT, 11, 1, 256, 128, (X, Y, Z0, Z1)),
    (PAIR, 8, 1, 0, 256, (X, Y, Z0, Z1)),
    (PAIR, 8, 1, 256, 128, (X, Y, Z1, Z0)),
    (PAIR + 1, 9, 1, 0, 256, (X, Y, Z1, Z0)),
    (PAIR + 1, 9, 1, 256, 128, (Y, Z0, Z1, X)),
    (PAIR + 2, 10, 1, 0, 128, (Y, Z0, Z1, X)),
    (PAIR + 2, 10, 1, 128, 128, (Y, Z0, Z1, X)),
    (PAIR + 2, 10, 1, 256, 128, (Z0, Y, Z1, X)),
)
PLAN = (
    (),
    (),
    (),
    (),
    ((0, -1), (1, -1)),
    (),
    ((2, -1),),
    ((3, -1),),
    ((4, -1),),
    ((5, -1),),
    ((6, -1),),
    ((7, -1),),
    ((0, 0), (1, 0)),
    (),
    ((S1, 0),),
    (),
    ((5, 0),),
    ((2, 0),),
    ((0, 1),),
    (),
    ((1, 1),),
    ((4, 0), (3, 0), (6, 0), (9, 0)),
    (),
    ((0, 2), (2, 1)),
    (),
    ((5, 1), (7, 0), (1, 2), (S1, 1)),
    ((10, 0), (3, 1)),
    (),
    ((11, 0), (8, 0), (2, 2)),
    ((5, 2), (1, 3), (7, 1), (4, 1)),
    ((S1, 2), (3, 2)),
    ((6, 1), (12, 0), (2, 3), (8, 1), (9, 1), (1, 4)),
    ((0, 3), (S1, 3), (4, 2), (7, 2)),
    ((13, 0), (3, 3)),
    ((2, 4), (S2, 0), (8, 2)),
    (
        (1, 5), (3, 5), (6, 2), (10, 1), (0, 4), (2, 5), (S2, 1), (S1, 4), (9, 2), (11, 1), (4, 3), (5, 3),
        (0, 5), (7, 3), (12, 1), (16, 0), (9, 3), (11, 2), (13, 1), (14, 0), (10, 2), (15, 0), (11, 3), (S2, 2),
        (12, 2), (16, 1), (13, 2), (14, 1), (8, 3), (10, 3), (15, 1), (8, 5), (S2, 3), (6, 3), (16, 2), (4, 4),
        (12, 3), (6, 5), (5, 4), (14, 2), (4, 5), (7, 4), (9, 4), (11, 4), (15, 2), (5, 5), (S2, 4), (13, 3),
        (7, 5), (9, 5), (10, 4), (11, 5), (16, 3), (12, 4), (13, 5), (14, 3), (10, 5), (15, 3), (16, 5), (12, 5),
        (14, 5), (15, 5),
    ),
)

QB, VB, OB, AG, AS, XB, FG, FS, IB = range(9)
HX, HC, HF, GO, GA, HO, GP, GI, AT = 0, 2, 3, 5, 6, 7, 8, 10, 11


def nn(left, right):
    return jnp.dot(left, right, preferred_element_type=F32)


def nt(left, right):
    return lax.dot_general(left, right, (((1,), (1,)), ((), ())), preferred_element_type=F32)


def tn(left, right):
    return lax.dot_general(left, right, (((0,), (0,)), ((), ())), preferred_element_type=F32)


def fold8(values):
    rows, width = values.shape
    return jnp.sum(values.reshape(rows // 8, 8, width), axis=0)


def halves_rows(order, k):
    return X in order[: k + 1] and order.index(X) < 3


def recv_shape(flow, k, rows):
    part, f, nf, start, cols, order = flow
    free = [2 for ax in BITS if ax not in order[: k + 1]]
    return (nf, *free, rows // 2 if halves_rows(order, k) else rows, cols)


def layer_kernel(groups, names, *refs):
    r = SimpleNamespace(**dict(zip(names, refs)))
    seq = lax.axis_index("seq")
    blk = lax.axis_index("blk")
    x = lax.div(blk, 2)
    c = lax.rem(blk, 2)
    hi = lax.div(seq, groups)
    own = {X: x, Y: lax.rem(hi, 2), Z0: lax.rem(lax.div(hi, 2), 2), Z1: lax.div(hi, 4)}
    peers = {
        C: (seq, blk + 1 - 2 * c),
        X: (seq, blk + 2 - 4 * x),
        Y: (seq + (1 - 2 * own[Y]) * groups, blk),
        Z0: (seq + (1 - 2 * own[Z0]) * 2 * groups, blk),
        Z1: (seq + (1 - 2 * own[Z1]) * 4 * groups, blk),
    }
    tok, width = r.xall.shape[2:]
    slots = 4
    seq_len = slots * tok
    half = width // 2
    ff = r.wi.shape[1]
    pairs = half // 128
    me, at_x, at_c, at_xc = (x, c), (1 - x, c), (x, 1 - c), (1 - x, 1 - c)
    mine = (me, at_x)
    own_heads = pl.ds(pl.multiple_of(c * half, 128), half)
    other_heads = pl.ds(pl.multiple_of((1 - c) * half, 128), half)

    def seq_rows(slot, start=0, rows=tok):
        return pl.ds(pl.multiple_of((2 * slot[0] + slot[1]) * tok + start, rows), rows)

    def vec(i, start=0, size=width):
        return r.vec[:, pl.ds(width * i + start, size)]

    def pair_lanes(p, base=0):
        return pl.ds(pl.multiple_of(base * width + c * half + p * 128, 128), 128)

    def remote(src, dst, send, recv, peer):
        return pltpu.make_async_remote_copy(
            src_ref=src, dst_ref=dst, send_sem=send, recv_sem=recv, device_id=peers[peer], device_id_type=MESH
        )

    barrier = pltpu.get_barrier_semaphore()
    for peer in peers.values():
        pl.semaphore_signal(barrier, inc=1, device_id=peer, device_id_type=MESH)

    lcount = itertools.count()

    def fetch(src, dst):
        return pltpu.make_async_copy(src, dst, r.lsem.at[next(lcount)])

    first = [fetch(r.hid.at[x], r.xall.at[me])]
    for p in range(pairs):
        for i, w in enumerate((r.wq, r.wk, r.wv)):
            first.append(fetch(w.at[:, pair_lanes(p)], r.wcat.at[:, pl.ds((3 * p + i) * 128, 128)]))
    second = [
        fetch(r.go.at[x], r.gown.at[0]),
        fetch(r.wo_in, r.wo),
        fetch(r.wi_in, r.wi),
        fetch(r.wx_in, r.wx),
    ]
    for copy in first + second:
        copy.start()
    params = (r.qb, r.vb, r.ob, r.ag, r.sh, r.xb, r.fg, r.fs, r.ib)
    for i, ref in enumerate(params):
        r.vec[:, pl.ds(width * i, ref.shape[0])] = ref[...].astype(F32).reshape(1, ref.shape[0])
    r.sg8[...] = jnp.zeros_like(r.sg8)
    kept = jnp.where(r.dg[x] == 2, 0.0, 1.0).astype(F32)
    pl.semaphore_wait(barrier, len(peers))

    hrows = tok // 2

    def ex(i):
        if i < HC:
            hs = pl.ds((i - HX) * hrows, hrows)
            src, dst, peer = r.hid.at[1 - x, hs], r.xall.at[x, c, hs], X
        elif i == HC:
            src, dst, peer = r.hid.at[x], r.xall.at[me], C
        elif i < GO:
            hs = pl.ds((i - HF) * hrows, hrows)
            src = dst = r.xall.at[1 - x, c, hs]
            peer = C
        elif i == GO:
            src, dst, peer = r.go.at[1 - x], r.gown.at[1], X
        elif i == GA:
            src = dst = r.ga.at[:, c]
            peer = C
        elif i == HO:
            src, dst, peer = r.hbuf.at[1], r.hout.at[x], X
        elif i < GI:
            rows = pl.ds((i - GP) * tok, tok)
            src, dst, peer = r.gffn.at[rows], r.grecv.at[rows], C
        elif i == GI:
            src, dst, peer = r.inn.at[pl.ds(tok, tok)], r.gin.at[x], X
        else:
            core = c if (i - AT) % 2 else 1 - c
            src = dst = r.att.at[:, core, :, pair_lanes((i - AT) // 2)]
            peer = C
        return remote(src, dst, r.ex_s.at[i], r.ex_r.at[i], peer)

    for i in (HX, HX + 1, HC, GO):
        ex(i).start()

    lane_head = lax.broadcasted_iota(jnp.int32, (tok, 128), 1) // HD
    ones = jnp.ones((seq_len, 128), BF)
    for p in range(pairs):
        r.vp[p, :, pl.ds(128, 128)] = ones

    def project(slot, start, rows):
        out = nn(r.xall[(*slot, pl.ds(start, rows), slice(None))], r.wcat[...])
        at = seq_rows(slot, start, rows)
        for p in range(pairs):
            lanes = pl.ds(p * 128, 128)
            base = 3 * p * 128
            r.q[at, lanes] = (out[:, base : base + 128] + r.vec[:, pair_lanes(p, QB)]).astype(BF)
            key = out[:, base + 128 : base + 256].astype(BF)
            r.k[at, lanes] = key
            r.kt[lanes, at] = key.T
            r.vp[p, at, pl.ds(0, 128)] = (out[:, base + 256 : base + 384] + r.vec[:, pair_lanes(p, VB)]).astype(BF)

    for copy in first:
        copy.wait()
    project(me, 0, tok)
    ex(HC).wait_recv()
    project(at_c, 0, tok)
    for i in range(2):
        ex(HX + i).wait_recv()
        ex(HF + i).start()
        project(at_x, i * hrows, hrows)
    for i in range(2):
        ex(HF + i).wait_recv()
        project(at_xc, i * hrows, hrows)

    def forward(p, slot):
        lanes = pl.ds(p * 128, 128)
        rows = seq_rows(slot)
        qp = r.q[rows, lanes]
        outs, sums = [], []
        for h in range(2):
            qm = jnp.where(lane_head == h, qp, jnp.zeros_like(qp))
            s = nn(qm, r.kt[lanes, :])
            top = jnp.max(s, axis=1, keepdims=True)
            pt = jnp.exp2((s - top) * SCALE2).astype(BF)
            o = nn(pt, r.vp[p])
            sums.append(top * SCALE2 + jnp.log2(o[:, 128:]))
            outs.append(o[:, :128] / o[:, 128:])
        r.att[(*slot, slice(None), pair_lanes(p))] = jnp.where(lane_head == 0, outs[0], outs[1]).astype(BF)
        both = jnp.where(lane_head == 0, sums[0], sums[1]).T
        for h in range(2):
            r.lse[2 * p + h, :, rows] = both[h * HD : h * HD + 1]

    for p in range(pairs):
        forward(p, at_c)
        forward(p, at_xc)
        ex(AT + 2 * p).start()
        forward(p, me)
        forward(p, at_x)
        ex(AT + 2 * p + 1).start()

    for copy in second:
        copy.wait()
    chunk = tok // 2

    def own_rows(i):
        inner = pl.ds((i % 2) * chunk, chunk)
        return mine[i // 2], i // 2, inner, pl.ds(i * chunk, chunk)

    def fold_in(i, values):
        at = pl.ds(width * i, values.shape[1])
        r.sg8[:, at] += fold8(values)

    def heads_out(i, heads):
        return nn(r.att[(*mine[i], slice(None), heads)], r.wo[heads, :])

    for i in range(2):
        r.acc[pl.ds(i * tok, tok), :] = heads_out(i, own_heads)
    for p in range(pairs):
        ex(AT + 2 * p).wait_recv()
    for i in range(2):
        r.acc[pl.ds(i * tok, tok), :] += heads_out(i, other_heads)

    for i in range(4):
        slot, which, inner, rows = own_rows(i)
        v = r.acc[rows, :] + vec(OB) + r.xall[(*slot, inner, slice(None))].astype(F32)
        cen = v - jnp.mean(v, axis=-1, keepdims=True)
        rstd = lax.rsqrt(jnp.mean(cen * cen, axis=-1, keepdims=True) + EPS)
        xh = cen * rstd
        normed = xh * vec(AG) + vec(AS)
        r.xh[rows, :] = xh
        r.rs[rows, :] = rstd
        r.acc[rows, :] = normed
        r.inn[rows, :] = normed.astype(BF)

    tile = 512
    for j in range(ff // tile):
        at = pl.ds(j * tile, tile)
        pre = nn(r.inn[...], r.wi[:, at]) + vec(IB, j * tile, tile)
        phi = 0.5 + 0.5 * lax.erf(pre * math.sqrt(0.5))
        dens = jnp.exp2(pre * pre * (-0.5 * LOG2E)) * (1.0 / math.sqrt(2.0 * math.pi))
        r.act[:, at] = (pre * phi).astype(BF)
        r.gp[:, at] = (phi + pre * dens).astype(BF)
    for j in range(width // 256):
        at = pl.ds(j * 256, 256)
        r.acc[:, at] += nn(r.act[...], r.wx[:, at])

    ex(GO).wait_recv()
    for i in range(4):
        slot, which, inner, rows = own_rows(i)
        xf = r.xall[(*slot, inner, slice(None))].astype(F32)
        v = r.acc[rows, :] + vec(XB)
        cen = v - jnp.mean(v, axis=-1, keepdims=True)
        rstd = lax.rsqrt(jnp.mean(cen * cen, axis=-1, keepdims=True) + EPS)
        xh = cen * rstd
        out = kept * (xh * vec(FG) + vec(FS)) + (1.0 - kept) * xf
        r.hbuf[which, inner, :] = out.astype(BF)
        g = kept * r.gown[which, inner, :].astype(F32)
        fold_in(FG, g * xh)
        fold_in(FS, g)
        gx = g * vec(FG)
        m1 = jnp.mean(gx, axis=-1, keepdims=True)
        m2 = jnp.mean(gx * xh, axis=-1, keepdims=True)
        gs = rstd * (gx - m1 - xh * m2)
        low = gs.astype(BF)
        r.acc[rows, :] = gs
        r.gffn[rows, :] = low
        fold_in(XB, low.astype(F32))

    ex(HO).start()
    hout_local = fetch(r.hbuf.at[0], r.hout.at[x])
    hout_local.start()

    rows_f, cols_f = r.dc.shape[-2:]
    x_rows = pl.ds(pl.multiple_of(x * (rows_f // 2), 16), rows_f // 2)

    def pieces(flow):
        f, nf = flow[1:3]
        return r.d2.at[c, pl.ds(f, nf)] if f < 8 else r.dc.at[pl.ds(f - 8, nf)]

    def view(flow, k, send):
        part, f, nf, start, cols, order = flow
        idx = [slice(None)] * 3
        row = pl.ds(0, rows_f)
        for j, ax in enumerate(order[: k + 1]):
            want = 1 - own[ax] if (j == k and send) else own[ax]
            if ax != X:
                idx[BITS.index(ax)] = want
            elif j < 3:
                row = pl.ds(pl.multiple_of(want * (rows_f // 2), 16), rows_f // 2)
        return (slice(None), *idx, row, pl.ds(start, cols))

    def hop(i, k):
        flow = FLOWS[i]
        src = pieces(flow).at[view(flow, k, True)]
        return remote(src, r.land[i][k], r.rs_s.at[i, k], r.rs_r.at[i, k], flow[5][k])

    def add_in(i, k):
        flow = FLOWS[i]
        nf, order = flow[2], flow[5]
        idx = list(view(flow, k, False))
        ref = pieces(flow)
        free = [ax for ax in BITS if ax not in order[: k + 1]]
        for n in range(nf):
            idx[0] = n
            for combo in itertools.product((0, 1), repeat=len(free)):
                for ax, bit in zip(free, combo):
                    idx[1 + BITS.index(ax)] = bit
                at = tuple(idx)
                ref[at] = ref[at] + r.land[i][k][(n, *combo, slice(None), slice(None))]

    def spread(i, k):
        part, f, nf, start, cols, order = FLOWS[i]
        rows = x_rows if k == 4 else pl.ds(0, rows_f)
        ref = r.fin.at[pl.ds(f, nf), c, rows, pl.ds(start, cols)]
        return remote(ref, ref, r.rs_s.at[i, k], r.rs_r.at[i, k], X if k == 4 else C)

    def core_sum(i):
        part, f, nf, start, cols, order = FLOWS[i]
        at = pl.ds(f, nf)
        return remote(r.d2.at[1 - c, at], r.rc.at[at], r.rs_s.at[i, 6], r.rs_r.at[i, 6], C)

    def small(which, k):
        send, recv = (r.s1s, r.s1r) if which == S1 else (r.s2s, r.s2r)
        at = k if which == S1 else 5 + k
        return remote(send.at[k], recv.at[k], r.sm_s.at[at], r.sm_r.at[at], SMALL_ORDER[which][k])

    def step(i, k):
        if i < 0:
            send, recv = (r.s1s, r.s1r) if i == S1 else (r.s2s, r.s2r)
            small(i, k).wait_recv()
            send[k + 1] = send[k] + recv[k]
            if k < 4:
                small(i, k + 1).start()
            return
        flow = FLOWS[i]
        part, f, nf, start, cols, order = flow
        if k == -1:
            core_sum(i).wait_recv()
            ref = pieces(flow)
            for combo in itertools.product(range(nf), (0, 1), (0, 1), (0, 1)):
                ref[combo] = ref[combo] + r.rc[(f + combo[0], *combo[1:])]
            hop(i, 0).start()
        elif k < 3:
            hop(i, k).wait_recv()
            add_in(i, k)
            hop(i, k + 1).start()
        elif k == 3:
            hop(i, 3).wait_recv()
            rows = pl.ds(0, rows_f) if order[3] == X else x_rows
            at = pl.ds(start, cols)
            for n in range(nf):
                mine_part = pieces(flow)[(n, own[Z1], own[Z0], own[Y], rows, at)]
                r.fin[f + n, c, rows, at] = mine_part + r.land[i][3][n]
            spread(i, 5 if order[3] == X else 4).start()
        elif k == 4:
            spread(i, 4).wait_recv()
            spread(i, 5).start()
        else:
            spread(i, 5).wait_recv()

    plan = iter(PLAN)

    def tick():
        for i, k in next(plan):
            step(i, k)

    def begin(part):
        for i, flow in enumerate(FLOWS):
            if flow[0] == part:
                (core_sum(i) if flow[1] < 8 else hop(i, 0)).start()

    outer_rows = ff // 8
    for j in range(8):
        val = tn(r.act[:, pl.ds(j * outer_rows, outer_rows)], r.gffn[...]).astype(BF)
        for f in range(4):
            for h in range(2):
                part = val[f * rows_f : (f + 1) * rows_f, h * cols_f : (h + 1) * cols_f]
                r.d2[h, f, j // 4, (j // 2) % 2, j % 2] = part

    begin(OUTER)
    tick()

    tile = ff // 4
    for j in range(4):
        at = pl.ds(j * tile, tile)
        gpre = (nt(r.gffn[...], r.wx[at, :]) * r.gp[:, at].astype(F32)).astype(BF)
        r.gp[:, at] = gpre
        r.sg8[:, pl.ds(width * IB + j * tile, tile)] = fold8(gpre.astype(F32))
        tick()
    for i, j in enumerate((0, 2, 1, 3)):
        val = tn(r.inn[...], r.gp[:, pl.ds(j * tile, tile)]).astype(BF)
        for m in range(2):
            g = 2 * j + m
            part = val[:, m * cols_f : (m + 1) * cols_f]
            r.d2[g // 4, 4 + g % 4] = part.reshape(2, 2, 2, rows_f, cols_f)
        if i % 2:
            for n, flow in enumerate(FLOWS):
                if flow[0] == INNER and flow[1] + flow[2] - 4 in (i, i + 1):
                    core_sum(n).start()
        tick()
    for j in range(3):
        at = pl.ds(j * 256, 256)
        r.acc[:, at] += nt(r.gp[...], r.wi[at, :])
        tick()

    for i in range(4):
        slot, which, inner, rows = own_rows(i)
        g = r.acc[rows, :]
        xh = r.xh[rows, :]
        fold_in(AG, g * xh)
        fold_in(AS, g)
        gx = g * vec(AG)
        m1 = jnp.mean(gx, axis=-1, keepdims=True)
        m2 = jnp.mean(gx * xh, axis=-1, keepdims=True)
        gs = r.rs[rows, :] * (gx - m1 - xh * m2)
        low = gs.astype(BF)
        r.acc[rows, :] = gs
        r.ga[(*slot, inner, slice(None))] = low
        fold_in(OB, low.astype(F32))

    ex(GA).start()
    late = 2 * width
    r.s1s[0] = jnp.sum(r.sg8[:, pl.ds(late, r.s1s.shape[2])], axis=0, keepdims=True)
    small(S1, 0).start()
    tick()

    def dqkv(p):
        return r.wx.at[pl.ds((p // 2) * seq_len, seq_len), pl.ds((p % 2) * 384, 384)]

    do = r.wx.at[pl.ds(seq_len, seq_len), pl.ds(384, half)]
    xt = r.wi.at[:, pl.ds(0, seq_len)]

    def upstream(slot):
        do[seq_rows(slot), :] = nt(r.ga[slot], r.wo[own_heads, :]).astype(BF)

    xt[...] = r.xall[...].reshape(seq_len, width).T
    upstream(me)
    upstream(at_x)
    tick()
    ex(GA).wait_recv()
    upstream(at_c)
    upstream(at_xc)

    for p in range(pairs):
        at = r.att[:, :, :, pair_lanes(p)].reshape(seq_len, 128)
        prod = (at.astype(F32) * do[:, pl.ds(p * 128, 128)].astype(F32)).T
        for h in range(2):
            r.delta[2 * p + h] = jnp.sum(prod[h * HD : (h + 1) * HD], axis=0, keepdims=True)
    tick()

    for p in range(pairs):
        ex(AT + 2 * p + 1).wait_recv()
    att_all = r.att[...].reshape(seq_len, width)
    ga_cols = r.ga[:, :, :, own_heads].reshape(seq_len, half)
    r.dc[3] = tn(att_all, ga_cols).astype(BF).reshape(2, 2, 2, rows_f, cols_f)
    begin(OUTPUT)
    tick()

    def backward(p, t):
        lanes = pl.ds(p * 128, 128)
        rows = pl.ds(t * tok, tok)
        qp = r.q[rows, lanes]
        dp = do[rows, lanes]
        kp = r.k[:, lanes]
        vp = r.vp[p, :, pl.ds(0, 128)]
        zero = jnp.zeros_like(qp)
        dqs = []
        for h in range(2):
            qm = jnp.where(lane_head == h, qp, zero)
            dm = jnp.where(lane_head == h, dp, zero)
            pt = jnp.exp2(nt(kp, qm) * SCALE2 - r.lse[2 * p + h, :, rows])
            ds = (pt * (nt(vp, dm) - r.delta[2 * p + h, :, rows])).astype(BF)
            dv, dk = nn(pt.astype(BF), dm), nn(ds, qm)
            if t == 0 and h == 0:
                r.dva[...] = dv
                r.dka[...] = dk
            else:
                r.dva[...] += dv
                r.dka[...] += dk
            dqs.append(nn(r.kt[pl.ds(p * 128 + h * HD, HD), :], ds))
        both = (jnp.concatenate(dqs, axis=0) * 0.125).astype(BF)
        dqkv(p)[rows, pl.ds(0, 128)] = both.T

    def partial(p, slot):
        return nt(dqkv(p)[seq_rows(slot), :], r.wcat[:, pl.ds(p * 384, 384)])

    def weight_part(p):
        r.dc[p] = nn(xt[...], dqkv(p)[...]).astype(BF).reshape(2, 2, 2, rows_f, cols_f)
        r.sg8[:, pair_lanes(p, QB)] = fold8(dqkv(p)[:, pl.ds(0, 128)].astype(F32))
        r.sg8[:, pair_lanes(p, VB)] = fold8(dqkv(p)[:, pl.ds(256, 128)].astype(F32))
        begin(PAIR + p)

    def other_part(p, i):
        rows = pl.ds(i * tok, tok)
        part = partial(p, (at_c, at_xc)[i])
        if p == 0:
            r.xh[rows, :] = part
        elif p < pairs - 1:
            r.xh[rows, :] += part
        else:
            r.gffn[rows, :] = (r.xh[rows, :] + part).astype(BF)

    def own_part(p, i):
        r.acc[pl.ds(i * tok, tok), :] += partial(p, mine[i])

    for p in range(pairs):
        for t in range(slots):
            backward(p, t)
            if t == slots - 1:
                dqkv(p)[:, pl.ds(128, 128)] = (r.dka[...] * 0.125).astype(BF)
                dqkv(p)[:, pl.ds(256, 128)] = r.dva[...].astype(BF)
            tick()
        if p < pairs - 1:
            weight_part(p)
            tick()
            for i in range(2):
                other_part(p, i)
                own_part(p, i)
            tick()
        else:
            for i in (1, 0):
                other_part(p, i)
                ex(GP + i).start()
            weight_part(p)
            r.s2s[0] = jnp.sum(r.sg8[:, pl.ds(0, late)], axis=0, keepdims=True)
            small(S2, 0).start()
            tick()
            for i in (1, 0):
                own_part(p, i)
            tick()

    for i in (1, 0):
        rows = pl.ds(i * tok, tok)
        ex(GP + i).wait_recv()
        total = r.acc[rows, :] + r.grecv[rows, :].astype(F32) + (1.0 - kept) * r.gown[i].astype(F32)
        r.inn[rows, :] = total.astype(BF)
        if i == 1:
            ex(GI).start()
    gin_local = fetch(r.inn.at[pl.ds(0, tok)], r.gin.at[x])
    gin_local.start()
    tick()
    tick()
    r.sout[:, pl.ds(0, late)] = r.s2s[5]
    r.sout[:, pl.ds(late, r.s1s.shape[2])] = r.s1s[5]

    ex(HO).wait_recv()
    ex(GI).wait_recv()
    hout_local.wait()
    gin_local.wait()
    for i in range(AT + 2 * pairs):
        ex(i).wait_send()
    for k in range(5):
        small(S1, k).wait_send()
        small(S2, k).wait_send()
    for i, flow in enumerate(FLOWS):
        for k in range(4):
            hop(i, k).wait_send()
        if flow[5][3] != X:
            spread(i, 4).wait_send()
        spread(i, 5).wait_send()
        if flow[1] < 8:
            core_sum(i).wait_send()


def finish_kernel(n_seq, names, *refs):
    r = SimpleNamespace(**dict(zip(names, refs)))
    pairs = ((r.hout_in, r.hout), (r.gin_in, r.gin))
    arrive = [pltpu.make_async_copy(pair[0], r.through.at[i], r.sem.at[i]) for i, pair in enumerate(pairs)]
    leave = [pltpu.make_async_copy(r.through.at[i], pair[1], r.sem.at[2 + i]) for i, pair in enumerate(pairs)]
    for copy in arrive:
        copy.start()
    for before, after in zip(arrive, leave):
        before.wait()
        after.start()
    fin = r.fin
    rows_f, cols_f = fin.shape[2:]
    half = cols_f
    for h in range(2):
        for f in range(4):
            r.outer[pl.ds(f * rows_f, rows_f), pl.ds(h * half, half)] = fin[f, h].astype(F32)
            r.inner[:, pl.ds((4 * h + f) * cols_f, cols_f)] = fin[4 + f, h].astype(F32)
        r.output[:, pl.ds(h * half, half)] = fin[11, h].astype(F32)
        for p in range(half // 128):
            for i, ref in enumerate((r.query, r.key, r.value)):
                part = fin[8 + p, h, :, pl.ds(i * 128, 128)].astype(F32)
                ref[:, pl.ds(h * half + p * 128, 128)] = part
    seq = lax.axis_index("seq")
    width = 2 * half
    share = width // n_seq
    for i in range(8):
        r.rows[pl.ds(i, 1), :] = r.sout[:, pl.ds(i * width, width)]
    turned = pltpu.roll(r.rows[...], lax.rem(width - seq * share, width), 1)
    for i, ref in enumerate((r.qb, r.vb, r.ob, r.ag, r.sh, r.xb, r.fg, r.fs)):
        ref[...] = turned[i, :share]
    ib = r.ib.shape[0]
    full = r.sout.shape[1] - 8 * width
    r.wide[...] = jnp.broadcast_to(r.sout[:, pl.ds(8 * width, full)], (8, full))
    r.ib[...] = pltpu.roll(r.wide[...], lax.rem(full - seq * ib, full), 1)[0, :ib]
    for copy in leave:
        copy.wait()


def call(kernel, ins, outs, scratch, params, name, land=()):
    names = [*ins, *outs, *scratch]

    def body(*refs):
        extra = refs[len(names) :]
        shelf = iter(extra)
        nested = [[next(shelf) for _ in group] for group in land]
        kernel([*names, *(("land",) if land else ())], *refs[: len(names)], *((nested,) if land else ()))

    res = pl.pallas_call(
        body,
        out_shape=[jax.ShapeDtypeStruct(e[0], e[1]) for e in outs.values()],
        in_specs=[e[1] for e in ins.values()],
        out_specs=[e[2] for e in outs.values()],
        scratch_shapes=[*scratch.values(), *(e for group in land for e in group)],
        compiler_params=params,
        name=name,
    )(*[e[0] for e in ins.values()])
    return SimpleNamespace(**dict(zip(outs, res)))


def build(mesh):
    n_seq = mesh.shape["seq"]
    groups = n_seq // 8

    def local(
        hidden_in,
        depth_group,
        query_weight,
        query_bias,
        key_weight,
        value_weight,
        value_bias,
        output_weight,
        output_bias,
        attn_gain,
        attn_shift,
        inner_weight,
        inner_bias,
        outer_weight,
        outer_bias,
        final_gain,
        final_shift,
        grad_out,
    ):
        seqs, tok, width = hidden_in.shape
        ff = inner_weight.shape[1]
        seq_len = 4 * tok
        half = width // 2
        heads = half // HD
        pairs = half // 128
        rows_f, cols_f = width // 8, half
        small, late = 8 * width + ff, 2 * width
        hbm = pl.BlockSpec(memory_space=pl.ANY)
        vmem = pl.BlockSpec(memory_space=pltpu.VMEM)
        v = pltpu.VMEM
        dma = pltpu.SemaphoreType.DMA
        o = call(
            lambda *refs: layer_kernel(groups, *refs),
            dict(
                qb=(query_bias, vmem),
                vb=(value_bias, vmem),
                ob=(output_bias, vmem),
                ag=(attn_gain, vmem),
                sh=(attn_shift, vmem),
                xb=(outer_bias, vmem),
                fg=(final_gain, vmem),
                fs=(final_shift, vmem),
                ib=(inner_bias, vmem),
                dg=(depth_group, pl.BlockSpec(memory_space=pltpu.SMEM)),
                hid=(hidden_in, hbm),
                go=(grad_out, hbm),
                wq=(query_weight, hbm),
                wk=(key_weight, hbm),
                wv=(value_weight, hbm),
                wo_in=(output_weight, hbm),
                wi_in=(inner_weight, hbm),
                wx_in=(outer_weight, hbm),
            ),
            dict(
                hout=((seqs, tok, width), BF, hbm),
                gin=((seqs, tok, width), BF, hbm),
                fin=((PIECES, 2, rows_f, cols_f), BF, vmem),
                sout=((1, small), F32, vmem),
            ),
            dict(
                vec=v((1, small), F32),
                xall=v((2, 2, tok, width), BF),
                gown=v((2, tok, width), BF),
                wcat=v((width, 3 * half), BF),
                wo=v((width, width), BF),
                wi=v((width, ff), BF),
                wx=v((ff, width), BF),
                q=v((seq_len, half), BF),
                k=v((seq_len, half), BF),
                kt=v((half, seq_len), BF),
                vp=v((pairs, seq_len, 256), BF),
                lse=v((heads, 1, seq_len), F32),
                delta=v((heads, 1, seq_len), F32),
                att=v((2, 2, tok, width), BF),
                ga=v((2, 2, tok, width), BF),
                act=v((2 * tok, ff), BF),
                gp=v((2 * tok, ff), BF),
                inn=v((2 * tok, width), BF),
                gffn=v((2 * tok, width), BF),
                xh=v((2 * tok, width), F32),
                acc=v((2 * tok, width), F32),
                rs=v((2 * tok, 1), F32),
                hbuf=v((2, tok, width), BF),
                grecv=v((2 * tok, width), BF),
                dka=v((seq_len, 128), F32),
                dva=v((seq_len, 128), F32),
                d2=v((2, 8, 2, 2, 2, rows_f, cols_f), BF),
                rc=v((8, 2, 2, 2, rows_f, cols_f), BF),
                dc=v((4, 2, 2, 2, rows_f, cols_f), BF),
                sg8=v((8, small), F32),
                s1s=v((6, 1, small - late), F32),
                s1r=v((5, 1, small - late), F32),
                s2s=v((6, 1, late), F32),
                s2r=v((5, 1, late), F32),
                lsem=dma((7 + 3 * pairs,)),
                ex_s=dma((AT + 2 * pairs,)),
                ex_r=dma((AT + 2 * pairs,)),
                rs_s=dma((len(FLOWS), 7)),
                rs_r=dma((len(FLOWS), 7)),
                sm_s=dma((10,)),
                sm_r=dma((10,)),
            ),
            pltpu.CompilerParams(collective_id=0, has_side_effects=True, vmem_limit_bytes=64 * 1024 * 1024),
            "layer",
            [[v(recv_shape(flow, k, rows_f), BF) for k in range(4)] for flow in FLOWS],
        )

        rows = [[g * groups + i for i in range(groups)] for g in range(8)]
        sout = o.sout
        if groups > 1:
            sout = lax.psum(sout, "seq", axis_index_groups=rows)
        mat, one = ((rows_f, width), F32, vmem), ((width // n_seq,), F32, vmem)
        f = call(
            lambda *refs: finish_kernel(n_seq, *refs),
            dict(hout_in=(o.hout, hbm), gin_in=(o.gin, hbm), fin=(o.fin, vmem), sout=(sout, vmem)),
            dict(
                hout=(o.hout.shape, BF, hbm),
                gin=(o.gin.shape, BF, hbm),
                query=mat,
                key=mat,
                value=mat,
                output=mat,
                inner=((rows_f, ff), F32, vmem),
                outer=((ff // 8, width), F32, vmem),
                qb=one,
                vb=one,
                ob=one,
                ag=one,
                sh=one,
                xb=one,
                fg=one,
                fs=one,
                ib=((ff // n_seq,), F32, vmem),
            ),
            dict(
                sem=dma((4,)),
                through=v((2, seqs, tok, width), BF),
                rows=v((8, width), F32),
                wide=v((8, ff), F32),
            ),
            pltpu.CompilerParams(vmem_limit_bytes=64 * 1024 * 1024),
            "finish",
        )

        def across(values):
            if groups == 1:
                return values
            return lax.psum_scatter(values, "seq", scatter_dimension=0, axis_index_groups=rows, tiled=True)

        return (
            f.hout,
            f.gin,
            across(f.query),
            f.qb,
            across(f.key),
            across(f.value),
            f.vb,
            across(f.output),
            f.ob,
            f.ag,
            f.sh,
            across(f.inner),
            f.ib,
            across(f.outer),
            f.xb,
            f.fg,
            f.fs,
        )

    return local


def solution(mesh):
    rows = P("seq", "blk", None)
    placed = (rows, P("seq"), *([P()] * 15), rows)
    mat, one = P("seq", None), P("seq")
    return jax.shard_map(
        build(mesh),
        mesh=mesh,
        in_specs=placed,
        out_specs=(rows, rows, mat, one, mat, mat, one, mat, one, one, one, mat, one, mat, one, one, one),
        check_vma=False,
    )
```

```python
import itertools
import math
from types import SimpleNamespace

import jax
import jax.numpy as jnp
from jax import lax
from jax.experimental import pallas as pl
from jax.experimental.pallas import tpu as pltpu
from jax.sharding import PartitionSpec as P

HD = 64
MESH = pl.DeviceIdType.MESH
BF = jnp.bfloat16
F32 = jnp.float32
LOG2E = math.log2(math.e)
SCALE2 = 0.125 * LOG2E
EPS = 1e-05

X, Y, Z0, Z1, C = range(5)
BITS = (Z1, Z0, Y)

PIECES = 12
OUTER, INNER, OUTPUT, PAIR = range(4)
S1, S2 = -1, -2
SMALL_ORDER = {S1: (C, Y, Z0, Z1, X), S2: (X, C, Y, Z0, Z1)}
FLOWS = (
    (OUTER, 0, 1, 0, 384, (Y, Z1, Z0, X)),
    (OUTER, 1, 1, 0, 384, (Z0, Y, X, Z1)),
    (OUTER, 2, 1, 0, 384, (Y, X, Z1, Z0)),
    (OUTER, 3, 1, 0, 384, (Z1, Y, Z0, X)),
    (INNER, 4, 1, 0, 384, (X, Y, Z0, Z1)),
    (INNER, 5, 1, 0, 384, (Z0, Y, X, Z1)),
    (INNER, 6, 1, 0, 384, (Y, Z0, X, Z1)),
    (INNER, 7, 1, 0, 384, (X, Y, Z1, Z0)),
    (OUTPUT, 11, 1, 0, 256, (X, Y, Z0, Z1)),
    (OUTPUT, 11, 1, 256, 128, (Z1, Y, Z0, X)),
    (PAIR, 8, 1, 0, 256, (X, Y, Z1, Z0)),
    (PAIR, 8, 1, 256, 128, (Y, Z0, X, Z1)),
    (PAIR + 1, 9, 1, 0, 256, (X, Z1, Y, Z0)),
    (PAIR + 1, 9, 1, 256, 128, (Y, Z1, Z0, X)),
    (PAIR + 2, 10, 1, 0, 128, (Y, Z0, Z1, X)),
    (PAIR + 2, 10, 1, 128, 128, (Z0, Y, Z1, X)),
    (PAIR + 2, 10, 1, 256, 128, (Y, Z0, Z1, X)),
)
PLAN = (
    (),
    ((0, -1), (1, -1)),
    ((2, -1), (3, -1)),
    (),
    ((4, -1), (5, -1)),
    ((6, -1),),
    ((7, -1),),
    (),
    ((0, 0),),
    ((S1, 0),),
    (),
    ((1, 0), (4, 0)),
    ((2, 0),),
    ((3, 0),),
    (),
    ((7, 0),),
    ((6, 0), (S1, 1)),
    ((0, 1),),
    ((8, 0), (1, 1), (5, 0)),
    ((2, 1), (9, 0)),
    ((4, 1), (6, 1)),
    ((S1, 2),),
    ((3, 1), (10, 0)),
    ((1, 2), (2, 2), (11, 0), (0, 2), (S1, 3), (6, 2)),
    ((4, 2), (7, 1)),
    ((1, 3), (3, 2), (8, 1)),
    ((12, 0), (6, 3), (2, 3), (0, 3)),
    ((S1, 4), (4, 3), (5, 1), (11, 1), (1, 4), (9, 1)),
    ((3, 3), (8, 2)),
    ((6, 4), (7, 2), (13, 0), (2, 4), (S2, 0)),
    (
        (0, 5), (1, 5), (3, 5), (4, 4), (6, 5), (2, 5), (S2, 1), (10, 1), (5, 2), (4, 5), (11, 2), (12, 1),
        (15, 0), (14, 0), (8, 3), (9, 2), (16, 0), (7, 3), (S2, 2), (13, 1), (12, 2), (14, 1), (15, 1), (10, 2),
        (5, 3), (16, 1), (S2, 3), (11, 3), (13, 2), (14, 2), (8, 4), (9, 3), (12, 3), (15, 2), (7, 4), (8, 5),
        (9, 5), (10, 3), (16, 2), (5, 4), (S2, 4), (11, 4), (7, 5), (13, 3), (14, 3), (5, 5), (12, 4), (11, 5),
        (15, 3), (13, 5), (14, 5), (10, 4), (12, 5), (16, 3), (15, 5), (10, 5), (16, 5),
    ),
)

QB, VB, OB, AG, AS, XB, FG, FS, IB = range(9)
HX, HC, HF, GO, GA, HO, GP, GI, AT = 0, 2, 3, 5, 6, 7, 8, 10, 11
EXCHANGES = 13


def nn(left, right):
    return jnp.dot(left, right, preferred_element_type=F32)


def nt(left, right):
    return lax.dot_general(left, right, (((1,), (1,)), ((), ())), preferred_element_type=F32)


def tn(left, right):
    return lax.dot_general(left, right, (((0,), (0,)), ((), ())), preferred_element_type=F32)


def fold8(values):
    rows, width = values.shape
    return jnp.sum(values.reshape(rows // 8, 8, width), axis=0)


def halves_rows(order, k):
    return X in order[: k + 1] and order.index(X) < 3


def recv_shape(flow, k, rows):
    part, f, nf, start, cols, order = flow
    free = [2 for ax in BITS if ax not in order[: k + 1]]
    return (nf, *free, rows // 2 if halves_rows(order, k) else rows, cols)


def layer_kernel(groups, names, *refs):
    r = SimpleNamespace(**dict(zip(names, refs)))
    seq = lax.axis_index("seq")
    blk = lax.axis_index("blk")
    x = lax.div(blk, 2)
    c = lax.rem(blk, 2)
    hi = lax.div(seq, groups)
    own = {X: x, Y: lax.rem(hi, 2), Z0: lax.rem(lax.div(hi, 2), 2), Z1: lax.div(hi, 4)}
    peers = {
        C: (seq, blk + 1 - 2 * c),
        X: (seq, blk + 2 - 4 * x),
        Y: (seq + (1 - 2 * own[Y]) * groups, blk),
        Z0: (seq + (1 - 2 * own[Z0]) * 2 * groups, blk),
        Z1: (seq + (1 - 2 * own[Z1]) * 4 * groups, blk),
    }
    tok, width = r.xall.shape[2:]
    slots = 4
    seq_len = slots * tok
    half = width // 2
    ff = r.wi.shape[1]
    pairs = half // 128
    me, at_x, at_c, at_xc = (x, c), (1 - x, c), (x, 1 - c), (1 - x, 1 - c)
    mine = (me, at_x)
    own_heads = pl.ds(pl.multiple_of(c * half, 128), half)
    other_heads = pl.ds(pl.multiple_of((1 - c) * half, 128), half)

    def seq_rows(slot, start=0, rows=tok):
        return pl.ds(pl.multiple_of((2 * slot[0] + slot[1]) * tok + start, rows), rows)

    def vec(i, start=0, size=width):
        return r.vec[:, pl.ds(width * i + start, size)]

    def pair_lanes(p, base=0):
        return pl.ds(pl.multiple_of(base * width + c * half + p * 128, 128), 128)

    def remote(src, dst, send, recv, peer):
        return pltpu.make_async_remote_copy(
            src_ref=src, dst_ref=dst, send_sem=send, recv_sem=recv, device_id=peers[peer], device_id_type=MESH
        )

    barrier = pltpu.get_barrier_semaphore()
    for peer in peers.values():
        pl.semaphore_signal(barrier, inc=1, device_id=peer, device_id_type=MESH)

    lcount = itertools.count()

    def fetch(src, dst):
        return pltpu.make_async_copy(src, dst, r.lsem.at[next(lcount)])

    first = [fetch(r.hid.at[x], r.xall.at[me])]
    for p in range(pairs):
        for i, w in enumerate((r.wq, r.wk, r.wv)):
            first.append(fetch(w.at[:, pair_lanes(p)], r.wcat.at[:, pl.ds((3 * p + i) * 128, 128)]))
    second = [
        fetch(r.go.at[x], r.gown.at[0]),
        fetch(r.wo_in, r.wo),
        fetch(r.wi_in, r.wi),
        fetch(r.wx_in, r.wx),
    ]
    for copy in first + second:
        copy.start()
    params = (r.qb, r.vb, r.ob, r.ag, r.sh, r.xb, r.fg, r.fs, r.ib)
    for i, ref in enumerate(params):
        r.vec[:, pl.ds(width * i, ref.shape[0])] = ref[...].astype(F32).reshape(1, ref.shape[0])
    r.sg8[...] = jnp.zeros_like(r.sg8)
    kept = jnp.where(r.dg[x] == 2, 0.0, 1.0).astype(F32)
    pl.semaphore_wait(barrier, len(peers))

    hrows = tok // 2

    def ex(i):
        if i == HC:
            src, dst, peer = r.hid.at[x], r.xall.at[me], C
        elif i == GO:
            src, dst, peer = r.go.at[1 - x], r.gown.at[1], X
        elif i == GA:
            src = dst = r.ga.at[:, c]
            peer = C
        elif i == HO:
            src, dst, peer = r.ga.at[at_x], r.hout.at[x], X
        elif i == GI:
            src, dst, peer = r.inn.at[pl.ds(tok, tok)], r.gin.at[x], X
        else:
            src, dst, peer = r.gffn.at[pl.ds((i - GP) * tok, tok)], r.xall.at[(at_c, at_xc)[i - GP]], C
        return remote(src, dst, r.ex_s.at[i], r.ex_r.at[i], peer)

    def ex_in(i):
        hs = pl.ds(i * hrows, hrows)
        return remote(r.hid.at[1 - x, hs], r.xall.at[x, c, hs], r.ex_s.at[HX + i], r.ex_r.at[HX + i], X)

    def ex_on(i):
        ref = r.xall.at[1 - x, c, pl.ds(i * hrows, hrows)]
        return remote(ref, ref, r.ex_s.at[HF + i], r.ex_r.at[HF + i], C)

    def ex_att(i):
        ref = r.att.at[:, 1 - c + i * (2 * c - 1), :, own_heads]
        return remote(ref, ref, r.ex_s.at[AT + i], r.ex_r.at[AT + i], C)

    ex_in(0).start()
    ex_in(1).start()
    ex(HC).start()
    ex(GO).start()

    lane_head = lax.broadcasted_iota(jnp.int32, (tok, 128), 1) // HD
    ones = jnp.ones((seq_len, 128), BF)
    for p in range(pairs):
        r.vp[p, :, pl.ds(128, 128)] = ones

    def project(slot, start, rows):
        out = nn(r.xall[(*slot, pl.ds(start, rows), slice(None))], r.wcat[...])
        at = seq_rows(slot, start, rows)
        for p in range(pairs):
            lanes = pl.ds(p * 128, 128)
            base = 3 * p * 128
            r.q[at, lanes] = (out[:, base : base + 128] + r.vec[:, pair_lanes(p, QB)]).astype(BF)
            key = out[:, base + 128 : base + 256].astype(BF)
            r.k[at, lanes] = key
            r.kt[lanes, at] = key.T
            r.vp[p, at, pl.ds(0, 128)] = (out[:, base + 256 : base + 384] + r.vec[:, pair_lanes(p, VB)]).astype(BF)

    for copy in first:
        copy.wait()
    ex(HC).wait_recv()

    @pl.loop(0, 2)
    def _(i):
        project((x, i), 0, tok)

    @pl.loop(0, 2)
    def _(i):
        ex_in(i).wait_recv()
        ex_on(i).start()
        project(at_x, i * hrows, hrows)

    @pl.loop(0, 2)
    def _(i):
        ex_on(i).wait_recv()
        project(at_xc, i * hrows, hrows)

    def forward(p, slot):
        lanes = pl.ds(p * 128, 128)
        rows = seq_rows(slot)
        qp = r.q[rows, lanes]
        outs, sums = [], []
        for h in range(2):
            qm = jnp.where(lane_head == h, qp, jnp.zeros_like(qp))
            s = nn(qm, r.kt[lanes, :])
            top = jnp.max(s, axis=1, keepdims=True)
            pt = jnp.exp2((s - top) * SCALE2).astype(BF)
            o = nn(pt, r.vp[p])
            sums.append(top * SCALE2 + jnp.log2(o[:, 128:]))
            outs.append(o[:, :128] / o[:, 128:])
        r.att[(*slot, slice(None), pair_lanes(p))] = jnp.where(lane_head == 0, outs[0], outs[1]).astype(BF)
        both = jnp.where(lane_head == 0, sums[0], sums[1]).T
        for h in range(2):
            r.lse[2 * p + h, :, rows] = both[h * HD : h * HD + 1]

    @pl.loop(0, 2)
    def _(i):
        core = 1 - c + i * (2 * c - 1)
        for p in range(pairs):
            forward(p, (x, core))
            forward(p, (1 - x, core))
        ex_att(i).start()

    for copy in second:
        copy.wait()
    chunk = tok // 2

    def own_rows(i):
        inner = pl.ds((i % 2) * chunk, chunk)
        return mine[i // 2], i // 2, inner, pl.ds(i * chunk, chunk)

    def fold_in(i, values):
        at = pl.ds(width * i, values.shape[1])
        r.sg8[:, at] += fold8(values)

    def heads_out(i, heads):
        return nn(r.att[(*mine[i], slice(None), heads)], r.wo[heads, :])

    for i in range(2):
        r.acc[pl.ds(i * tok, tok), :] = heads_out(i, own_heads)
    ex_att(0).wait_recv()
    for i in range(2):
        r.acc[pl.ds(i * tok, tok), :] += heads_out(i, other_heads)

    for i in range(4):
        slot, which, inner, rows = own_rows(i)
        v = r.acc[rows, :] + vec(OB) + r.xall[(*slot, inner, slice(None))].astype(F32)
        cen = v - jnp.mean(v, axis=-1, keepdims=True)
        rstd = lax.rsqrt(jnp.mean(cen * cen, axis=-1, keepdims=True) + EPS)
        xh = cen * rstd
        normed = xh * vec(AG) + vec(AS)
        r.xh[rows, :] = xh
        r.dva[rows, pl.ds(0, 1)] = rstd
        r.acc[rows, :] = normed
        r.inn[rows, :] = normed.astype(BF)

    tile = 512

    def activate(j):
        start = pl.multiple_of(j * tile, tile)
        at = pl.ds(start, tile)
        pre = nn(r.inn[...], r.wi[:, at]) + r.vec[:, pl.ds(pl.multiple_of(width * IB + start, 128), tile)]
        phi = 0.5 + 0.5 * lax.erf(pre * math.sqrt(0.5))
        dens = jnp.exp2(pre * pre * (-0.5 * LOG2E)) * (1.0 / math.sqrt(2.0 * math.pi))
        r.act[:, at] = (pre * phi).astype(BF)
        r.gp[:, at] = (phi + pre * dens).astype(BF)

    @pl.loop(0, 2)
    def _(i):
        for j in range(ff // tile // 2):
            activate(i * (ff // tile // 2) + j)

    for j in range(width // 256):
        at = pl.ds(j * 256, 256)
        r.acc[:, at] += nn(r.act[...], r.wx[:, at])

    ex(GO).wait_recv()
    for i in range(4):
        slot, which, inner, rows = own_rows(i)
        xf = r.xall[(*slot, inner, slice(None))].astype(F32)
        v = r.acc[rows, :] + vec(XB)
        cen = v - jnp.mean(v, axis=-1, keepdims=True)
        rstd = lax.rsqrt(jnp.mean(cen * cen, axis=-1, keepdims=True) + EPS)
        xh = cen * rstd
        out = kept * (xh * vec(FG) + vec(FS)) + (1.0 - kept) * xf
        r.ga[(*slot, inner, slice(None))] = out.astype(BF)
        g = kept * r.gown[which, inner, :].astype(F32)
        fold_in(FG, g * xh)
        fold_in(FS, g)
        gx = g * vec(FG)
        m1 = jnp.mean(gx, axis=-1, keepdims=True)
        m2 = jnp.mean(gx * xh, axis=-1, keepdims=True)
        gs = rstd * (gx - m1 - xh * m2)
        low = gs.astype(BF)
        r.acc[rows, :] = gs
        r.gffn[rows, :] = low
        fold_in(XB, low.astype(F32))

    ex(HO).start()
    hout_local = fetch(r.ga.at[me], r.hout.at[x])
    hout_local.start()

    rows_f, cols_f = r.dc.shape[-2:]
    x_rows = pl.ds(pl.multiple_of(x * (rows_f // 2), 16), rows_f // 2)

    def pieces(flow):
        f, nf = flow[1:3]
        return r.d2.at[c, pl.ds(f, nf)] if f < 8 else r.dc.at[pl.ds(f - 8, nf)]

    def view(flow, k, send):
        part, f, nf, start, cols, order = flow
        idx = [slice(None)] * 3
        row = pl.ds(0, rows_f)
        for j, ax in enumerate(order[: k + 1]):
            want = 1 - own[ax] if (j == k and send) else own[ax]
            if ax != X:
                idx[BITS.index(ax)] = want
            elif j < 3:
                row = pl.ds(pl.multiple_of(want * (rows_f // 2), 16), rows_f // 2)
        return (slice(None), *idx, row, pl.ds(start, cols))

    def hop(i, k):
        flow = FLOWS[i]
        src = pieces(flow).at[view(flow, k, True)]
        return remote(src, r.land[i][k], r.rs_s.at[i, k], r.rs_r.at[i, k], flow[5][k])

    def add_in(i, k):
        flow = FLOWS[i]
        nf, order = flow[2], flow[5]
        idx = list(view(flow, k, False))
        ref = pieces(flow)
        free = [ax for ax in BITS if ax not in order[: k + 1]]
        for n in range(nf):
            idx[0] = n
            for combo in itertools.product((0, 1), repeat=len(free)):
                for ax, bit in zip(free, combo):
                    idx[1 + BITS.index(ax)] = bit
                at = tuple(idx)
                ref[at] = ref[at] + r.land[i][k][(n, *combo, slice(None), slice(None))]

    def spread(i, k):
        part, f, nf, start, cols, order = FLOWS[i]
        rows = x_rows if k == 4 else pl.ds(0, rows_f)
        ref = r.fin.at[pl.ds(f, nf), c, rows, pl.ds(start, cols)]
        return remote(ref, ref, r.rs_s.at[i, k], r.rs_r.at[i, k], X if k == 4 else C)

    def core_sum(i):
        part, f, nf, start, cols, order = FLOWS[i]
        at = pl.ds(f, nf)
        return remote(r.d2.at[1 - c, at], r.rc.at[at], r.rs_s.at[i, 6], r.rs_r.at[i, 6], C)

    def small(which, k):
        send, recv = (r.s1s, r.s1r) if which == S1 else (r.s2s, r.s2r)
        at = k if which == S1 else 5 + k
        return remote(send.at[k], recv.at[k], r.sm_s.at[at], r.sm_r.at[at], SMALL_ORDER[which][k])

    def step(i, k):
        if i < 0:
            send, recv = (r.s1s, r.s1r) if i == S1 else (r.s2s, r.s2r)
            small(i, k).wait_recv()
            send[k + 1] = send[k] + recv[k]
            if k < 4:
                small(i, k + 1).start()
            return
        flow = FLOWS[i]
        part, f, nf, start, cols, order = flow
        if k == -1:
            core_sum(i).wait_recv()
            ref = pieces(flow)
            for combo in itertools.product(range(nf), (0, 1), (0, 1), (0, 1)):
                ref[combo] = ref[combo] + r.rc[(f + combo[0], *combo[1:])]
            hop(i, 0).start()
        elif k < 3:
            hop(i, k).wait_recv()
            add_in(i, k)
            hop(i, k + 1).start()
        elif k == 3:
            hop(i, 3).wait_recv()
            rows = pl.ds(0, rows_f) if order[3] == X else x_rows
            at = pl.ds(start, cols)
            for n in range(nf):
                mine_part = pieces(flow)[(n, own[Z1], own[Z0], own[Y], rows, at)]
                r.fin[f + n, c, rows, at] = mine_part + r.land[i][3][n]
            spread(i, 5 if order[3] == X else 4).start()
        elif k == 4:
            spread(i, 4).wait_recv()
            spread(i, 5).start()
        else:
            spread(i, 5).wait_recv()

    plan = iter(PLAN)

    def tick():
        for i, k in next(plan):
            step(i, k)

    def begin(part):
        for i, flow in enumerate(FLOWS):
            if flow[0] == part:
                (core_sum(i) if flow[1] < 8 else hop(i, 0)).start()

    outer_rows = ff // 8

    @pl.loop(0, 2)
    def _(i):
        for j in range(4):
            at = pl.ds(pl.multiple_of((4 * i + j) * outer_rows, 128), outer_rows)
            val = tn(r.act[:, at], r.gffn[...]).astype(BF)
            for f in range(4):
                for h in range(2):
                    part = val[f * rows_f : (f + 1) * rows_f, h * cols_f : (h + 1) * cols_f]
                    r.d2[h, f, i, j // 2, j % 2] = part

    begin(OUTER)
    tick()

    tile = ff // 4

    @pl.loop(0, 2)
    def _(i):
        for j in range(2):
            start = pl.multiple_of((2 * i + j) * tile, tile)
            at = pl.ds(start, tile)
            gpre = (nt(r.gffn[...], r.wx[at, :]) * r.gp[:, at].astype(F32)).astype(BF)
            r.gp[:, at] = gpre
            r.sg8[:, pl.ds(pl.multiple_of(width * IB + start, 128), tile)] = fold8(gpre.astype(F32))

    tick()

    @pl.loop(0, 2)
    def _(i):
        for h in range(2):
            at = pl.ds(pl.multiple_of((2 * h + i) * tile, tile), tile)
            val = tn(r.inn[...], r.gp[:, at]).astype(BF)
            for m in range(2):
                part = val[:, m * cols_f : (m + 1) * cols_f]
                r.d2[h, 4 + 2 * i + m] = part.reshape(2, 2, 2, rows_f, cols_f)
        for n in range(2):

            @pl.when(i == n)
            def _():
                for g, flow in enumerate(FLOWS):
                    if flow[0] == INNER and (flow[1] + flow[2] - 1) // 2 == 2 + n:
                        core_sum(g).start()
                tick()

    for j in range(3):
        at = pl.ds(j * 256, 256)
        r.acc[:, at] += nt(r.gp[...], r.wi[at, :])
        tick()

    ex(HO).wait_send()
    hout_local.wait()
    for i in range(4):
        slot, which, inner, rows = own_rows(i)
        g = r.acc[rows, :]
        xh = r.xh[rows, :]
        fold_in(AG, g * xh)
        fold_in(AS, g)
        gx = g * vec(AG)
        m1 = jnp.mean(gx, axis=-1, keepdims=True)
        m2 = jnp.mean(gx * xh, axis=-1, keepdims=True)
        gs = r.dva[rows, pl.ds(0, 1)] * (gx - m1 - xh * m2)
        low = gs.astype(BF)
        r.acc[rows, :] = gs
        r.ga[(*slot, inner, slice(None))] = low
        fold_in(OB, low.astype(F32))

    xt = r.wi.at[:, pl.ds(0, seq_len)]
    xt[...] = r.xall[...].reshape(seq_len, width).T
    for i in range(2):
        ex_on(i).wait_send()
    ex(GA).start()
    late = 2 * width
    r.s1s[0] = jnp.sum(r.sg8[:, pl.ds(late, r.s1s.shape[2])], axis=0, keepdims=True)
    small(S1, 0).start()
    tick()

    def dqkv(p):
        rows = pl.ds(pl.multiple_of(lax.div(p, 2) * seq_len, 1024), seq_len)
        return r.wx.at[rows, pl.ds(pl.multiple_of(lax.rem(p, 2) * 384, 128), 384)]

    do = r.wx.at[pl.ds(seq_len, seq_len), pl.ds(384, half)]

    def upstream(slot):
        do[seq_rows(slot), :] = nt(r.ga[slot], r.wo[own_heads, :]).astype(BF)

    upstream(me)
    upstream(at_x)
    tick()
    ex(GA).wait_recv()
    upstream(at_c)
    upstream(at_xc)

    for p in range(pairs):
        at = r.att[:, :, :, pair_lanes(p)].reshape(seq_len, 128)
        prod = (at.astype(F32) * do[:, pl.ds(p * 128, 128)].astype(F32)).T
        for h in range(2):
            r.delta[2 * p + h] = jnp.sum(prod[h * HD : (h + 1) * HD], axis=0, keepdims=True)
    tick()

    ex_att(1).wait_recv()
    att_all = r.att[...].reshape(seq_len, width)
    ga_cols = r.ga[:, :, :, own_heads].reshape(seq_len, half)
    r.dc[3] = tn(att_all, ga_cols).astype(BF).reshape(2, 2, 2, rows_f, cols_f)
    begin(OUTPUT)
    tick()

    r.xh[...] = jnp.zeros_like(r.xh)
    steps = [[next(plan) for _ in range(slots + 2)] for _ in range(pairs)]

    def tick_at(p, j):
        for n in range(pairs):
            if steps[n][j]:

                @pl.when(p == n)
                def _():
                    for i, k in steps[n][j]:
                        step(i, k)

    @pl.loop(0, pairs)
    def _(p):
        lanes = pl.ds(pl.multiple_of(p * 128, 128), 128)
        for t in range(slots):
            rows = pl.ds(t * tok, tok)
            qp = r.q[rows, lanes]
            dp = do[rows, lanes]
            kp = r.k[:, lanes]
            vp = r.vp[p, :, pl.ds(0, 128)]
            zero = jnp.zeros_like(qp)
            dqs = []
            for h in range(2):
                qm = jnp.where(lane_head == h, qp, zero)
                dm = jnp.where(lane_head == h, dp, zero)
                pt = jnp.exp2(nt(kp, qm) * SCALE2 - r.lse[2 * p + h, :, rows])
                ds = (pt * (nt(vp, dm) - r.delta[2 * p + h, :, rows])).astype(BF)
                dv, dk = nn(pt.astype(BF), dm), nn(ds, qm)
                if t == 0 and h == 0:
                    r.dva[...] = dv
                    r.dka[...] = dk
                else:
                    r.dva[...] += dv
                    r.dka[...] += dk
                dqs.append(nn(r.kt[pl.ds(pl.multiple_of(p * 128 + h * HD, HD), HD), :], ds))
            both = (jnp.concatenate(dqs, axis=0) * 0.125).astype(BF)
            dqkv(p)[rows, pl.ds(0, 128)] = both.T
            if t == slots - 1:
                dqkv(p)[:, pl.ds(128, 128)] = (r.dka[...] * 0.125).astype(BF)
                dqkv(p)[:, pl.ds(256, 128)] = r.dva[...].astype(BF)
            tick_at(p, t)

        weights = r.wcat[:, pl.ds(pl.multiple_of(p * 384, 128), 384)]

        def partial(slot):
            return nt(dqkv(p)[seq_rows(slot), :], weights)

        for i in (1, 0):
            r.xh[pl.ds(i * tok, tok), :] += partial((at_c, at_xc)[i])

        @pl.when(p == pairs - 1)
        def _():
            for i in (1, 0):
                rows = pl.ds(i * tok, tok)
                r.gffn[rows, :] = r.xh[rows, :].astype(BF)
                ex(GP + i).start()

        r.dc[p] = nn(xt[...], dqkv(p)[...]).astype(BF).reshape(2, 2, 2, rows_f, cols_f)
        r.sg8[:, pair_lanes(p, QB)] = fold8(dqkv(p)[:, pl.ds(0, 128)].astype(F32))
        r.sg8[:, pair_lanes(p, VB)] = fold8(dqkv(p)[:, pl.ds(256, 128)].astype(F32))
        for n in range(pairs):

            @pl.when(p == n)
            def _():
                begin(PAIR + n)
                if n == pairs - 1:
                    r.s2s[0] = jnp.sum(r.sg8[:, pl.ds(0, late)], axis=0, keepdims=True)
                    small(S2, 0).start()

        tick_at(p, slots)
        for i in (1, 0):
            r.acc[pl.ds(i * tok, tok), :] += partial(mine[i])
        tick_at(p, slots + 1)

    for i in (1, 0):
        rows = pl.ds(i * tok, tok)
        ex(GP + i).wait_recv()
        total = r.acc[rows, :] + r.xall[mine[i]].astype(F32) + (1.0 - kept) * r.gown[i].astype(F32)
        r.inn[rows, :] = total.astype(BF)
        if i == 1:
            ex(GI).start()
    gin_local = fetch(r.inn.at[pl.ds(0, tok)], r.gin.at[x])
    gin_local.start()
    tick()
    tick()
    r.sout[:, pl.ds(0, late)] = r.s2s[5]
    r.sout[:, pl.ds(late, r.s1s.shape[2])] = r.s1s[5]

    ex(HO).wait_recv()
    ex(GI).wait_recv()
    gin_local.wait()
    for i in (HC, GO, GA, GP, GP + 1, GI):
        ex(i).wait_send()
    for i in range(2):
        ex_in(i).wait_send()
        ex_att(i).wait_send()
    for k in range(5):
        small(S1, k).wait_send()
        small(S2, k).wait_send()
    for i, flow in enumerate(FLOWS):
        for k in range(4):
            hop(i, k).wait_send()
        if flow[5][3] != X:
            spread(i, 4).wait_send()
        spread(i, 5).wait_send()
        if flow[1] < 8:
            core_sum(i).wait_send()


def finish_kernel(n_seq, names, *refs):
    r = SimpleNamespace(**dict(zip(names, refs)))
    pairs = ((r.hout_in, r.hout), (r.gin_in, r.gin))
    arrive = [pltpu.make_async_copy(pair[0], r.through.at[i], r.sem.at[i]) for i, pair in enumerate(pairs)]
    leave = [pltpu.make_async_copy(r.through.at[i], pair[1], r.sem.at[2 + i]) for i, pair in enumerate(pairs)]
    for copy in arrive:
        copy.start()
    for before, after in zip(arrive, leave):
        before.wait()
        after.start()
    rows_f, cols_f = r.fin.shape[2:]
    half = cols_f
    outs = (r.outer, r.inner, r.output, r.query, r.key, r.value)
    made = (r.t_outer, r.t_inner, r.t_output, r.t_query, r.t_key, r.t_value)
    done = [pltpu.make_async_copy(src, dst, r.sem.at[4 + i]) for i, (src, dst) in enumerate(zip(made, outs))]

    def take(f):
        return pltpu.make_async_copy(r.fin.at[f], r.got.at[f], r.sem.at[10 + f])

    for f in range(PIECES):
        take(f).start()
    for f in range(4):
        take(f).wait()
        for h in range(2):
            r.t_outer[pl.ds(f * rows_f, rows_f), pl.ds(h * half, half)] = r.got[f, h].astype(F32)
    done[0].start()
    for f in range(4):
        take(4 + f).wait()
        for h in range(2):
            r.t_inner[:, pl.ds((4 * h + f) * cols_f, cols_f)] = r.got[4 + f, h].astype(F32)
    done[1].start()
    for f in range(8, PIECES):
        take(f).wait()
    for h in range(2):
        r.t_output[:, pl.ds(h * half, half)] = r.got[11, h].astype(F32)
    done[2].start()
    for i, ref in enumerate(made[3:]):
        for h in range(2):
            for p in range(half // 128):
                part = r.got[8 + p, h, :, pl.ds(i * 128, 128)].astype(F32)
                ref[:, pl.ds(h * half + p * 128, 128)] = part
        done[3 + i].start()
    seq = lax.axis_index("seq")
    width = 2 * half
    share = width // n_seq
    for i in range(8):
        r.rows[pl.ds(i, 1), :] = r.sout[:, pl.ds(i * width, width)]
    turned = pltpu.roll(r.rows[...], lax.rem(width - seq * share, width), 1)
    for i, ref in enumerate((r.qb, r.vb, r.ob, r.ag, r.sh, r.xb, r.fg, r.fs)):
        ref[...] = turned[i, :share]
    ib = r.ib.shape[0]
    full = r.sout.shape[1] - 8 * width
    r.wide[...] = jnp.broadcast_to(r.sout[:, pl.ds(8 * width, full)], (8, full))
    r.ib[...] = pltpu.roll(r.wide[...], lax.rem(full - seq * ib, full), 1)[0, :ib]
    for copy in leave + done:
        copy.wait()


def call(kernel, ins, outs, scratch, params, name, land=()):
    names = [*ins, *outs, *scratch]

    def body(*refs):
        extra = refs[len(names) :]
        shelf = iter(extra)
        nested = [[next(shelf) for _ in group] for group in land]
        kernel([*names, *(("land",) if land else ())], *refs[: len(names)], *((nested,) if land else ()))

    res = pl.pallas_call(
        body,
        out_shape=[jax.ShapeDtypeStruct(e[0], e[1]) for e in outs.values()],
        in_specs=[e[1] for e in ins.values()],
        out_specs=[e[2] for e in outs.values()],
        scratch_shapes=[*scratch.values(), *(e for group in land for e in group)],
        compiler_params=params,
        name=name,
    )(*[e[0] for e in ins.values()])
    return SimpleNamespace(**dict(zip(outs, res)))


def build(mesh):
    n_seq = mesh.shape["seq"]
    groups = n_seq // 8

    def local(
        hidden_in,
        depth_group,
        query_weight,
        query_bias,
        key_weight,
        value_weight,
        value_bias,
        output_weight,
        output_bias,
        attn_gain,
        attn_shift,
        inner_weight,
        inner_bias,
        outer_weight,
        outer_bias,
        final_gain,
        final_shift,
        grad_out,
    ):
        seqs, tok, width = hidden_in.shape
        ff = inner_weight.shape[1]
        seq_len = 4 * tok
        half = width // 2
        heads = half // HD
        pairs = half // 128
        rows_f, cols_f = width // 8, half
        small, late = 8 * width + ff, 2 * width
        hbm = pl.BlockSpec(memory_space=pl.ANY)
        vmem = pl.BlockSpec(memory_space=pltpu.VMEM)
        v = pltpu.VMEM
        dma = pltpu.SemaphoreType.DMA
        o = call(
            lambda *refs: layer_kernel(groups, *refs),
            dict(
                qb=(query_bias, vmem),
                vb=(value_bias, vmem),
                ob=(output_bias, vmem),
                ag=(attn_gain, vmem),
                sh=(attn_shift, vmem),
                xb=(outer_bias, vmem),
                fg=(final_gain, vmem),
                fs=(final_shift, vmem),
                ib=(inner_bias, vmem),
                dg=(depth_group, pl.BlockSpec(memory_space=pltpu.SMEM)),
                hid=(hidden_in, hbm),
                go=(grad_out, hbm),
                wq=(query_weight, hbm),
                wk=(key_weight, hbm),
                wv=(value_weight, hbm),
                wo_in=(output_weight, hbm),
                wi_in=(inner_weight, hbm),
                wx_in=(outer_weight, hbm),
            ),
            dict(
                hout=((seqs, tok, width), BF, hbm),
                gin=((seqs, tok, width), BF, hbm),
                fin=((PIECES, 2, rows_f, cols_f), BF, vmem),
                sout=((1, small), F32, vmem),
            ),
            dict(
                vec=v((1, small), F32),
                xall=v((2, 2, tok, width), BF),
                gown=v((2, tok, width), BF),
                wcat=v((width, 3 * half), BF),
                wo=v((width, width), BF),
                wi=v((width, ff), BF),
                wx=v((ff, width), BF),
                q=v((seq_len, half), BF),
                k=v((seq_len, half), BF),
                kt=v((half, seq_len), BF),
                vp=v((pairs, seq_len, 256), BF),
                lse=v((heads, 1, seq_len), F32),
                delta=v((heads, 1, seq_len), F32),
                att=v((2, 2, tok, width), BF),
                ga=v((2, 2, tok, width), BF),
                act=v((2 * tok, ff), BF),
                gp=v((2 * tok, ff), BF),
                inn=v((2 * tok, width), BF),
                gffn=v((2 * tok, width), BF),
                xh=v((2 * tok, width), F32),
                acc=v((2 * tok, width), F32),
                dka=v((seq_len, 128), F32),
                dva=v((seq_len, 128), F32),
                d2=v((2, 8, 2, 2, 2, rows_f, cols_f), BF),
                rc=v((8, 2, 2, 2, rows_f, cols_f), BF),
                dc=v((4, 2, 2, 2, rows_f, cols_f), BF),
                sg8=v((8, small), F32),
                s1s=v((6, 1, small - late), F32),
                s1r=v((5, 1, small - late), F32),
                s2s=v((6, 1, late), F32),
                s2r=v((5, 1, late), F32),
                lsem=dma((7 + 3 * pairs,)),
                ex_s=dma((EXCHANGES,)),
                ex_r=dma((EXCHANGES,)),
                rs_s=dma((len(FLOWS), 7)),
                rs_r=dma((len(FLOWS), 7)),
                sm_s=dma((10,)),
                sm_r=dma((10,)),
            ),
            pltpu.CompilerParams(collective_id=0, has_side_effects=True, vmem_limit_bytes=64 * 1024 * 1024),
            "layer",
            [[v(recv_shape(flow, k, rows_f), BF) for k in range(4)] for flow in FLOWS],
        )

        rows = [[g * groups + i for i in range(groups)] for g in range(8)]
        sout = o.sout
        if groups > 1:
            sout = lax.psum(sout, "seq", axis_index_groups=rows)
        mat, one = ((rows_f, width), F32, hbm), ((width // n_seq,), F32, vmem)
        staged = v((rows_f, width), F32)
        f = call(
            lambda *refs: finish_kernel(n_seq, *refs),
            dict(hout_in=(o.hout, hbm), gin_in=(o.gin, hbm), fin=(o.fin, hbm), sout=(sout, vmem)),
            dict(
                hout=(o.hout.shape, BF, hbm),
                gin=(o.gin.shape, BF, hbm),
                query=mat,
                key=mat,
                value=mat,
                output=mat,
                inner=((rows_f, ff), F32, hbm),
                outer=((ff // 8, width), F32, hbm),
                qb=one,
                vb=one,
                ob=one,
                ag=one,
                sh=one,
                xb=one,
                fg=one,
                fs=one,
                ib=((ff // n_seq,), F32, vmem),
            ),
            dict(
                sem=dma((10 + PIECES,)),
                got=v((PIECES, 2, rows_f, cols_f), BF),
                t_query=staged,
                t_key=staged,
                t_value=staged,
                t_output=staged,
                t_inner=v((rows_f, ff), F32),
                t_outer=v((ff // 8, width), F32),
                through=v((2, seqs, tok, width), BF),
                rows=v((8, width), F32),
                wide=v((8, ff), F32),
            ),
            pltpu.CompilerParams(vmem_limit_bytes=64 * 1024 * 1024),
            "finish",
        )

        def across(values):
            if groups == 1:
                return values
            return lax.psum_scatter(values, "seq", scatter_dimension=0, axis_index_groups=rows, tiled=True)

        return (
            f.hout,
            f.gin,
            across(f.query),
            f.qb,
            across(f.key),
            across(f.value),
            f.vb,
            across(f.output),
            f.ob,
            f.ag,
            f.sh,
            across(f.inner),
            f.ib,
            across(f.outer),
            f.xb,
            f.fg,
            f.fs,
        )

    return local


def solution(mesh):
    rows = P("seq", "blk", None)
    placed = (rows, P("seq"), *([P()] * 15), rows)
    mat, one = P("seq", None), P("seq")
    return jax.shard_map(
        build(mesh),
        mesh=mesh,
        in_specs=placed,
        out_specs=(rows, rows, mat, one, mat, mat, one, mat, one, one, one, mat, one, mat, one, one, one),
        check_vma=False,
    )
```

```python
import itertools
import math
from types import SimpleNamespace

import jax
import jax.numpy as jnp
from jax import lax
from jax.experimental import pallas as pl
from jax.experimental.pallas import tpu as pltpu
from jax.sharding import PartitionSpec as P

HD = 64
MESH = pl.DeviceIdType.MESH
BF = jnp.bfloat16
F32 = jnp.float32
LOG2E = math.log2(math.e)
SCALE2 = 0.125 * LOG2E
EPS = 1e-05

X, Y, Z0, Z1, C = range(5)
BITS = (Z1, Z0, Y)

PIECES = 12
OUTER, INNER, OUTPUT, PAIR = range(4)
S1, S2 = -1, -2
SMALL_ORDER = {S1: (C, Y, Z0, Z1, X), S2: (X, C, Y, Z0, Z1)}
FLOWS = (
    (OUTER, 0, 1, 0, 384, (Z0, X, Z1, Y)),
    (OUTER, 1, 1, 0, 384, (Y, Z1, Z0, X)),
    (OUTER, 2, 1, 0, 384, (X, Y, Z0, Z1)),
    (OUTER, 3, 1, 0, 384, (Z0, Y, Z1, X)),
    (INNER, 4, 1, 0, 384, (Y, Z1, Z0, X)),
    (INNER, 5, 1, 0, 384, (Y, X, Z0, Z1)),
    (INNER, 6, 1, 0, 384, (X, Y, Z0, Z1)),
    (INNER, 7, 1, 0, 384, (Z0, Y, Z1, X)),
    (OUTPUT, 11, 1, 0, 384, (X, Z0, Y, Z1)),
    (PAIR, 8, 1, 0, 384, (X, Y, Z0, Z1)),
    (PAIR + 1, 9, 1, 0, 384, (Y, Z0, Z1, X)),
    (PAIR + 2, 10, 1, 0, 128, (Z0, Y, Z1, X)),
    (PAIR + 2, 10, 1, 128, 128, (X, Z1, Y, Z0)),
    (PAIR + 2, 10, 1, 256, 128, (Y, Z0, Z1, X)),
)
PLAN = (
    (),
    ((0, -1), (1, -1)),
    ((2, -1), (3, -1)),
    (),
    (),
    ((S1, 0), (4, -1), (0, 0), (1, 0)),
    ((5, -1),),
    ((6, -1), (S1, 1), (7, -1)),
    (),
    ((2, 0),),
    ((0, 1), (1, 1), (4, 0), (3, 0), (S1, 2)),
    (),
    ((6, 0), (5, 0), (0, 2)),
    ((2, 1), (7, 0)),
    ((8, 0), (3, 1), (1, 2), (4, 1)),
    ((S1, 3), (6, 1), (2, 2), (0, 3), (9, 0)),
    ((3, 2), (7, 1), (5, 1), (8, 1), (2, 3)),
    ((1, 3), (4, 2), (S1, 4), (0, 4)),
    ((6, 2), (3, 3), (10, 0), (2, 4), (7, 2)),
    ((5, 2), (12, 0), (S2, 0), (9, 1)),
    ((4, 3), (6, 3), (8, 2), (11, 0), (S2, 1)),
    (
        (7, 3), (13, 0), (5, 3), (11, 1), (S2, 2), (12, 1), (10, 1), (8, 3), (12, 2), (11, 2), (9, 2), (13, 1),
        (S2, 3), (10, 2), (6, 4), (12, 3), (5, 4), (9, 3), (8, 4), (11, 3), (13, 2), (S2, 4), (10, 3), (12, 4),
        (9, 4), (13, 3), (1, 5), (0, 5), (3, 5), (2, 5), (4, 5), (7, 5), (6, 5), (5, 5), (8, 5), (11, 5),
        (10, 5), (12, 5), (9, 5), (13, 5),
    ),
)

QB, VB, OB, AG, AS, XB, FG, FS, IB = range(9)
GO, GA, HX, HC, HF, HO, GP, GI, AT, AO = 0, 1, 2, 4, 6, 8, 10, 12, 14, 18
EXCHANGES = 19


def nn(left, right):
    return jnp.dot(left, right, preferred_element_type=F32)


def nt(left, right):
    return lax.dot_general(left, right, (((1,), (1,)), ((), ())), preferred_element_type=F32)


def tn(left, right):
    return lax.dot_general(left, right, (((0,), (0,)), ((), ())), preferred_element_type=F32)


def fold8(values):
    rows, width = values.shape
    return jnp.sum(values.reshape(rows // 8, 8, width), axis=0)


def halves_rows(order, k):
    return X in order[: k + 1] and order.index(X) < 3


def recv_shape(flow, k, rows):
    part, f, nf, start, cols, order = flow
    free = [2 for ax in BITS if ax not in order[: k + 1]]
    return (nf, *free, rows // 2 if halves_rows(order, k) else rows, cols)


def layer_kernel(groups, names, *refs):
    r = SimpleNamespace(**dict(zip(names, refs)))
    seq = lax.axis_index("seq")
    blk = lax.axis_index("blk")
    x = lax.div(blk, 2)
    c = lax.rem(blk, 2)
    hi = lax.div(seq, groups)
    own = {X: x, Y: lax.rem(hi, 2), Z0: lax.rem(lax.div(hi, 2), 2), Z1: lax.div(hi, 4)}
    peers = {
        C: (seq, blk + 1 - 2 * c),
        X: (seq, blk + 2 - 4 * x),
        Y: (seq + (1 - 2 * own[Y]) * groups, blk),
        Z0: (seq + (1 - 2 * own[Z0]) * 2 * groups, blk),
        Z1: (seq + (1 - 2 * own[Z1]) * 4 * groups, blk),
    }
    part_tok, width = r.xall.shape[2:]
    tok = 2 * part_tok
    groups_q = r.xall.shape[0]
    seq_len = groups_q * tok
    half = width // 2
    ff = r.wi.shape[1]
    pairs = half // 128
    own_heads = pl.ds(pl.multiple_of(c * half, 128), half)
    other_heads = pl.ds(pl.multiple_of((1 - c) * half, 128), half)

    def vec(i, start=0, size=width):
        return r.vec[:, pl.ds(width * i + start, size)]

    def pair_lanes(p, base=0):
        return pl.ds(pl.multiple_of(base * width + c * half + p * 128, 128), 128)

    def remote(src, dst, send, recv, peer):
        return pltpu.make_async_remote_copy(
            src_ref=src, dst_ref=dst, send_sem=send, recv_sem=recv, device_id=peers[peer], device_id_type=MESH
        )

    barrier = pltpu.get_barrier_semaphore()
    for peer in peers.values():
        pl.semaphore_signal(barrier, inc=1, device_id=peer, device_id_type=MESH)

    lcount = itertools.count()

    def fetch(src, dst):
        return pltpu.make_async_copy(src, dst, r.lsem.at[next(lcount)])

    def half_block(ref, seq_at, i):
        return ref.at[seq_at, pl.ds(i * part_tok, part_tok)]

    first = [fetch(half_block(r.hid, x, i), r.xall.at[i, c]) for i in range(2)]
    for p in range(pairs):
        for i, w in enumerate((r.wq, r.wk, r.wv)):
            first.append(fetch(w.at[:, pair_lanes(p)], r.wcat.at[:, pl.ds((3 * p + i) * 128, 128)]))
    second = [
        fetch(r.go.at[x], r.gown.at[0]),
        fetch(r.wo_in, r.wo),
        fetch(r.wi_in, r.wi),
        fetch(r.wx_in, r.wx),
    ]
    for copy in first + second:
        copy.start()
    params = (r.qb, r.vb, r.ob, r.ag, r.sh, r.xb, r.fg, r.fs, r.ib)
    third = [fetch(ref, r.raw.at[pl.ds(width * i, ref.shape[0])]) for i, ref in enumerate(params)]
    third.append(fetch(r.dg, r.kept))
    for copy in third:
        copy.start()
    pl.semaphore_wait(barrier, len(peers))

    def ex(i):
        if i == GO:
            src, dst, peer = r.go.at[1 - x], r.gown.at[1], X
        elif i == GA:
            src = dst = r.ga.at[:, c]
            peer = C
        elif i < HC:
            src, dst, peer = half_block(r.hid, 1 - x, i - HX), r.xall.at[2 + i - HX, c], X
        elif i < HF:
            src, dst, peer = half_block(r.hid, x, i - HC), r.xall.at[i - HC, c], C
        elif i < HO:
            src = dst = r.xall.at[2 + i - HF, c]
            peer = C
        elif i < GP:
            src, dst, peer = r.ga.at[2 + i - HO, c], half_block(r.hout, x, i - HO), X
        elif i < GI:
            at = pl.ds(2 * (i - GP), 2)
            src, dst, peer = r.gffn.at[at], r.xall.at[at, 1 - c], C
        elif i < AT:
            src, dst, peer = r.inn.at[2 + i - GI], half_block(r.gin, x, i - GI), X
        elif i < AO:
            src = dst = r.att.at[i - AT, 1 - c, :, own_heads]
            peer = C
        else:
            src = dst = r.att.at[:, c, :, own_heads]
            peer = C
        return remote(src, dst, r.ex_s.at[i], r.ex_r.at[i], peer)

    for i in (HX, HX + 1, HC, HC + 1, GO):
        ex(i).start()
    for copy in third:
        copy.wait()
    r.vec[...] = r.raw[...].astype(F32).reshape(1, r.raw.shape[0])
    r.sg8[...] = jnp.zeros_like(r.sg8)
    kept = jnp.where(r.kept[x] == 2, 0.0, 1.0).astype(F32)

    lane_head = lax.broadcasted_iota(jnp.int32, (tok, 128), 1) // HD
    ones = jnp.ones((seq_len, 128), BF)
    for p in range(pairs):
        r.vp[p, :, pl.ds(128, 128)] = ones

    def project(j):
        out = nn(r.xall[j].reshape(tok, width), r.wcat[...])
        at = pl.ds(pl.multiple_of(j * tok, tok), tok)
        for p in range(pairs):
            lanes = pl.ds(p * 128, 128)
            base = 3 * p * 128
            r.q[at, lanes] = (out[:, base : base + 128] + r.vec[:, pair_lanes(p, QB)]).astype(BF)
            key = out[:, base + 128 : base + 256].astype(BF)
            r.k[at, lanes] = key
            r.kt[lanes, at] = key.T
            r.vp[p, at, pl.ds(0, 128)] = (out[:, base + 256 : base + 384] + r.vec[:, pair_lanes(p, VB)]).astype(BF)

    def attend(j, start, count, begin_here, end_here):
        rows = pl.ds(pl.multiple_of(j * tok, tok), tok)
        keys = pl.ds(start, count)
        for p in range(pairs):
            lanes = pl.ds(p * 128, 128)
            out_ref = r.work.at[rows, lanes]
            top_ref = r.work.at[rows, pl.ds(half + p * 128, 128)]
            sum_lanes = pl.ds(pl.multiple_of(j * 128, 128), 128)
            sum_ref = (r.dva.at[rows], r.dka.at[rows], r.work.at[pl.ds(3 * tok, tok), sum_lanes])[p]
            qp = r.q[rows, lanes]
            tops, parts = [], []
            for h in range(2):
                qm = jnp.where(lane_head == h, qp, jnp.zeros_like(qp))
                s = nn(qm, r.kt[lanes, keys])
                top = jnp.max(s, axis=1, keepdims=True)
                pt = jnp.exp2((s - top) * SCALE2).astype(BF)
                tops.append(top)
                parts.append(nn(pt, r.vp[p, keys, :]))
            top = jnp.where(lane_head == 0, tops[0], tops[1])
            out = jnp.where(lane_head == 0, parts[0][:, :128], parts[1][:, :128])
            total = jnp.where(lane_head == 0, parts[0][:, 128:], parts[1][:, 128:])
            if not begin_here:
                old = top_ref[...]
                both = jnp.maximum(old, top)
                grow, shrink = jnp.exp2((top - both) * SCALE2), jnp.exp2((old - both) * SCALE2)
                out = out * grow + out_ref[...] * shrink
                total = total * grow + sum_ref[...] * shrink
                top = both
            if end_here:
                r.att[j, :, :, pair_lanes(p)] = (out / total).astype(BF).reshape(2, part_tok, 128)
                both = (top * SCALE2 + jnp.log2(total)).T
                for h in range(2):
                    r.lse[2 * p + h, :, rows] = both[h * HD : h * HD + 1]
            else:
                out_ref[...] = out
                top_ref[...] = top
                sum_ref[...] = total

    for copy in first:
        copy.wait()
    for i in range(2):
        ex(HC + i).wait_recv()

    @pl.loop(0, 2)
    def _(j):
        project(j)

    @pl.loop(0, 2)
    def _(j):
        attend(j, 0, 2 * tok, True, False)

    ex(HX).wait_recv()
    ex(HF).start()
    ex(HF).wait_recv()
    project(2)

    attend(2, 0, 3 * tok, True, False)
    ex(HX + 1).wait_recv()
    ex(HF + 1).start()
    ex(HF + 1).wait_recv()
    project(3)
    attend(3, 0, 4 * tok, True, True)
    ex(AT + 3).start()
    for j, start in ((2, 3 * tok), (1, 2 * tok), (0, 2 * tok)):
        attend(j, start, 4 * tok - start, False, True)
        ex(AT + j).start()
    ex(AO).start()

    for copy in second:
        copy.wait()

    def own_rows(i):
        return i // 2, pl.ds((i % 2) * part_tok, part_tok), pl.ds(i * part_tok, part_tok)

    def fold_in(i, values):
        at = pl.ds(width * i, values.shape[1])
        r.sg8[:, at] += fold8(values)

    def heads_out(heads):
        return nn(r.att[:, c, :, heads].reshape(2 * tok, half), r.wo[heads, :])

    acc, xh_ref = r.work.at[pl.ds(0, 2 * tok)], r.work.at[pl.ds(2 * tok, 2 * tok)]
    acc[...] = heads_out(own_heads)
    for j in range(groups_q):
        ex(AT + j).wait_recv()
    acc[...] += heads_out(other_heads)

    for i in range(4):
        which, inner, rows = own_rows(i)
        v = acc[rows, :] + vec(OB) + r.xall[i, c].astype(F32)
        cen = v - jnp.mean(v, axis=-1, keepdims=True)
        rstd = lax.rsqrt(jnp.mean(cen * cen, axis=-1, keepdims=True) + EPS)
        xh = cen * rstd
        normed = xh * vec(AG) + vec(AS)
        xh_ref[rows, :] = xh
        r.dva[rows, pl.ds(0, 1)] = rstd
        acc[rows, :] = normed
        r.inn[i] = normed.astype(BF)

    tile = 512

    def activate(j):
        start = pl.multiple_of(j * tile, tile)
        at = pl.ds(start, tile)
        pre = nn(r.inn[...].reshape(2 * tok, width), r.wi[:, at]) + r.vec[:, pl.ds(pl.multiple_of(width * IB + start, 128), tile)]
        phi = 0.5 + 0.5 * lax.erf(pre * math.sqrt(0.5))
        dens = jnp.exp2(pre * pre * (-0.5 * LOG2E)) * (1.0 / math.sqrt(2.0 * math.pi))
        r.act[:, at] = (pre * phi).astype(BF)
        r.gp[:, at] = (phi + pre * dens).astype(BF)

    @pl.loop(0, 2)
    def _(i):
        for j in range(ff // tile // 2):
            activate(i * (ff // tile // 2) + j)

    @pl.loop(0, width // 256)
    def _(j):
        at = pl.ds(pl.multiple_of(j * 256, 256), 256)
        acc[:, at] += nn(r.act[...], r.wx[:, at])

    ex(GO).wait_recv()
    for i in range(4):
        which, inner, rows = own_rows(i)
        xf = r.xall[i, c].astype(F32)
        v = acc[rows, :] + vec(XB)
        cen = v - jnp.mean(v, axis=-1, keepdims=True)
        rstd = lax.rsqrt(jnp.mean(cen * cen, axis=-1, keepdims=True) + EPS)
        xh = cen * rstd
        out = kept * (xh * vec(FG) + vec(FS)) + (1.0 - kept) * xf
        r.ga[i, c] = out.astype(BF)
        g = kept * r.gown[which, inner, :].astype(F32)
        fold_in(FG, g * xh)
        fold_in(FS, g)
        gx = g * vec(FG)
        m1 = jnp.mean(gx, axis=-1, keepdims=True)
        m2 = jnp.mean(gx * xh, axis=-1, keepdims=True)
        gs = rstd * (gx - m1 - xh * m2)
        low = gs.astype(BF)
        acc[rows, :] = gs
        r.gffn[i] = low
        fold_in(XB, low.astype(F32))

    ex(HO).start()
    ex(HO + 1).start()
    hout_local = [fetch(r.ga.at[i, c], half_block(r.hout, x, i)) for i in range(2)]
    for copy in hout_local:
        copy.start()

    rows_f, cols_f = r.dc.shape[-2:]
    x_rows = pl.ds(pl.multiple_of(x * (rows_f // 2), 16), rows_f // 2)

    def pieces(flow):
        f, nf = flow[1:3]
        return r.d2.at[c, pl.ds(f, nf)] if f < 8 else r.dc.at[pl.ds(f - 8, nf)]

    def view(flow, k, send):
        part, f, nf, start, cols, order = flow
        idx = [slice(None)] * 3
        row = pl.ds(0, rows_f)
        for j, ax in enumerate(order[: k + 1]):
            want = 1 - own[ax] if (j == k and send) else own[ax]
            if ax != X:
                idx[BITS.index(ax)] = want
            elif j < 3:
                row = pl.ds(pl.multiple_of(want * (rows_f // 2), 16), rows_f // 2)
        return (slice(None), *idx, row, pl.ds(start, cols))

    def hop(i, k):
        flow = FLOWS[i]
        src = pieces(flow).at[view(flow, k, True)]
        return remote(src, r.land[i][k], r.rs_s.at[i, k], r.rs_r.at[i, k], flow[5][k])

    def add_in(i, k):
        flow = FLOWS[i]
        nf, order = flow[2], flow[5]
        idx = list(view(flow, k, False))
        ref = pieces(flow)
        free = [ax for ax in BITS if ax not in order[: k + 1]]
        for n in range(nf):
            idx[0] = n
            for combo in itertools.product((0, 1), repeat=len(free)):
                for ax, bit in zip(free, combo):
                    idx[1 + BITS.index(ax)] = bit
                at = tuple(idx)
                ref[at] = ref[at] + r.land[i][k][(n, *combo, slice(None), slice(None))]

    def spread(i, k):
        part, f, nf, start, cols, order = FLOWS[i]
        rows = x_rows if k == 4 else pl.ds(0, rows_f)
        ref = r.sums.at[pl.ds(f, nf), c, rows, pl.ds(start, cols)]
        return remote(ref, ref, r.rs_s.at[i, k], r.rs_r.at[i, k], X if k == 4 else C)

    def save(i):
        part, f, nf, start, cols, order = FLOWS[i]
        at = (pl.ds(f, nf), slice(None), slice(None), pl.ds(start, cols))
        return pltpu.make_async_copy(r.sums.at[at], r.fin.at[at], r.rs_s.at[i, 7])

    def core_sum(i):
        part, f, nf, start, cols, order = FLOWS[i]
        at = pl.ds(f, nf)
        return remote(r.d2.at[1 - c, at], r.rc.at[at], r.rs_s.at[i, 6], r.rs_r.at[i, 6], C)

    def small(which, k):
        send, recv = (r.s1s, r.s1r) if which == S1 else (r.s2s, r.s2r)
        at = k if which == S1 else 5 + k
        return remote(send.at[k], recv.at[k], r.sm_s.at[at], r.sm_r.at[at], SMALL_ORDER[which][k])

    def step(i, k):
        if i < 0:
            send, recv = (r.s1s, r.s1r) if i == S1 else (r.s2s, r.s2r)
            small(i, k).wait_recv()
            send[k + 1] = send[k] + recv[k]
            if k < 4:
                small(i, k + 1).start()
            return
        flow = FLOWS[i]
        part, f, nf, start, cols, order = flow
        if k == -1:
            core_sum(i).wait_recv()
            ref = pieces(flow)
            for combo in itertools.product(range(nf), (0, 1), (0, 1), (0, 1)):
                ref[combo] = ref[combo] + r.rc[(f + combo[0], *combo[1:])]
            hop(i, 0).start()
        elif k < 3:
            hop(i, k).wait_recv()
            add_in(i, k)
            hop(i, k + 1).start()
        elif k == 3:
            hop(i, 3).wait_recv()
            rows = pl.ds(0, rows_f) if order[3] == X else x_rows
            at = pl.ds(start, cols)
            for n in range(nf):
                mine_part = pieces(flow)[(n, own[Z1], own[Z0], own[Y], rows, at)]
                r.sums[f + n, c, rows, at] = mine_part + r.land[i][3][n]
            spread(i, 5 if order[3] == X else 4).start()
        elif k == 4:
            spread(i, 4).wait_recv()
            spread(i, 5).start()
        else:
            spread(i, 5).wait_recv()
            save(i).start()

    plan = iter(PLAN)

    def tick():
        for i, k in next(plan):
            step(i, k)

    def begin(part):
        for i, flow in enumerate(FLOWS):
            if flow[0] == part:
                (core_sum(i) if flow[1] < 8 else hop(i, 0)).start()

    outer_rows = ff // 8

    @pl.loop(0, 2)
    def _(i):
        for j in range(4):
            at = pl.ds(pl.multiple_of((4 * i + j) * outer_rows, 128), outer_rows)
            val = tn(r.act[:, at], r.gffn[...].reshape(2 * tok, width)).astype(BF)
            for f in range(4):
                for h in range(2):
                    part = val[f * rows_f : (f + 1) * rows_f, h * cols_f : (h + 1) * cols_f]
                    r.d2[h, f, i, j // 2, j % 2] = part

    begin(OUTER)
    tick()

    tile = ff // 4

    @pl.loop(0, 2)
    def _(i):
        for j in range(2):
            start = pl.multiple_of((2 * i + j) * tile, tile)
            at = pl.ds(start, tile)
            gpre = (nt(r.gffn[...].reshape(2 * tok, width), r.wx[at, :]) * r.gp[:, at].astype(F32)).astype(BF)
            r.gp[:, at] = gpre
            r.sg8[:, pl.ds(pl.multiple_of(width * IB + start, 128), tile)] = fold8(gpre.astype(F32))

    tick()


    @pl.loop(0, width // 256)
    def _(j):
        at = pl.ds(pl.multiple_of(j * 256, 256), 256)
        acc[:, at] += nt(r.gp[...], r.wi[at, :])

    tick()
    ex(HO).wait_send()
    ex(HO + 1).wait_send()
    for copy in hout_local:
        copy.wait()
    for i in range(4):
        which, inner, rows = own_rows(i)
        g = acc[rows, :]
        xh = xh_ref[rows, :]
        fold_in(AG, g * xh)
        fold_in(AS, g)
        gx = g * vec(AG)
        m1 = jnp.mean(gx, axis=-1, keepdims=True)
        m2 = jnp.mean(gx * xh, axis=-1, keepdims=True)
        gs = r.dva[rows, pl.ds(0, 1)] * (gx - m1 - xh * m2)
        low = gs.astype(BF)
        acc[rows, :] = gs
        r.ga[i, c] = low
        fold_in(OB, low.astype(F32))

    xt = r.wi.at[:, pl.ds(0, seq_len)]
    xt[...] = r.xall[...].reshape(seq_len, width).T
    for i in range(2):
        ex(HF + i).wait_send()
    ex(GA).start()
    late = 2 * width
    r.s1s[0] = jnp.sum(r.sg8[:, pl.ds(late, r.s1s.shape[2])], axis=0, keepdims=True)
    small(S1, 0).start()
    tick()

    @pl.loop(0, 2)
    def _(i):
        for h in range(2):
            at = pl.ds(pl.multiple_of((2 * h + i) * tile, tile), tile)
            val = tn(r.inn[...].reshape(2 * tok, width), r.gp[:, at]).astype(BF)
            for m in range(2):
                part = val[:, m * cols_f : (m + 1) * cols_f]
                r.d2[h, 4 + 2 * i + m] = part.reshape(2, 2, 2, rows_f, cols_f)
        for n in range(2):

            @pl.when(i == n)
            def _():
                for g, flow in enumerate(FLOWS):
                    if flow[0] == INNER and (flow[1] + flow[2] - 1) // 2 == 2 + n:
                        core_sum(g).start()
                tick()


    def dqkv(p):
        rows = pl.ds(pl.multiple_of(lax.div(p, 2) * seq_len, 1024), seq_len)
        return r.wx.at[rows, pl.ds(pl.multiple_of(lax.rem(p, 2) * 384, 128), 384)]

    do = r.wx.at[pl.ds(seq_len, seq_len), pl.ds(384, half)]

    def upstream(core):
        val = nt(r.ga[:, core].reshape(2 * tok, width), r.wo[own_heads, :]).astype(BF)
        for j in range(groups_q):
            at = pl.ds(pl.multiple_of(j * tok + core * part_tok, part_tok), part_tok)
            do[at, :] = val[j * part_tok : (j + 1) * part_tok]

    upstream(c)
    tick()
    ex(GA).wait_recv()
    upstream(1 - c)

    for p in range(pairs):
        at = r.att[:, :, :, pair_lanes(p)].reshape(seq_len, 128)
        prod = (at.astype(F32) * do[:, pl.ds(p * 128, 128)].astype(F32)).T
        for h in range(2):
            r.delta[2 * p + h] = jnp.sum(prod[h * HD : (h + 1) * HD], axis=0, keepdims=True)
    tick()

    ex(AO).wait_recv()
    att_all = r.att[...].reshape(seq_len, width)
    ga_cols = r.ga[:, :, :, own_heads].reshape(seq_len, half)
    r.dc[3] = tn(att_all, ga_cols).astype(BF).reshape(2, 2, 2, rows_f, cols_f)
    begin(OUTPUT)
    tick()

    steps = [[next(plan) for _ in range(groups_q // 2 + 1)] for _ in range(pairs)]

    def tick_at(p, j):
        for n in range(pairs):
            if steps[n][j]:

                @pl.when(p == n)
                def _():
                    for i, k in steps[n][j]:
                        step(i, k)

    def backward(p, t):
        lanes = pl.ds(pl.multiple_of(p * 128, 128), 128)
        rows = pl.ds(pl.multiple_of(t * tok, tok), tok)
        qp = r.q[rows, lanes]
        dp = do[rows, lanes]
        kp = r.k[:, lanes]
        vp = r.vp[p, :, pl.ds(0, 128)]
        zero = jnp.zeros_like(qp)
        dqs = []
        for h in range(2):
            qm = jnp.where(lane_head == h, qp, zero)
            dm = jnp.where(lane_head == h, dp, zero)
            pt = jnp.exp2(nt(kp, qm) * SCALE2 - r.lse[2 * p + h, :, rows])
            ds = (pt * (nt(vp, dm) - r.delta[2 * p + h, :, rows])).astype(BF)
            r.dva[...] += nn(pt.astype(BF), dm)
            r.dka[...] += nn(ds, qm)
            dqs.append(nn(r.kt[pl.ds(pl.multiple_of(p * 128 + h * HD, HD), HD), :], ds))
        both = (jnp.concatenate(dqs, axis=0) * 0.125).astype(BF)
        dqkv(p)[rows, pl.ds(0, 128)] = both.T

    @pl.loop(0, pairs)
    def _(p):
        r.dva[...] = jnp.zeros_like(r.dva)
        r.dka[...] = jnp.zeros_like(r.dka)

        for t in range(groups_q):
            backward(p, t)
            if t % 2:
                tick_at(p, t // 2)

        dqkv(p)[:, pl.ds(128, 128)] = (r.dka[...] * 0.125).astype(BF)
        dqkv(p)[:, pl.ds(256, 128)] = r.dva[...].astype(BF)
        r.dc[p] = nn(xt[...], dqkv(p)[...]).astype(BF).reshape(2, 2, 2, rows_f, cols_f)
        r.sg8[:, pair_lanes(p, QB)] = fold8(dqkv(p)[:, pl.ds(0, 128)].astype(F32))
        r.sg8[:, pair_lanes(p, VB)] = fold8(dqkv(p)[:, pl.ds(256, 128)].astype(F32))
        for n in range(pairs):

            @pl.when(p == n)
            def _():
                begin(PAIR + n)
                if n == pairs - 1:
                    r.s2s[0] = jnp.sum(r.sg8[:, pl.ds(0, late)], axis=0, keepdims=True)
                    small(S2, 0).start()

        tick_at(p, 2)

    def partial(core, j):
        rows = [pl.ds(pl.multiple_of(n * tok + core * part_tok, part_tok), part_tok) for n in (2 * j, 2 * j + 1)]
        left = jnp.concatenate([r.wx[at, pl.ds(0, 768)] for at in rows], axis=0)
        right = jnp.concatenate([dqkv(2)[at, :] for at in rows], axis=0)
        return nt(left, r.wcat[:, pl.ds(0, 768)]) + nt(right, r.wcat[:, pl.ds(768, 384)])

    for i in (1, 0):
        r.gffn[pl.ds(2 * i, 2)] = partial(1 - c, i).astype(BF).reshape(2, part_tok, width)
        ex(GP + i).start()
    tick()
    for i in (1, 0):
        acc[pl.ds(i * tok, tok), :] += partial(c, i)
    tick()
    for i in (1, 0):
        ex(GP + i).wait_recv()
        for j in (2 * i, 2 * i + 1):
            which, inner, rows = own_rows(j)
            total = acc[rows, :] + r.xall[j, c].astype(F32) + (1.0 - kept) * r.gown[which, inner, :].astype(F32)
            r.inn[j] = total.astype(BF)
            if i:
                ex(GI + j - 2).start()
    gin_local = [fetch(r.inn.at[i], half_block(r.gin, x, i)) for i in range(2)]
    for copy in gin_local:
        copy.start()
    tick()
    tick()
    r.sout[:, pl.ds(0, late)] = r.s2s[5]
    r.sout[:, pl.ds(late, r.s1s.shape[2])] = r.s1s[5]

    for i in (HO, HO + 1, GI, GI + 1):
        ex(i).wait_recv()
    for copy in gin_local:
        copy.wait()
    for i in range(EXCHANGES):
        if i not in (HF, HF + 1, HO, HO + 1):
            ex(i).wait_send()
    for k in range(5):
        small(S1, k).wait_send()
        small(S2, k).wait_send()
    for i, flow in enumerate(FLOWS):
        for k in range(4):
            hop(i, k).wait_send()
        if flow[5][3] != X:
            spread(i, 4).wait_send()
        spread(i, 5).wait_send()
        save(i).wait()
        if flow[1] < 8:
            core_sum(i).wait_send()


def finish_kernel(n_seq, names, *refs):
    r = SimpleNamespace(**dict(zip(names, refs)))
    pairs = ((r.hout_in, r.hout), (r.gin_in, r.gin))
    arrive = [pltpu.make_async_copy(pair[0], r.through.at[i], r.sem.at[i]) for i, pair in enumerate(pairs)]
    leave = [pltpu.make_async_copy(r.through.at[i], pair[1], r.sem.at[2 + i]) for i, pair in enumerate(pairs)]
    flat = pltpu.make_async_copy(r.sout, r.flat, r.sem.at[10 + PIECES])
    flat.start()
    for copy in arrive:
        copy.start()
    for before, after in zip(arrive, leave):
        before.wait()
        after.start()
    rows_f, cols_f = r.fin.shape[2:]
    half = cols_f
    outs = (r.outer, r.inner, r.output, r.query, r.key, r.value)
    made = (r.t_outer, r.t_inner, r.t_output, r.t_query, r.t_key, r.t_value)
    done = [pltpu.make_async_copy(src, dst, r.sem.at[4 + i]) for i, (src, dst) in enumerate(zip(made, outs))]

    def take(f):
        return pltpu.make_async_copy(r.fin.at[f], r.got.at[f], r.sem.at[10 + f])

    for f in range(PIECES):
        take(f).start()
    for f in range(4):
        take(f).wait()
        for h in range(2):
            r.t_outer[pl.ds(f * rows_f, rows_f), pl.ds(h * half, half)] = r.got[f, h].astype(F32)
    done[0].start()
    for f in range(4):
        take(4 + f).wait()
        for h in range(2):
            r.t_inner[:, pl.ds((4 * h + f) * cols_f, cols_f)] = r.got[4 + f, h].astype(F32)
    done[1].start()
    for f in range(8, PIECES):
        take(f).wait()
    for h in range(2):
        r.t_output[:, pl.ds(h * half, half)] = r.got[11, h].astype(F32)
    done[2].start()
    for i, ref in enumerate(made[3:]):
        for h in range(2):
            for p in range(half // 128):
                part = r.got[8 + p, h, :, pl.ds(i * 128, 128)].astype(F32)
                ref[:, pl.ds(h * half + p * 128, 128)] = part
        done[3 + i].start()
    seq = lax.axis_index("seq")
    width = 2 * half
    share = width // n_seq
    flat.wait()
    for i in range(8):
        r.rows[pl.ds(i, 1), :] = r.flat[:, pl.ds(i * width, width)]
    turned = pltpu.roll(r.rows[...], lax.rem(width - seq * share, width), 1)
    for i, ref in enumerate((r.t_qb, r.t_vb, r.t_ob, r.t_ag, r.t_sh, r.t_xb, r.t_fg, r.t_fs)):
        ref[...] = turned[i, :share]
    ib = r.ib.shape[0]
    full = r.flat.shape[1] - 8 * width
    r.wide[...] = jnp.broadcast_to(r.flat[:, pl.ds(8 * width, full)], (8, full))
    r.t_ib[...] = pltpu.roll(r.wide[...], lax.rem(full - seq * ib, full), 1)[0, :ib]
    vectors = (r.qb, r.vb, r.ob, r.ag, r.sh, r.xb, r.fg, r.fs, r.ib)
    shares = (r.t_qb, r.t_vb, r.t_ob, r.t_ag, r.t_sh, r.t_xb, r.t_fg, r.t_fs, r.t_ib)
    for i, (src, dst) in enumerate(zip(shares, vectors)):
        done.append(pltpu.make_async_copy(src, dst, r.sem.at[11 + PIECES + i]))
        done[-1].start()
    for copy in leave + done:
        copy.wait()


def call(kernel, ins, outs, scratch, params, name, land=()):
    names = [*ins, *outs, *scratch]

    def body(*refs):
        extra = refs[len(names) :]
        shelf = iter(extra)
        nested = [[next(shelf) for _ in group] for group in land]
        kernel([*names, *(("land",) if land else ())], *refs[: len(names)], *((nested,) if land else ()))

    res = pl.pallas_call(
        body,
        out_shape=[jax.ShapeDtypeStruct(e[0], e[1]) for e in outs.values()],
        in_specs=[e[1] for e in ins.values()],
        out_specs=[e[2] for e in outs.values()],
        scratch_shapes=[*scratch.values(), *(e for group in land for e in group)],
        compiler_params=params,
        name=name,
    )(*[e[0] for e in ins.values()])
    return SimpleNamespace(**dict(zip(outs, res)))


def build(mesh):
    n_seq = mesh.shape["seq"]
    groups = n_seq // 8

    def local(
        hidden_in,
        depth_group,
        query_weight,
        query_bias,
        key_weight,
        value_weight,
        value_bias,
        output_weight,
        output_bias,
        attn_gain,
        attn_shift,
        inner_weight,
        inner_bias,
        outer_weight,
        outer_bias,
        final_gain,
        final_shift,
        grad_out,
    ):
        seqs, tok, width = hidden_in.shape
        ff = inner_weight.shape[1]
        seq_len = 4 * tok
        half = width // 2
        heads = half // HD
        pairs = half // 128
        rows_f, cols_f = width // 8, half
        small, late = 8 * width + ff, 2 * width
        hbm = pl.BlockSpec(memory_space=pl.ANY)
        vmem = pl.BlockSpec(memory_space=pltpu.VMEM)
        v = pltpu.VMEM
        dma = pltpu.SemaphoreType.DMA
        o = call(
            lambda *refs: layer_kernel(groups, *refs),
            dict(
                qb=(query_bias, hbm),
                vb=(value_bias, hbm),
                ob=(output_bias, hbm),
                ag=(attn_gain, hbm),
                sh=(attn_shift, hbm),
                xb=(outer_bias, hbm),
                fg=(final_gain, hbm),
                fs=(final_shift, hbm),
                ib=(inner_bias, hbm),
                dg=(depth_group, hbm),
                hid=(hidden_in, hbm),
                go=(grad_out, hbm),
                wq=(query_weight, hbm),
                wk=(key_weight, hbm),
                wv=(value_weight, hbm),
                wo_in=(output_weight, hbm),
                wi_in=(inner_weight, hbm),
                wx_in=(outer_weight, hbm),
            ),
            dict(
                hout=((seqs, tok, width), BF, hbm),
                gin=((seqs, tok, width), BF, hbm),
                fin=((PIECES, 2, rows_f, cols_f), BF, hbm),
                sout=((1, small), F32, vmem),
            ),
            dict(
                kept=pltpu.SMEM((seqs,), jnp.int32),
                raw=v((small,), BF),
                vec=v((1, small), F32),
                xall=v((4, 2, tok // 2, width), BF),
                gown=v((2, tok, width), BF),
                wcat=v((width, 3 * half), BF),
                wo=v((width, width), BF),
                wi=v((width, ff), BF),
                wx=v((ff, width), BF),
                q=v((seq_len, half), BF),
                k=v((seq_len, half), BF),
                kt=v((half, seq_len), BF),
                vp=v((pairs, seq_len, 256), BF),
                lse=v((heads, 1, seq_len), F32),
                delta=v((heads, 1, seq_len), F32),
                att=v((4, 2, tok // 2, width), BF),
                ga=v((4, 2, tok // 2, width), BF),
                act=v((2 * tok, ff), BF),
                gp=v((2 * tok, ff), BF),
                inn=v((4, tok // 2, width), BF),
                gffn=v((4, tok // 2, width), BF),
                work=v((4 * tok, width), F32),
                dka=v((seq_len, 128), F32),
                dva=v((seq_len, 128), F32),
                d2=v((2, 8, 2, 2, 2, rows_f, cols_f), BF),
                rc=v((8, 2, 2, 2, rows_f, cols_f), BF),
                dc=v((4, 2, 2, 2, rows_f, cols_f), BF),
                sg8=v((8, small), F32),
                s1s=v((6, 1, small - late), F32),
                s1r=v((5, 1, small - late), F32),
                s2s=v((6, 1, late), F32),
                s2r=v((5, 1, late), F32),
                lsem=dma((20 + 3 * pairs,)),
                ex_s=dma((EXCHANGES,)),
                ex_r=dma((EXCHANGES,)),
                sums=v((PIECES, 2, rows_f, cols_f), BF),
                rs_s=dma((len(FLOWS), 8)),
                rs_r=dma((len(FLOWS), 7)),
                sm_s=dma((10,)),
                sm_r=dma((10,)),
            ),
            pltpu.CompilerParams(collective_id=0, has_side_effects=True, vmem_limit_bytes=64 * 1024 * 1024),
            "layer",
            [[v(recv_shape(flow, k, rows_f), BF) for k in range(4)] for flow in FLOWS],
        )

        rows = [[g * groups + i for i in range(groups)] for g in range(8)]
        sout = o.sout
        if groups > 1:
            sout = lax.psum(sout, "seq", axis_index_groups=rows)
        mat, one = ((rows_f, width), F32, hbm), ((width // n_seq,), F32, hbm)
        staged, short = v((rows_f, width), F32), v((width // n_seq,), F32)
        f = call(
            lambda *refs: finish_kernel(n_seq, *refs),
            dict(hout_in=(o.hout, hbm), gin_in=(o.gin, hbm), fin=(o.fin, hbm), sout=(sout, hbm)),
            dict(
                hout=(o.hout.shape, BF, hbm),
                gin=(o.gin.shape, BF, hbm),
                query=mat,
                key=mat,
                value=mat,
                output=mat,
                inner=((rows_f, ff), F32, hbm),
                outer=((ff // 8, width), F32, hbm),
                qb=one,
                vb=one,
                ob=one,
                ag=one,
                sh=one,
                xb=one,
                fg=one,
                fs=one,
                ib=((ff // n_seq,), F32, hbm),
            ),
            dict(
                sem=dma((20 + PIECES,)),
                flat=v((1, small), F32),
                t_qb=short,
                t_vb=short,
                t_ob=short,
                t_ag=short,
                t_sh=short,
                t_xb=short,
                t_fg=short,
                t_fs=short,
                t_ib=v((ff // n_seq,), F32),
                got=v((PIECES, 2, rows_f, cols_f), BF),
                t_query=staged,
                t_key=staged,
                t_value=staged,
                t_output=staged,
                t_inner=v((rows_f, ff), F32),
                t_outer=v((ff // 8, width), F32),
                through=v((2, seqs, tok, width), BF),
                rows=v((8, width), F32),
                wide=v((8, ff), F32),
            ),
            pltpu.CompilerParams(vmem_limit_bytes=64 * 1024 * 1024),
            "finish",
        )

        def across(values):
            if groups == 1:
                return values
            return lax.psum_scatter(values, "seq", scatter_dimension=0, axis_index_groups=rows, tiled=True)

        return (
            f.hout,
            f.gin,
            across(f.query),
            f.qb,
            across(f.key),
            across(f.value),
            f.vb,
            across(f.output),
            f.ob,
            f.ag,
            f.sh,
            across(f.inner),
            f.ib,
            across(f.outer),
            f.xb,
            f.fg,
            f.fs,
        )

    return local


def solution(mesh):
    rows = P("seq", "blk", None)
    placed = (rows, P("seq"), *([P()] * 15), rows)
    mat, one = P("seq", None), P("seq")
    return jax.shard_map(
        build(mesh),
        mesh=mesh,
        in_specs=placed,
        out_specs=(rows, rows, mat, one, mat, mat, one, mat, one, one, one, mat, one, mat, one, one, one),
        check_vma=False,
    )
```

```python
import itertools
import math
from types import SimpleNamespace

import jax
import jax.numpy as jnp
from jax import lax
from jax.experimental import pallas as pl
from jax.experimental.pallas import tpu as pltpu
from jax.sharding import PartitionSpec as P

HD = 64
MESH = pl.DeviceIdType.MESH
BF = jnp.bfloat16
F32 = jnp.float32
LOG2E = math.log2(math.e)
SCALE2 = 0.125 * LOG2E
EPS = 1e-05

X, Y, Z0, Z1, C = range(5)
BITS = (Z1, Z0, Y)

PIECES = 12
OUTER, INNER, OUTPUT, PAIR = range(4)
S1, S2 = -1, -2
SMALL_ORDER = {S1: (C, Y, Z0, Z1, X), S2: (X, C, Y, Z0, Z1)}
FLOWS = (
    (OUTER, 0, 1, 0, 384, (Y, X, Z1, Z0)),
    (OUTER, 1, 1, 0, 384, (Z0, Z1, Y, X)),
    (OUTER, 2, 1, 0, 384, (X, Z0, Z1, Y)),
    (OUTER, 3, 1, 0, 384, (Z0, Y, Z1, X)),
    (INNER, 4, 1, 0, 384, (Y, Z0, Z1, X)),
    (INNER, 5, 1, 0, 384, (X, Y, Z1, Z0)),
    (INNER, 6, 1, 0, 384, (X, Y, Z1, Z0)),
    (INNER, 7, 1, 0, 384, (X, Z0, Y, Z1)),
    (OUTPUT, 11, 1, 0, 384, (Y, Z0, X, Z1)),
    (PAIR, 8, 1, 0, 384, (Y, X, Z1, Z0)),
    (PAIR + 1, 9, 1, 0, 384, (Z0, Y, Z1, X)),
    (PAIR + 2, 10, 1, 0, 128, (Y, Z0, Z1, X)),
    (PAIR + 2, 10, 1, 128, 128, (X, Y, Z1, Z0)),
    (PAIR + 2, 10, 1, 256, 128, (Y, Z0, Z1, X)),
)
PLAN = (
    (),
    ((0, -1), (1, -1)),
    ((2, -1), (3, -1)),
    (),
    (),
    ((S1, 0), (4, -1), (0, 0), (1, 0)),
    ((5, -1),),
    ((6, -1), (S1, 1), (7, -1)),
    (),
    ((2, 0),),
    ((0, 1), (1, 1), (4, 0), (3, 0), (S1, 2)),
    (),
    ((2, 1), (5, 0), (8, 0), (0, 2), (1, 2)),
    ((S1, 3), (4, 1), (3, 1), (6, 0)),
    ((2, 2),),
    ((8, 1), (0, 3), (4, 2), (9, 0), (7, 0)),
    ((1, 3), (S1, 4), (3, 2), (5, 1), (8, 2)),
    ((0, 4), (6, 1), (4, 3), (2, 3)),
    ((10, 0),),
    ((9, 1), (5, 2), (11, 0), (3, 3), (8, 3)),
    ((13, 0),),
    (
        (12, 0), (S2, 0), (7, 1), (2, 4), (S2, 1), (6, 2), (8, 4), (10, 1), (5, 3), (12, 1), (11, 1), (9, 2),
        (7, 2), (S2, 2), (13, 1), (10, 2), (6, 3), (12, 2), (9, 3), (11, 2), (S2, 3), (5, 4), (7, 3), (12, 3),
        (13, 2), (10, 3), (S2, 4), (6, 4), (9, 4), (11, 3), (7, 4), (12, 4), (13, 3), (1, 5), (0, 5), (4, 5),
        (3, 5), (2, 5), (8, 5), (5, 5), (10, 5), (6, 5), (9, 5), (11, 5), (7, 5), (12, 5), (13, 5),
    ),
)

QB, VB, OB, AG, AS, XB, FG, FS, IB = range(9)
GO, GA, HX, HC, HF, HO, GP, GI, AT, AO = 0, 1, 2, 4, 6, 8, 10, 12, 14, 18
EXCHANGES = 19


def nn(left, right):
    return jnp.dot(left, right, preferred_element_type=F32)


def nt(left, right):
    return lax.dot_general(left, right, (((1,), (1,)), ((), ())), preferred_element_type=F32)


def tn(left, right):
    return lax.dot_general(left, right, (((0,), (0,)), ((), ())), preferred_element_type=F32)


def fold8(values):
    rows, width = values.shape
    return jnp.sum(values.reshape(rows // 8, 8, width), axis=0)


def halves_rows(order, k):
    return X in order[: k + 1] and order.index(X) < 3


def recv_shape(flow, k, rows):
    part, f, nf, start, cols, order = flow
    free = [2 for ax in BITS if ax not in order[: k + 1]]
    return (nf, *free, rows // 2 if halves_rows(order, k) else rows, cols)


def layer_kernel(groups, names, *refs):
    r = SimpleNamespace(**dict(zip(names, refs)))
    seq = lax.axis_index("seq")
    blk = lax.axis_index("blk")
    x = lax.div(blk, 2)
    c = lax.rem(blk, 2)
    hi = lax.div(seq, groups)
    own = {X: x, Y: lax.rem(hi, 2), Z0: lax.rem(lax.div(hi, 2), 2), Z1: lax.div(hi, 4)}
    peers = {
        C: (seq, blk + 1 - 2 * c),
        X: (seq, blk + 2 - 4 * x),
        Y: (seq + (1 - 2 * own[Y]) * groups, blk),
        Z0: (seq + (1 - 2 * own[Z0]) * 2 * groups, blk),
        Z1: (seq + (1 - 2 * own[Z1]) * 4 * groups, blk),
    }
    part_tok, width = r.xall.shape[2:]
    tok = 2 * part_tok
    groups_q = r.xall.shape[0]
    seq_len = groups_q * tok
    half = width // 2
    ff = r.wi.shape[1]
    pairs = half // 128
    own_heads = pl.ds(pl.multiple_of(c * half, 128), half)
    other_heads = pl.ds(pl.multiple_of((1 - c) * half, 128), half)

    def vec(i, start=0, size=width):
        return r.vec[:, pl.ds(width * i + start, size)]

    def pair_lanes(p, base=0):
        return pl.ds(pl.multiple_of(base * width + c * half + p * 128, 128), 128)

    def remote(src, dst, send, recv, peer):
        return pltpu.make_async_remote_copy(
            src_ref=src, dst_ref=dst, send_sem=send, recv_sem=recv, device_id=peers[peer], device_id_type=MESH
        )

    barrier = pltpu.get_barrier_semaphore()
    for peer in peers.values():
        pl.semaphore_signal(barrier, inc=1, device_id=peer, device_id_type=MESH)

    lcount = itertools.count()

    def fetch(src, dst):
        return pltpu.make_async_copy(src, dst, r.lsem.at[next(lcount)])

    def half_block(ref, seq_at, i):
        return ref.at[seq_at, pl.ds(i * part_tok, part_tok)]

    first = [fetch(half_block(r.hid, x, i), r.xall.at[i, c]) for i in range(2)]
    for p in range(pairs):
        for i, w in enumerate((r.wq, r.wk, r.wv)):
            first.append(fetch(w.at[:, pair_lanes(p)], r.wcat.at[:, pl.ds((3 * p + i) * 128, 128)]))
    second = [
        fetch(r.go.at[x], r.gown.at[0]),
        fetch(r.wo_in, r.wo),
        fetch(r.wi_in, r.wi),
        fetch(r.wx_in, r.wx),
    ]
    for copy in first + second:
        copy.start()
    params = (r.qb, r.vb, r.ob, r.ag, r.sh, r.xb, r.fg, r.fs, r.ib)
    third = [fetch(ref, r.raw.at[pl.ds(width * i, ref.shape[0])]) for i, ref in enumerate(params)]
    third.append(fetch(r.dg, r.kept))
    for copy in third:
        copy.start()
    pl.semaphore_wait(barrier, len(peers))

    def ex(i):
        if i == GO:
            src, dst, peer = r.go.at[1 - x], r.gown.at[1], X
        elif i == GA:
            src = dst = r.ga.at[:, c]
            peer = C
        elif i < HC:
            src, dst, peer = half_block(r.hid, 1 - x, i - HX), r.xall.at[2 + i - HX, c], X
        elif i < HF:
            src, dst, peer = half_block(r.hid, x, i - HC), r.xall.at[i - HC, c], C
        elif i < HO:
            src = dst = r.xall.at[2 + i - HF, c]
            peer = C
        elif i < GP:
            src, dst, peer = r.ga.at[2 + i - HO, c], half_block(r.hout, x, i - HO), X
        elif i < GI:
            at = pl.ds(2 * (i - GP), 2)
            src, dst, peer = r.gffn.at[at], r.xall.at[at, 1 - c], C
        elif i < AT:
            src, dst, peer = r.inn.at[2 + i - GI], half_block(r.gin, x, i - GI), X
        elif i < AO:
            src = dst = r.att.at[i - AT, 1 - c, :, own_heads]
            peer = C
        else:
            src = dst = r.att.at[:, c, :, own_heads]
            peer = C
        return remote(src, dst, r.ex_s.at[i], r.ex_r.at[i], peer)

    for i in (HX, HX + 1, HC, HC + 1, GO):
        ex(i).start()
    for copy in third:
        copy.wait()
    r.vec[...] = r.raw[...].astype(F32).reshape(1, r.raw.shape[0])
    r.sg8[...] = jnp.zeros_like(r.sg8)
    kept = jnp.where(r.kept[x] == 2, 0.0, 1.0).astype(F32)

    lane_head = lax.broadcasted_iota(jnp.int32, (tok, 128), 1) // HD
    ones = jnp.ones((seq_len, 128), BF)
    for p in range(pairs):
        r.vp[p, :, pl.ds(128, 128)] = ones

    def project(j):
        out = nn(r.xall[j].reshape(tok, width), r.wcat[...])
        at = pl.ds(pl.multiple_of(j * tok, tok), tok)
        for p in range(pairs):
            lanes = pl.ds(p * 128, 128)
            base = 3 * p * 128
            r.q[at, lanes] = (out[:, base : base + 128] + r.vec[:, pair_lanes(p, QB)]).astype(BF)
            key = out[:, base + 128 : base + 256].astype(BF)
            r.k[at, lanes] = key
            r.kt[lanes, at] = key.T
            r.vp[p, at, pl.ds(0, 128)] = (out[:, base + 256 : base + 384] + r.vec[:, pair_lanes(p, VB)]).astype(BF)

    def attend(j, start, count, begin_here, end_here):
        rows = pl.ds(pl.multiple_of(j * tok, tok), tok)
        keys = pl.ds(start, count)
        for p in range(pairs):
            lanes = pl.ds(p * 128, 128)
            out_ref = r.work.at[rows, lanes]
            top_ref = r.work.at[rows, pl.ds(half + p * 128, 128)]
            sum_lanes = pl.ds(pl.multiple_of(j * 128, 128), 128)
            sum_ref = (r.dva.at[rows], r.dka.at[rows], r.work.at[pl.ds(3 * tok, tok), sum_lanes])[p]
            qp = r.q[rows, lanes]
            tops, parts = [], []
            for h in range(2):
                qm = jnp.where(lane_head == h, qp, jnp.zeros_like(qp))
                s = nn(qm, r.kt[lanes, keys])
                top = jnp.max(s, axis=1, keepdims=True)
                pt = jnp.exp2((s - top) * SCALE2).astype(BF)
                tops.append(top)
                parts.append(nn(pt, r.vp[p, keys, :]))
            top = jnp.where(lane_head == 0, tops[0], tops[1])
            out = jnp.where(lane_head == 0, parts[0][:, :128], parts[1][:, :128])
            total = jnp.where(lane_head == 0, parts[0][:, 128:], parts[1][:, 128:])
            if not begin_here:
                old = top_ref[...]
                both = jnp.maximum(old, top)
                grow, shrink = jnp.exp2((top - both) * SCALE2), jnp.exp2((old - both) * SCALE2)
                out = out * grow + out_ref[...] * shrink
                total = total * grow + sum_ref[...] * shrink
                top = both
            if end_here:
                r.att[j, :, :, pair_lanes(p)] = (out / total).astype(BF).reshape(2, part_tok, 128)
                both = (top * SCALE2 + jnp.log2(total)).T
                for h in range(2):
                    r.lse[2 * p + h, :, rows] = both[h * HD : h * HD + 1]
            else:
                out_ref[...] = out
                top_ref[...] = top
                sum_ref[...] = total

    for copy in first:
        copy.wait()
    for i in range(2):
        ex(HC + i).wait_recv()

    @pl.loop(0, 2)
    def _(j):
        project(j)

    @pl.loop(0, 2)
    def _(j):
        attend(j, 0, 2 * tok, True, False)

    ex(HX).wait_recv()
    ex(HF).start()
    ex(HF).wait_recv()
    project(2)

    attend(2, 0, 3 * tok, True, False)
    ex(HX + 1).wait_recv()
    ex(HF + 1).start()
    ex(HF + 1).wait_recv()
    project(3)
    attend(3, 0, 4 * tok, True, True)
    ex(AT + 3).start()
    for j, start in ((2, 3 * tok), (1, 2 * tok), (0, 2 * tok)):
        attend(j, start, 4 * tok - start, False, True)
        ex(AT + j).start()
    ex(AO).start()

    for copy in second:
        copy.wait()

    def own_rows(i):
        return i // 2, pl.ds((i % 2) * part_tok, part_tok), pl.ds(i * part_tok, part_tok)

    def fold_in(i, values):
        at = pl.ds(width * i, values.shape[1])
        r.sg8[:, at] += fold8(values)

    def heads_out(heads):
        return nn(r.att[:, c, :, heads].reshape(2 * tok, half), r.wo[heads, :])

    acc, xh_ref = r.work.at[pl.ds(0, 2 * tok)], r.work.at[pl.ds(2 * tok, 2 * tok)]
    acc[...] = heads_out(own_heads)
    for j in range(groups_q):
        ex(AT + j).wait_recv()
    acc[...] += heads_out(other_heads)

    for i in range(4):
        which, inner, rows = own_rows(i)
        v = acc[rows, :] + vec(OB) + r.xall[i, c].astype(F32)
        cen = v - jnp.mean(v, axis=-1, keepdims=True)
        rstd = lax.rsqrt(jnp.mean(cen * cen, axis=-1, keepdims=True) + EPS)
        xh = cen * rstd
        normed = xh * vec(AG) + vec(AS)
        xh_ref[rows, :] = xh
        r.dva[rows, pl.ds(0, 1)] = rstd
        acc[rows, :] = normed
        r.inn[i] = normed.astype(BF)

    tile = 512

    def activate(j):
        start = pl.multiple_of(j * tile, tile)
        at = pl.ds(start, tile)
        pre = nn(r.inn[...].reshape(2 * tok, width), r.wi[:, at]) + r.vec[:, pl.ds(pl.multiple_of(width * IB + start, 128), tile)]
        phi = 0.5 + 0.5 * lax.erf(pre * math.sqrt(0.5))
        dens = jnp.exp2(pre * pre * (-0.5 * LOG2E)) * (1.0 / math.sqrt(2.0 * math.pi))
        r.act[:, at] = (pre * phi).astype(BF)
        r.gp[:, at] = (phi + pre * dens).astype(BF)

    @pl.loop(0, 2)
    def _(i):
        for j in range(ff // tile // 2):
            activate(i * (ff // tile // 2) + j)

    @pl.loop(0, width // 256)
    def _(j):
        at = pl.ds(pl.multiple_of(j * 256, 256), 256)
        acc[:, at] += nn(r.act[...], r.wx[:, at])

    ex(GO).wait_recv()
    for i in range(4):
        which, inner, rows = own_rows(i)
        xf = r.xall[i, c].astype(F32)
        v = acc[rows, :] + vec(XB)
        cen = v - jnp.mean(v, axis=-1, keepdims=True)
        rstd = lax.rsqrt(jnp.mean(cen * cen, axis=-1, keepdims=True) + EPS)
        xh = cen * rstd
        out = kept * (xh * vec(FG) + vec(FS)) + (1.0 - kept) * xf
        r.ga[i, c] = out.astype(BF)
        g = kept * r.gown[which, inner, :].astype(F32)
        fold_in(FG, g * xh)
        fold_in(FS, g)
        gx = g * vec(FG)
        m1 = jnp.mean(gx, axis=-1, keepdims=True)
        m2 = jnp.mean(gx * xh, axis=-1, keepdims=True)
        gs = rstd * (gx - m1 - xh * m2)
        low = gs.astype(BF)
        acc[rows, :] = gs
        r.gffn[i] = low
        fold_in(XB, low.astype(F32))

    ex(HO).start()
    ex(HO + 1).start()
    hout_local = [fetch(r.ga.at[i, c], half_block(r.hout, x, i)) for i in range(2)]
    for copy in hout_local:
        copy.start()

    rows_f, cols_f = r.dc.shape[-2:]
    x_rows = pl.ds(pl.multiple_of(x * (rows_f // 2), 16), rows_f // 2)

    def pieces(flow):
        f, nf = flow[1:3]
        return r.d2.at[c, pl.ds(f, nf)] if f < 8 else r.dc.at[pl.ds(f - 8, nf)]

    def view(flow, k, send):
        part, f, nf, start, cols, order = flow
        idx = [slice(None)] * 3
        row = pl.ds(0, rows_f)
        for j, ax in enumerate(order[: k + 1]):
            want = 1 - own[ax] if (j == k and send) else own[ax]
            if ax != X:
                idx[BITS.index(ax)] = want
            elif j < 3:
                row = pl.ds(pl.multiple_of(want * (rows_f // 2), 16), rows_f // 2)
        return (slice(None), *idx, row, pl.ds(start, cols))

    def hop(i, k):
        flow = FLOWS[i]
        src = pieces(flow).at[view(flow, k, True)]
        return remote(src, r.land[i][k], r.rs_s.at[i, k], r.rs_r.at[i, k], flow[5][k])

    def add_in(i, k):
        flow = FLOWS[i]
        nf, order = flow[2], flow[5]
        idx = list(view(flow, k, False))
        ref = pieces(flow)
        free = [ax for ax in BITS if ax not in order[: k + 1]]
        for n in range(nf):
            idx[0] = n
            for combo in itertools.product((0, 1), repeat=len(free)):
                for ax, bit in zip(free, combo):
                    idx[1 + BITS.index(ax)] = bit
                at = tuple(idx)
                ref[at] = ref[at] + r.land[i][k][(n, *combo, slice(None), slice(None))]

    def spread(i, k):
        part, f, nf, start, cols, order = FLOWS[i]
        rows = x_rows if k == 4 else pl.ds(0, rows_f)
        ref = r.sums.at[pl.ds(f, nf), c, rows, pl.ds(start, cols)]
        return remote(ref, ref, r.rs_s.at[i, k], r.rs_r.at[i, k], X if k == 4 else C)

    def save(i):
        part, f, nf, start, cols, order = FLOWS[i]
        at = (pl.ds(f, nf), slice(None), slice(None), pl.ds(start, cols))
        return pltpu.make_async_copy(r.sums.at[at], r.fin.at[at], r.rs_s.at[i, 7])

    def core_sum(i):
        part, f, nf, start, cols, order = FLOWS[i]
        at = pl.ds(f, nf)
        return remote(r.d2.at[1 - c, at], r.rc.at[at], r.rs_s.at[i, 6], r.rs_r.at[i, 6], C)

    def small(which, k):
        send, recv = (r.s1s, r.s1r) if which == S1 else (r.s2s, r.s2r)
        at = k if which == S1 else 5 + k
        return remote(send.at[k], recv.at[k], r.sm_s.at[at], r.sm_r.at[at], SMALL_ORDER[which][k])

    def step(i, k):
        if i < 0:
            send, recv = (r.s1s, r.s1r) if i == S1 else (r.s2s, r.s2r)
            small(i, k).wait_recv()
            send[k + 1] = send[k] + recv[k]
            if k < 4:
                small(i, k + 1).start()
            return
        flow = FLOWS[i]
        part, f, nf, start, cols, order = flow
        if k == -1:
            core_sum(i).wait_recv()
            ref = pieces(flow)
            for combo in itertools.product(range(nf), (0, 1), (0, 1), (0, 1)):
                ref[combo] = ref[combo] + r.rc[(f + combo[0], *combo[1:])]
            hop(i, 0).start()
        elif k < 3:
            hop(i, k).wait_recv()
            add_in(i, k)
            hop(i, k + 1).start()
        elif k == 3:
            hop(i, 3).wait_recv()
            rows = pl.ds(0, rows_f) if order[3] == X else x_rows
            at = pl.ds(start, cols)
            for n in range(nf):
                mine_part = pieces(flow)[(n, own[Z1], own[Z0], own[Y], rows, at)]
                r.sums[f + n, c, rows, at] = mine_part + r.land[i][3][n]
            spread(i, 5 if order[3] == X else 4).start()
        elif k == 4:
            spread(i, 4).wait_recv()
            spread(i, 5).start()
        else:
            spread(i, 5).wait_recv()
            save(i).start()

    plan = iter(PLAN)

    def tick():
        for i, k in next(plan):
            step(i, k)

    def begin(part):
        for i, flow in enumerate(FLOWS):
            if flow[0] == part:
                (core_sum(i) if flow[1] < 8 else hop(i, 0)).start()

    outer_rows = ff // 8

    @pl.loop(0, 2)
    def _(i):
        for j in range(4):
            at = pl.ds(pl.multiple_of((4 * i + j) * outer_rows, 128), outer_rows)
            val = tn(r.act[:, at], r.gffn[...].reshape(2 * tok, width)).astype(BF)
            for f in range(4):
                for h in range(2):
                    part = val[f * rows_f : (f + 1) * rows_f, h * cols_f : (h + 1) * cols_f]
                    r.d2[h, f, i, j // 2, j % 2] = part

    begin(OUTER)
    tick()

    tile = ff // 4

    @pl.loop(0, 2)
    def _(i):
        for j in range(2):
            start = pl.multiple_of((2 * i + j) * tile, tile)
            at = pl.ds(start, tile)
            gpre = (nt(r.gffn[...].reshape(2 * tok, width), r.wx[at, :]) * r.gp[:, at].astype(F32)).astype(BF)
            r.gp[:, at] = gpre
            r.sg8[:, pl.ds(pl.multiple_of(width * IB + start, 128), tile)] = fold8(gpre.astype(F32))

    tick()


    @pl.loop(0, width // 256)
    def _(j):
        at = pl.ds(pl.multiple_of(j * 256, 256), 256)
        acc[:, at] += nt(r.gp[...], r.wi[at, :])

    tick()
    ex(HO).wait_send()
    ex(HO + 1).wait_send()
    for copy in hout_local:
        copy.wait()
    for i in range(4):
        which, inner, rows = own_rows(i)
        g = acc[rows, :]
        xh = xh_ref[rows, :]
        fold_in(AG, g * xh)
        fold_in(AS, g)
        gx = g * vec(AG)
        m1 = jnp.mean(gx, axis=-1, keepdims=True)
        m2 = jnp.mean(gx * xh, axis=-1, keepdims=True)
        gs = r.dva[rows, pl.ds(0, 1)] * (gx - m1 - xh * m2)
        low = gs.astype(BF)
        acc[rows, :] = gs
        r.ga[i, c] = low
        fold_in(OB, low.astype(F32))

    xt = r.wi.at[:, pl.ds(0, seq_len)]
    xt[...] = r.xall[...].reshape(seq_len, width).T
    for i in range(2):
        ex(HF + i).wait_send()
    ex(GA).start()
    late = 2 * width
    r.s1s[0] = jnp.sum(r.sg8[:, pl.ds(late, r.s1s.shape[2])], axis=0, keepdims=True)
    small(S1, 0).start()
    tick()

    @pl.loop(0, 2)
    def _(i):
        for h in range(2):
            at = pl.ds(pl.multiple_of((2 * h + i) * tile, tile), tile)
            val = tn(r.inn[...].reshape(2 * tok, width), r.gp[:, at]).astype(BF)
            for m in range(2):
                part = val[:, m * cols_f : (m + 1) * cols_f]
                r.d2[h, 4 + 2 * i + m] = part.reshape(2, 2, 2, rows_f, cols_f)
        for n in range(2):

            @pl.when(i == n)
            def _():
                for g, flow in enumerate(FLOWS):
                    if flow[0] == INNER and (flow[1] + flow[2] - 1) // 2 == 2 + n:
                        core_sum(g).start()
                tick()


    def dqkv(p):
        rows = pl.ds(pl.multiple_of(lax.div(p, 2) * seq_len, 1024), seq_len)
        return r.wx.at[rows, pl.ds(pl.multiple_of(lax.rem(p, 2) * 384, 128), 384)]

    do = r.wx.at[pl.ds(seq_len, seq_len), pl.ds(384, half)]

    def upstream(core):
        val = nt(r.ga[:, core].reshape(2 * tok, width), r.wo[own_heads, :]).astype(BF)
        for j in range(groups_q):
            at = pl.ds(pl.multiple_of(j * tok + core * part_tok, part_tok), part_tok)
            do[at, :] = val[j * part_tok : (j + 1) * part_tok]

    upstream(c)
    tick()
    ex(GA).wait_recv()
    upstream(1 - c)

    for p in range(pairs):
        at = r.att[:, :, :, pair_lanes(p)].reshape(seq_len, 128)
        prod = (at.astype(F32) * do[:, pl.ds(p * 128, 128)].astype(F32)).T
        for h in range(2):
            r.delta[2 * p + h] = jnp.sum(prod[h * HD : (h + 1) * HD], axis=0, keepdims=True)
    tick()

    ex(AO).wait_recv()
    att_all = r.att[...].reshape(seq_len, width)
    ga_cols = r.ga[:, :, :, own_heads].reshape(seq_len, half)
    r.dc[3] = tn(att_all, ga_cols).astype(BF).reshape(2, 2, 2, rows_f, cols_f)
    begin(OUTPUT)
    tick()

    steps = [[next(plan) for _ in range(groups_q // 2 + 1)] for _ in range(pairs)]

    def tick_at(p, j):
        for n in range(pairs):
            if steps[n][j]:

                @pl.when(p == n)
                def _():
                    for i, k in steps[n][j]:
                        step(i, k)

    def backward(p, t):
        lanes = pl.ds(pl.multiple_of(p * 128, 128), 128)
        rows = pl.ds(pl.multiple_of(t * tok, tok), tok)
        qp = r.q[rows, lanes]
        dp = do[rows, lanes]
        kp = r.k[:, lanes]
        vp = r.vp[p, :, pl.ds(0, 128)]
        zero = jnp.zeros_like(qp)
        dqs = []
        for h in range(2):
            qm = jnp.where(lane_head == h, qp, zero)
            dm = jnp.where(lane_head == h, dp, zero)
            pt = jnp.exp2(nt(kp, qm) * SCALE2 - r.lse[2 * p + h, :, rows])
            ds = (pt * (nt(vp, dm) - r.delta[2 * p + h, :, rows])).astype(BF)
            r.dva[...] += nn(pt.astype(BF), dm)
            r.dka[...] += nn(ds, qm)
            dqs.append(nn(r.kt[pl.ds(pl.multiple_of(p * 128 + h * HD, HD), HD), :], ds))
        both = (jnp.concatenate(dqs, axis=0) * 0.125).astype(BF)
        dqkv(p)[rows, pl.ds(0, 128)] = both.T

    @pl.loop(0, pairs)
    def _(p):
        r.dva[...] = jnp.zeros_like(r.dva)
        r.dka[...] = jnp.zeros_like(r.dka)

        for t in range(groups_q):
            backward(p, t)
            if t % 2:
                tick_at(p, t // 2)

        dqkv(p)[:, pl.ds(128, 128)] = (r.dka[...] * 0.125).astype(BF)
        dqkv(p)[:, pl.ds(256, 128)] = r.dva[...].astype(BF)
        r.dc[p] = nn(xt[...], dqkv(p)[...]).astype(BF).reshape(2, 2, 2, rows_f, cols_f)
        r.sg8[:, pair_lanes(p, QB)] = fold8(dqkv(p)[:, pl.ds(0, 128)].astype(F32))
        r.sg8[:, pair_lanes(p, VB)] = fold8(dqkv(p)[:, pl.ds(256, 128)].astype(F32))
        for n in range(pairs):

            @pl.when(p == n)
            def _():
                begin(PAIR + n)
                if n == pairs - 1:
                    r.s2s[0] = jnp.sum(r.sg8[:, pl.ds(0, late)], axis=0, keepdims=True)
                    small(S2, 0).start()

        tick_at(p, 2)

    def partial(core, j):
        rows = [pl.ds(pl.multiple_of(n * tok + core * part_tok, part_tok), part_tok) for n in (2 * j, 2 * j + 1)]
        left = jnp.concatenate([r.wx[at, pl.ds(0, 768)] for at in rows], axis=0)
        right = jnp.concatenate([dqkv(2)[at, :] for at in rows], axis=0)
        return nt(left, r.wcat[:, pl.ds(0, 768)]) + nt(right, r.wcat[:, pl.ds(768, 384)])

    for i in (1, 0):
        r.gffn[pl.ds(2 * i, 2)] = partial(1 - c, i).astype(BF).reshape(2, part_tok, width)
        ex(GP + i).start()
    tick()
    for i in (1, 0):
        acc[pl.ds(i * tok, tok), :] += partial(c, i)
    tick()
    for i in (1, 0):
        ex(GP + i).wait_recv()
        for j in (2 * i, 2 * i + 1):
            which, inner, rows = own_rows(j)
            total = acc[rows, :] + r.xall[j, c].astype(F32) + (1.0 - kept) * r.gown[which, inner, :].astype(F32)
            r.inn[j] = total.astype(BF)
            if i:
                ex(GI + j - 2).start()
    gin_local = [fetch(r.inn.at[i], half_block(r.gin, x, i)) for i in range(2)]
    for copy in gin_local:
        copy.start()
    tick()
    tick()
    r.sout[:, pl.ds(0, late)] = r.s2s[5]
    r.sout[:, pl.ds(late, r.s1s.shape[2])] = r.s1s[5]

    for i in (HO, HO + 1, GI, GI + 1):
        ex(i).wait_recv()
    for copy in gin_local:
        copy.wait()
    for i in range(EXCHANGES):
        if i not in (HF, HF + 1, HO, HO + 1):
            ex(i).wait_send()
    for k in range(5):
        small(S1, k).wait_send()
        small(S2, k).wait_send()
    for i, flow in enumerate(FLOWS):
        for k in range(4):
            hop(i, k).wait_send()
        if flow[5][3] != X:
            spread(i, 4).wait_send()
        spread(i, 5).wait_send()
        save(i).wait()
        if flow[1] < 8:
            core_sum(i).wait_send()


def finish_kernel(n_seq, names, *refs):
    r = SimpleNamespace(**dict(zip(names, refs)))
    pairs = ((r.hout_in, r.hout), (r.gin_in, r.gin))
    arrive = [pltpu.make_async_copy(pair[0], r.through.at[i], r.sem.at[i]) for i, pair in enumerate(pairs)]
    leave = [pltpu.make_async_copy(r.through.at[i], pair[1], r.sem.at[2 + i]) for i, pair in enumerate(pairs)]
    flat = pltpu.make_async_copy(r.sout, r.flat, r.sem.at[10 + PIECES])
    flat.start()
    for copy in arrive:
        copy.start()
    for before, after in zip(arrive, leave):
        before.wait()
        after.start()
    rows_f, cols_f = r.fin.shape[2:]
    half = cols_f
    outs = (r.outer, r.inner, r.output, r.query, r.key, r.value)
    made = (r.t_outer, r.t_inner, r.t_output, r.t_query, r.t_key, r.t_value)
    done = [pltpu.make_async_copy(src, dst, r.sem.at[4 + i]) for i, (src, dst) in enumerate(zip(made, outs))]

    def take(f):
        return pltpu.make_async_copy(r.fin.at[f], r.got.at[f], r.sem.at[10 + f])

    for f in range(PIECES):
        take(f).start()
    for f in range(4):
        take(f).wait()
        for h in range(2):
            r.t_outer[pl.ds(f * rows_f, rows_f), pl.ds(h * half, half)] = r.got[f, h].astype(F32)
    done[0].start()
    for f in range(4):
        take(4 + f).wait()
        for h in range(2):
            r.t_inner[:, pl.ds((4 * h + f) * cols_f, cols_f)] = r.got[4 + f, h].astype(F32)
    done[1].start()
    for f in range(8, PIECES):
        take(f).wait()
    for h in range(2):
        r.t_output[:, pl.ds(h * half, half)] = r.got[11, h].astype(F32)
    done[2].start()
    for i, ref in enumerate(made[3:]):
        for h in range(2):
            for p in range(half // 128):
                part = r.got[8 + p, h, :, pl.ds(i * 128, 128)].astype(F32)
                ref[:, pl.ds(h * half + p * 128, 128)] = part
        done[3 + i].start()
    seq = lax.axis_index("seq")
    width = 2 * half
    share = width // n_seq
    flat.wait()
    for i in range(8):
        r.rows[pl.ds(i, 1), :] = r.flat[:, pl.ds(i * width, width)]
    turned = pltpu.roll(r.rows[...], lax.rem(width - seq * share, width), 1)
    for i, ref in enumerate((r.t_qb, r.t_vb, r.t_ob, r.t_ag, r.t_sh, r.t_xb, r.t_fg, r.t_fs)):
        ref[...] = turned[i, :share]
    ib = r.ib.shape[0]
    full = r.flat.shape[1] - 8 * width
    r.wide[...] = jnp.broadcast_to(r.flat[:, pl.ds(8 * width, full)], (8, full))
    r.t_ib[...] = pltpu.roll(r.wide[...], lax.rem(full - seq * ib, full), 1)[0, :ib]
    vectors = (r.qb, r.vb, r.ob, r.ag, r.sh, r.xb, r.fg, r.fs, r.ib)
    shares = (r.t_qb, r.t_vb, r.t_ob, r.t_ag, r.t_sh, r.t_xb, r.t_fg, r.t_fs, r.t_ib)
    for i, (src, dst) in enumerate(zip(shares, vectors)):
        done.append(pltpu.make_async_copy(src, dst, r.sem.at[11 + PIECES + i]))
        done[-1].start()
    for copy in leave + done:
        copy.wait()


def call(kernel, ins, outs, scratch, params, name, land=()):
    names = [*ins, *outs, *scratch]

    def body(*refs):
        extra = refs[len(names) :]
        shelf = iter(extra)
        nested = [[next(shelf) for _ in group] for group in land]
        kernel([*names, *(("land",) if land else ())], *refs[: len(names)], *((nested,) if land else ()))

    res = pl.pallas_call(
        body,
        out_shape=[jax.ShapeDtypeStruct(e[0], e[1]) for e in outs.values()],
        in_specs=[e[1] for e in ins.values()],
        out_specs=[e[2] for e in outs.values()],
        scratch_shapes=[*scratch.values(), *(e for group in land for e in group)],
        compiler_params=params,
        name=name,
    )(*[e[0] for e in ins.values()])
    return SimpleNamespace(**dict(zip(outs, res)))


def build(mesh):
    n_seq = mesh.shape["seq"]
    groups = n_seq // 8

    def local(
        hidden_in,
        depth_group,
        query_weight,
        query_bias,
        key_weight,
        value_weight,
        value_bias,
        output_weight,
        output_bias,
        attn_gain,
        attn_shift,
        inner_weight,
        inner_bias,
        outer_weight,
        outer_bias,
        final_gain,
        final_shift,
        grad_out,
    ):
        seqs, tok, width = hidden_in.shape
        ff = inner_weight.shape[1]
        seq_len = 4 * tok
        half = width // 2
        heads = half // HD
        pairs = half // 128
        rows_f, cols_f = width // 8, half
        small, late = 8 * width + ff, 2 * width
        hbm = pl.BlockSpec(memory_space=pl.ANY)
        vmem = pl.BlockSpec(memory_space=pltpu.VMEM)
        v = pltpu.VMEM
        dma = pltpu.SemaphoreType.DMA
        o = call(
            lambda *refs: layer_kernel(groups, *refs),
            dict(
                qb=(query_bias, hbm),
                vb=(value_bias, hbm),
                ob=(output_bias, hbm),
                ag=(attn_gain, hbm),
                sh=(attn_shift, hbm),
                xb=(outer_bias, hbm),
                fg=(final_gain, hbm),
                fs=(final_shift, hbm),
                ib=(inner_bias, hbm),
                dg=(depth_group, hbm),
                hid=(hidden_in, hbm),
                go=(grad_out, hbm),
                wq=(query_weight, hbm),
                wk=(key_weight, hbm),
                wv=(value_weight, hbm),
                wo_in=(output_weight, hbm),
                wi_in=(inner_weight, hbm),
                wx_in=(outer_weight, hbm),
            ),
            dict(
                hout=((seqs, tok, width), BF, hbm),
                gin=((seqs, tok, width), BF, hbm),
                fin=((PIECES, 2, rows_f, cols_f), BF, hbm),
                sout=((1, small), F32, vmem),
            ),
            dict(
                kept=pltpu.SMEM((seqs,), jnp.int32),
                raw=v((small,), BF),
                vec=v((1, small), F32),
                xall=v((4, 2, tok // 2, width), BF),
                gown=v((2, tok, width), BF),
                wcat=v((width, 3 * half), BF),
                wo=v((width, width), BF),
                wi=v((width, ff), BF),
                wx=v((ff, width), BF),
                q=v((seq_len, half), BF),
                k=v((seq_len, half), BF),
                kt=v((half, seq_len), BF),
                vp=v((pairs, seq_len, 256), BF),
                lse=v((heads, 1, seq_len), F32),
                delta=v((heads, 1, seq_len), F32),
                att=v((4, 2, tok // 2, width), BF),
                ga=v((4, 2, tok // 2, width), BF),
                act=v((2 * tok, ff), BF),
                gp=v((2 * tok, ff), BF),
                inn=v((4, tok // 2, width), BF),
                gffn=v((4, tok // 2, width), BF),
                work=v((4 * tok, width), F32),
                dka=v((seq_len, 128), F32),
                dva=v((seq_len, 128), F32),
                d2=v((2, 8, 2, 2, 2, rows_f, cols_f), BF),
                rc=v((8, 2, 2, 2, rows_f, cols_f), BF),
                dc=v((4, 2, 2, 2, rows_f, cols_f), BF),
                sg8=v((8, small), F32),
                s1s=v((6, 1, small - late), F32),
                s1r=v((5, 1, small - late), F32),
                s2s=v((6, 1, late), F32),
                s2r=v((5, 1, late), F32),
                lsem=dma((20 + 3 * pairs,)),
                ex_s=dma((EXCHANGES,)),
                ex_r=dma((EXCHANGES,)),
                sums=v((PIECES, 2, rows_f, cols_f), BF),
                rs_s=dma((len(FLOWS), 8)),
                rs_r=dma((len(FLOWS), 7)),
                sm_s=dma((10,)),
                sm_r=dma((10,)),
            ),
            pltpu.CompilerParams(collective_id=0, has_side_effects=True, vmem_limit_bytes=64 * 1024 * 1024),
            "layer",
            [[v(recv_shape(flow, k, rows_f), BF) for k in range(4)] for flow in FLOWS],
        )

        rows = [[g * groups + i for i in range(groups)] for g in range(8)]
        sout = o.sout
        if groups > 1:
            sout = lax.psum(sout, "seq", axis_index_groups=rows)
        mat, one = ((rows_f, width), F32, hbm), ((width // n_seq,), F32, hbm)
        staged, short = v((rows_f, width), F32), v((width // n_seq,), F32)
        f = call(
            lambda *refs: finish_kernel(n_seq, *refs),
            dict(hout_in=(o.hout, hbm), gin_in=(o.gin, hbm), fin=(o.fin, hbm), sout=(sout, hbm)),
            dict(
                hout=(o.hout.shape, BF, hbm),
                gin=(o.gin.shape, BF, hbm),
                query=mat,
                key=mat,
                value=mat,
                output=mat,
                inner=((rows_f, ff), F32, hbm),
                outer=((ff // 8, width), F32, hbm),
                qb=one,
                vb=one,
                ob=one,
                ag=one,
                sh=one,
                xb=one,
                fg=one,
                fs=one,
                ib=((ff // n_seq,), F32, hbm),
            ),
            dict(
                sem=dma((20 + PIECES,)),
                flat=v((1, small), F32),
                t_qb=short,
                t_vb=short,
                t_ob=short,
                t_ag=short,
                t_sh=short,
                t_xb=short,
                t_fg=short,
                t_fs=short,
                t_ib=v((ff // n_seq,), F32),
                got=v((PIECES, 2, rows_f, cols_f), BF),
                t_query=staged,
                t_key=staged,
                t_value=staged,
                t_output=staged,
                t_inner=v((rows_f, ff), F32),
                t_outer=v((ff // 8, width), F32),
                through=v((2, seqs, tok, width), BF),
                rows=v((8, width), F32),
                wide=v((8, ff), F32),
            ),
            pltpu.CompilerParams(vmem_limit_bytes=64 * 1024 * 1024),
            "finish",
        )

        def across(values):
            if groups == 1:
                return values
            return lax.psum_scatter(values, "seq", scatter_dimension=0, axis_index_groups=rows, tiled=True)

        return (
            f.hout,
            f.gin,
            across(f.query),
            f.qb,
            across(f.key),
            across(f.value),
            f.vb,
            across(f.output),
            f.ob,
            f.ag,
            f.sh,
            across(f.inner),
            f.ib,
            across(f.outer),
            f.xb,
            f.fg,
            f.fs,
        )

    return local


def solution(mesh):
    rows = P("seq", "blk", None)
    placed = (rows, P("seq"), *([P()] * 15), rows)
    mat, one = P("seq", None), P("seq")
    return jax.shard_map(
        build(mesh),
        mesh=mesh,
        in_specs=placed,
        out_specs=(rows, rows, mat, one, mat, mat, one, mat, one, one, one, mat, one, mat, one, one, one),
        check_vma=False,
    )
```
